512 devices in a mesh: seq: 128 (over y, z, x_lo), mp: 2 (over x_hi), batch: 2 (over core).
Axes of the slice: x: 4 (x_hi: 2, x_lo: 2; x = x_hi * 2 + x_lo), y: 8, z: 8, core: 2. Of those that a mesh axis runs over, the one named last changes fastest.
Arguments:
- queries: bfloat16 [256, 256, 512], P(('batch', 'seq'), None, 'mp'), parts along dimension 0, may hold values from -10 to 10
- key_vectors: bfloat16 [256, 256, 512], P(('batch', 'seq'), None, 'mp'), parts along dimension 0, may hold values from -10 to 10
- value_vectors: bfloat16 [256, 256, 512], P(('batch', 'seq'), None, 'mp'), parts along dimension 0, may hold values from -6 to 6
- cotangent: bfloat16 [256, 256, 512], P(('batch', 'seq'), None, 'mp'), parts along dimension 0, may hold values from -6 to 6
- row_pattern: int32 [4, 2, 2], P('mp'), may hold values from 0 to 1, as said below
- column_pattern: int32 [4, 4, 4], P('mp'), may hold values from 0 to 1, as said below
Outputs:
- attended: bfloat16 [256, 256, 512], P(('batch', 'seq'), None, 'mp'), parts along dimension 0
- grad_queries: bfloat16 [256, 256, 512], P(('batch', 'seq'), None, 'mp'), parts along dimension 0
- grad_keys: bfloat16 [256, 256, 512], P(('batch', 'seq'), None, 'mp'), parts along dimension 0
- grad_values: bfloat16 [256, 256, 512], P(('batch', 'seq'), None, 'mp'), parts along dimension 0
The draws below stay inside these ranges and needn't reach their ends.
There are 2 independent parts, one for each index of `batch`. The reference program is written for one: setup_inputs(seed, part) draws one part's arguments, and reference() takes and returns one part's arrays. A program takes and returns all parts, laid end to end along the dimension named above; an argument that names none is the same for every part. Nothing has to cross between parts.
Inputs may be any that keep to these rules, and one draw needn't show every extreme that they name: `row_pattern`: every diagonal entry is 1. `column_pattern`: every diagonal entry is 1 and every entry above the diagonal is 0.
All inputs are finite; a program needn't handle non-finite values.
Results may differ from the reference program's by a relative error of at most 0.04.
Values may be sent and summed in bfloat16 or wider, within the bound.
A program may use at most 64 MiB of HBM per device.

```python
import math
import jax
import jax.numpy as jnp
from jax import lax

HEADS = 8
DH = 64
CBLK = 128
RB = 4
CW = 256
ROWS = 128
FEAT = 512
CB = 2
RBLK = 32


def shared_direction(key):
    return jax.random.rademacher(key, (FEAT,), dtype=jnp.float32)


def drawn(key, direction, spread, reach, lowest, highest, limit):
    first_key, second_key, third_key = jax.random.split(key, 3)
    base = jax.random.normal(first_key, (ROWS, CW, FEAT), jnp.float32) * spread
    strength = jax.random.uniform(second_key, (ROWS, CW, 1), jnp.float32, 0.0, reach)
    row_scale = jnp.exp(jax.random.uniform(third_key, (ROWS, CW, 1), jnp.float32, jnp.log(lowest), jnp.log(highest)))
    return jnp.clip(base * row_scale + strength * direction, -limit, limit).astype(jnp.bfloat16)


def draw_queries(key, part):
    direction = shared_direction(key)
    key = jax.random.fold_in(key, 3)
    return drawn(key, direction, 2.0, 0.0, 1.0, 1.0, 8.0)


def draw_key_vectors(key, part):
    direction = shared_direction(key)
    key = jax.random.fold_in(key, 5)
    return drawn(key, direction, 2.0, 0.0, 1.0, 1.0, 8.0)


def draw_row_pattern(key, part):
    key = jax.random.fold_in(key, 7)
    random_bits = jax.random.randint(key, (HEADS // 2, CB, CB), 0, 2, jnp.int32)
    return jnp.maximum(random_bits, jnp.eye(CB, dtype=jnp.int32)[None])


def draw_column_pattern(key, part):
    key = jax.random.fold_in(key, 9)
    random_bits = jax.random.randint(key, (HEADS // 2, RB, RB), 0, 2, jnp.int32)
    return jnp.tril(random_bits, -1) + jnp.eye(RB, dtype=jnp.int32)[None]


def levels(rng, shape, pieces, smallest, largest):
    gain, own = 1.0, jax.random.fold_in(rng, 6)
    for position, parts in pieces:
        steps = jnp.exp(jax.random.uniform(jax.random.fold_in(own, position), (parts,), jnp.float32, smallest / len(pieces), largest / len(pieces)))
        gain = gain * jnp.repeat(steps, shape[position] // parts).reshape([-1 if axis == position else 1 for axis in range(len(shape))])
    return gain


def centred(rng, shape, width, most, cuts=(), held_as=jnp.bfloat16):
    loudness = levels(rng, shape, cuts, -0.22, 0.18) if cuts else 1.0
    values = jax.random.normal(rng, shape, jnp.float32) * width * loudness
    return jnp.minimum(jnp.maximum(values, -most), most).astype(held_as)


def setup_inputs(seed: int = 0, part: int = 0) -> dict:
    seeds = jax.random.split(jax.random.key(seed), 7)
    part_splits = jax.random.split(jax.random.fold_in(seeds[6], part), 7)
    return {
        "queries": draw_queries(jax.random.fold_in(jax.random.fold_in(seeds[6], part), 71), part),
        "key_vectors": draw_key_vectors(jax.random.fold_in(jax.random.fold_in(seeds[6], part), 71), part),
        "value_vectors": centred(part_splits[2], (ROWS, CW, FEAT), 1.0, 6.0, ((0, 128), (2, 2))),
        "cotangent": centred(part_splits[3], (ROWS, CW, FEAT), 1.0, 6.0, ((0, 128), (2, 2))),
        "row_pattern": draw_row_pattern(jax.random.fold_in(seeds[6], 71), part),
        "column_pattern": draw_column_pattern(jax.random.fold_in(seeds[6], 71), part),
    }


NEG = -1e+30

def product(formula, left, right):
    return jnp.einsum(formula, left.astype(jnp.float32), right.astype(jnp.float32))

def expand(pattern, block):
    return jnp.repeat(jnp.repeat(pattern, block, axis=1), block, axis=2) > 0

def masked_scores(queries, key_block, allowed, layout):
    key_layout = layout.replace('q', 'k')
    scaling = 1.0 / math.sqrt(queries.shape[-1])
    scores = product(layout + ',' + key_layout + '->bhqk', queries, key_block) * scaling
    return jnp.where(allowed, scores, NEG)

def attend(queries, key_block, value_block, allowed, layout):
    key_layout = layout.replace('q', 'k')
    scores = masked_scores(queries, key_block, allowed, layout)
    highest = lax.optimization_barrier(jnp.max(scores, axis=-1))
    log_total = highest + jnp.log(lax.optimization_barrier(jnp.sum(jnp.exp(scores - highest[..., None]), axis=-1)))
    weights = jnp.exp(scores - log_total[..., None]).astype(jnp.bfloat16)
    attended = product('bhqk,' + key_layout + '->' + layout, weights, value_block).astype(jnp.bfloat16)
    return (attended, log_total)

def row_dots(grads, attended, layout):
    return product(layout + ',' + layout + '->bhq', grads, attended)

def backprop(queries, key_block, value_block, grads, log_total, dots, allowed, layout):
    key_layout = layout.replace('q', 'k')
    scaling = 1.0 / math.sqrt(queries.shape[-1])
    scores = masked_scores(queries, key_block, allowed, layout)
    weights = jnp.exp(scores - log_total[..., None])
    rounded = weights.astype(jnp.bfloat16)
    weight_grads = product(layout + ',' + key_layout + '->bhqk', grads, value_block)
    score_grads = (weights * (weight_grads - dots[..., None])).astype(jnp.bfloat16)
    grad_query = product('bhqk,' + key_layout + '->' + layout, score_grads, key_block) * scaling
    grad_key = product('bhqk,' + layout + '->' + key_layout, score_grads, queries) * scaling
    grad_value = product('bhqk,' + layout + '->' + key_layout, rounded, grads)
    return (grad_query, grad_key, grad_value)

def row_heads(queries, key_vectors, value_vectors, cotangent, pattern):
    block_map = expand(pattern, CBLK)
    column_ids = jnp.arange(CW, dtype=jnp.int32)
    same_row = block_map & (column_ids[None, None, :] <= column_ids[None, :, None])
    earlier_row = block_map & (column_ids[None, None, :] > column_ids[None, :, None])
    zero_row = jnp.zeros_like(key_vectors[:1])
    earlier_keys = jnp.concatenate([zero_row, key_vectors[:-1]], axis=0)
    earlier_values = jnp.concatenate([zero_row, value_vectors[:-1]], axis=0)

    def one_row(members):
        query_row, key_before, value_before, key_row, value_row, grad_row, row_index = members
        allowed = jnp.concatenate([earlier_row & (row_index >= 1), same_row], axis=-1)[None]
        key_block = jnp.concatenate([key_before, key_row], axis=0)[None]
        value_block = jnp.concatenate([value_before, value_row], axis=0)[None]
        attended, log_total = attend(query_row[None], key_block, value_block, allowed, 'bqhd')
        dots = row_dots(grad_row[None], attended, 'bqhd')
        grad_query, grad_key, grad_value = backprop(query_row[None], key_block, value_block, grad_row[None], log_total, dots, allowed, 'bqhd')
        return (attended[0], grad_query[0], grad_key[0], grad_value[0])
    row_numbers = jnp.arange(ROWS, dtype=jnp.int32)
    attended, grad_query, key_cat, value_cat = lax.map(one_row, (queries, earlier_keys, earlier_values, key_vectors, value_vectors, cotangent, row_numbers))
    zero_grads = jnp.zeros_like(key_cat[:1, :CW])
    grad_key = key_cat[:, CW:] + jnp.concatenate([key_cat[1:, :CW], zero_grads], axis=0)
    grad_value = value_cat[:, CW:] + jnp.concatenate([value_cat[1:, :CW], zero_grads], axis=0)
    return (attended, grad_query.astype(jnp.bfloat16), grad_key.astype(jnp.bfloat16), grad_value.astype(jnp.bfloat16))

def column_heads(queries, key_vectors, value_vectors, cotangent, pattern):
    block_map = expand(pattern, RBLK)
    row_ids = jnp.arange(ROWS, dtype=jnp.int32)
    allowed = (block_map & (row_ids[None, None, :] <= row_ids[None, :, None]))[None]

    def one_column(members):
        column_q, column_k, column_v, column_g = [member[:, None] for member in members]
        attended, log_total = attend(column_q, column_k, column_v, allowed, 'qbhd')
        dots = row_dots(column_g, attended, 'qbhd')
        grad_query, grad_key, grad_value = backprop(column_q, column_k, column_v, column_g, log_total, dots, allowed, 'qbhd')
        return (attended[:, 0], grad_query[:, 0], grad_key[:, 0], grad_value[:, 0])
    swapped = tuple((jnp.swapaxes(array, 0, 1) for array in (queries, key_vectors, value_vectors, cotangent)))
    results = lax.map(one_column, swapped)
    attended = jnp.swapaxes(results[0], 0, 1)
    grads = tuple((jnp.swapaxes(result, 0, 1).astype(jnp.bfloat16) for result in results[1:]))
    return (attended,) + grads

def grouped(array, start):
    return array.reshape(ROWS, CW, HEADS // 4, 4, DH)[:, :, :, start:start + 2].reshape(ROWS, CW, HEADS // 2, DH)

def joined(first, second):
    shaped = (ROWS, CW, HEADS // 4, 2, DH)
    return jnp.concatenate([first.reshape(shaped), second.reshape(shaped)], axis=3).reshape(ROWS, CW, HEADS * DH)

def reference(queries, key_vectors, value_vectors, cotangent, row_pattern, column_pattern):
    inputs = (queries, key_vectors, value_vectors, cotangent)
    row_results = row_heads(*[grouped(array, 0) for array in inputs], row_pattern)
    column_results = column_heads(*[grouped(array, 2) for array in inputs], column_pattern)
    return (joined(row_results[0], column_results[0]), joined(row_results[1], column_results[1]), joined(row_results[2], column_results[2]), joined(row_results[3], column_results[3]))
```

```python
import jax
import jax.numpy as jnp
from jax import lax
from jax.experimental import pallas as pl
from jax.experimental.pallas import tpu as pltpu
from jax.sharding import PartitionSpec as P

MESH = pl.DeviceIdType.MESH
F32 = jnp.float32
BF16 = jnp.bfloat16
NEG = -1e30

NY = 8
NZX = 16
ROWS = NY * NZX
CW = 256
HALF = 128
DH = 64
PIECES = 4
PAIRS = PIECES // 2
BLOCK = 2 * ROWS
PART = 32
UNROLL = 7
STRIDE = 37
PACK, UNPACK, ZX_TO_Y, Y_TO_ZX, SPREAD, GATHER = range(6)


def iota(shape, axis):
    return lax.broadcasted_iota(jnp.int32, shape, axis)


def matmul(a, b):
    return lax.dot_general(a, b, (((1,), (0,)), ((), ())), preferred_element_type=F32)


def matmul_nt(a, b):
    return lax.dot_general(a, b, (((1,), (1,)), ((), ())), preferred_element_type=F32)


def matmul_tn(a, b):
    return lax.dot_general(a, b, (((0,), (0,)), ((), ())), preferred_element_type=F32)


def per_head(x):
    first = iota(x.shape, 1) < DH
    zero = jnp.zeros_like(x)
    return jnp.concatenate([jnp.where(first, x, zero), jnp.where(first, zero, x)], axis=0)


def both_heads(stacked):
    half = stacked.shape[0] // 2
    top, bottom = stacked[:half], stacked[half:]
    return jnp.where(iota(top.shape, 1) < DH, top, bottom)


def softmax(blocks):
    highest = blocks[0].max(axis=-1, keepdims=True)
    for block in blocks[1:]:
        highest = jnp.maximum(highest, block.max(axis=-1, keepdims=True))
    powers = [jnp.exp(block - highest) for block in blocks]
    total = powers[0].sum(axis=-1, keepdims=True)
    for power in powers[1:]:
        total = total + power.sum(axis=-1, keepdims=True)
    return [power / total for power in powers]


def row_attention(x_ref, kv_ref, pattern_ref, row, out_ref, total_ref):
    total_ref[...] = jnp.zeros_like(total_ref)

    @pl.loop(0, 2)
    def _(b):
        start = pl.multiple_of(b * HALF, HALF)
        rows, window = pl.ds(start, HALF), pl.ds(start, 3 * HALF)
        shape = (2 * HALF, HALF)
        same = iota(shape, 1) <= lax.rem(iota(shape, 0), HALF)
        has_earlier = jnp.broadcast_to(row >= 1, shape)
        first, second = (
            jnp.where(b == 0, pattern_ref[h, 0, 1] * jnp.minimum(row, 1), pattern_ref[h, 1, 0])
            for h in range(2)
        )
        whole_open = jnp.where(iota(shape, 0) < HALF, first, second) > 0
        q = per_head(x_ref[0, rows, :]) * jnp.asarray(0.125, BF16)
        g = per_head(x_ref[1, rows, :])
        keys, values = kv_ref[0, window, :], kv_ref[1, window, :]
        scores, weight_grads = matmul_nt(q, keys), matmul_nt(g, values)

        def chosen(x, earlier_else):
            earlier, whole, this = (x[:, i * HALF : (i + 1) * HALF] for i in range(3))
            return jnp.where(same, this, earlier_else(earlier)), whole

        diag, whole = chosen(scores, lambda x: jnp.where(has_earlier, x, NEG))
        p_diag, p_whole = softmax([diag, jnp.where(whole_open, whole, NEG)])

        def spread(at_diag, at_whole):
            at_diag, at_whole = at_diag.astype(BF16), at_whole.astype(BF16)
            zero = jnp.zeros_like(at_diag)
            return jnp.concatenate(
                [jnp.where(same, zero, at_diag), at_whole, jnp.where(same, at_diag, zero)], axis=1
            )

        w = spread(p_diag, p_whole)
        attended = both_heads(matmul(w, values)).astype(BF16)
        out_ref[0, rows, :] = attended
        wide = attended.astype(F32)
        dots = (g.astype(F32) * jnp.concatenate([wide, wide], axis=0)).sum(-1, keepdims=True)
        d_diag, d_whole = chosen(weight_grads, lambda x: x)
        e = spread(p_diag * (d_diag - dots), p_whole * (d_whole - dots))
        out_ref[1, rows, :] = (both_heads(matmul(e, keys)) * 0.125).astype(BF16)
        total_ref[0, window, :] += matmul_tn(e, q)
        total_ref[1, window, :] += matmul_tn(w, g)


def column_attention(q, k, v, g, bias):
    q = per_head(q) * jnp.asarray(0.125, BF16)
    g = per_head(g)
    (p,) = softmax([matmul_nt(q, k) + bias])
    w = p.astype(BF16)
    attended = both_heads(matmul(w, v)).astype(BF16).astype(F32)
    dots = (g.astype(F32) * jnp.concatenate([attended, attended], axis=0)).sum(-1, keepdims=True)
    e = (p * (matmul_nt(g, v) - dots)).astype(BF16)
    return attended, both_heads(matmul(e, k)) * 0.125, matmul_tn(e, q), matmul_tn(w, g)


def column_bias(pattern_ref):
    shape = (2 * ROWS, ROWS)
    stacked, key = iota(shape, 0), iota(shape, 1)
    query = lax.rem(stacked, ROWS)
    which = query // 32 + jnp.where(stacked < ROWS, 0, 4)
    bits = jnp.zeros(shape, jnp.int32)
    for h in range(2):
        for b in range(4):
            code = sum(pattern_ref[h, b, j] * (1 << j) for j in range(4))
            bits = jnp.where(which == 4 * h + b, code, bits)
    allowed = (key <= query) & (((bits >> (key // 32)) & 1) > 0)
    return jnp.where(allowed, 0.0, NEG)


def reorder(source, target):
    order, size, row = {}, 1, iota((BLOCK, BLOCK), 1)
    for name in reversed(source):
        order[name] = lax.rem(row // size, source[name])
        size *= source[name]
    place = 0
    for name in target:
        place = place * source[name] + order[name]
    return jnp.where(place == iota((BLOCK, BLOCK), 0), 1.0, 0.0).astype(BF16)


def kernel(
    q_hbm, k_hbm, v_hbm, g_hbm, row_pattern_hbm, column_pattern_hbm,
    orow, ocol,
    xc, xr, kv, back, backr, total, perm, bias,
    s1a, r1a, r1b, s2a, r2a, s2b, r2b, found, s3, r3,
    row_pattern, column_pattern, pattern_sem, in_sem, ring_sem, send_sem, recv_sem, back_send_sem, back_recv_sem,
):
    me = lax.axis_index("seq")
    y, zx = me // NZX, lax.rem(me, NZX)
    place_here = {"mp": lax.axis_index("mp"), "batch": lax.axis_index("batch")}
    after = {"seq": lax.rem(me + 1, ROWS), **place_here}
    before = {"seq": lax.rem(me + ROWS - 1, ROWS), **place_here}

    def zx_peer(i):
        other = lax.rem(zx + i, NZX)
        return other, {"seq": y * NZX + other, **place_here}

    def y_peer(i):
        other = lax.rem(y + i, NY)
        return other, {"seq": other * NZX + zx, **place_here}

    inputs = (q_hbm, k_hbm, v_hbm, g_hbm)

    this_row = pl.ds(CW, CW)
    row_places = (xr.at[0], kv.at[0, this_row], kv.at[1, this_row], xr.at[1])

    def loads_of(part, places):
        return [
            pltpu.make_async_copy(h.at[0, :, pl.ds(part * HALF, HALF)], place, in_sem.at[part, i])
            for i, (h, place) in enumerate(zip(inputs, places))
        ]

    column_loads = loads_of(1, [xc.at[i // 2, i % 2] for i in range(PIECES)])
    row_loads = loads_of(0, row_places)
    patterns = [
        pltpu.make_async_copy(row_pattern_hbm, row_pattern, pattern_sem.at[0]),
        pltpu.make_async_copy(column_pattern_hbm, column_pattern, pattern_sem.at[1]),
    ]
    for load in column_loads:
        load.start()

    barrier = pltpu.get_barrier_semaphore()

    def greet(device):
        pl.semaphore_signal(barrier, inc=1, device_id=device, device_id_type=MESH)

    @pl.loop(1, NZX, unroll=True)
    def _(i):
        greet(zx_peer(i)[1])

    @pl.loop(1, NY, unroll=True)
    def _(i):
        greet(y_peer(i)[1])

    greet(after)
    greet(before)
    for load in row_loads + patterns:
        load.start()

    def exchange(step, source, landing, over_zx):
        place = (step, 0 if over_zx else 1)
        count, peer, mine = (NZX, zx_peer, zx) if over_zx else (NY, y_peer, y)

        @pl.loop(1, count, unroll=True)
        def _(i):
            other, device = peer(i)
            pltpu.make_async_remote_copy(
                src_ref=source(other),
                dst_ref=landing(mine),
                send_sem=send_sem.at[place],
                recv_sem=recv_sem.at[place],
                device_id=device,
                device_id_type=MESH,
            ).start()

        pltpu.make_async_copy(source(mine), landing(mine), recv_sem.at[place]).start()

    def send(step, source, dest, over_zx):
        exchange(step, lambda j: source.at[:, j], lambda j: dest.at[:, j], over_zx)

    def arrived(step, whole, over_zx):
        pltpu.make_async_copy(whole, whole, recv_sem.at[step, 0 if over_zx else 1]).wait()

    def sent(step, dest, over_zx):
        part = dest.at[:, pl.ds(0, dest.shape[1] - 1)]
        pltpu.make_async_copy(part, part, send_sem.at[step, 0 if over_zx else 1]).wait()

    def last_columns(j=None):
        rows = pl.ds(HALF, HALF) if j is None else pl.ds(pl.multiple_of(HALF + j * NZX, NZX), NZX)
        return (slice(None), slice(None), rows, slice(None))

    grid_rows = {"piece": 2, "y": NY, "zx": NZX}
    by_zx = ("zx", "piece", "y")
    perm[PACK] = reorder(grid_rows, by_zx)
    for load in column_loads:
        load.wait()
    for p in range(PAIRS):
        rows = xc[p, :, :HALF, :].reshape(BLOCK, HALF)
        s1a[p] = matmul(perm[PACK], rows).astype(BF16).reshape(s1a.shape[1:])
    pl.semaphore_wait(barrier, (NZX - 1) + (NY - 1) + 2)

    send(0, s1a, r1a, True)
    exchange(0, lambda j: xc.at[last_columns(j)], lambda j: r1b.at[:, j], False)
    for load in row_loads:
        load.wait()
    forward = pltpu.make_async_remote_copy(
        src_ref=kv.at[:, this_row],
        dst_ref=kv.at[:, pl.ds(0, CW)],
        send_sem=ring_sem.at[0],
        recv_sem=ring_sem.at[1],
        device_id=after,
        device_id_type=MESH,
    )
    forward.start()

    for t, source, target in (
        (UNPACK, {"zx": NZX, "piece": 2, "y": NY}, ("piece", "y", "zx")),
        (ZX_TO_Y, {"zx": NZX, "piece": 2, "y": NY}, ("y", "piece", "zx")),
        (Y_TO_ZX, {"y": NY, "piece": 2, "zx": NZX}, ("zx", "piece", "y")),
        (SPREAD, {"piece": 2 * PIECES, "row": PART}, ("row", "piece")),
        (GATHER, {"row": PART, "piece": 2 * PIECES}, ("piece", "row")),
    ):
        perm[t] = reorder(source, target)
    for load in patterns:
        load.wait()
    bias[...] = column_bias(column_pattern)

    def swap(dest, source, t):
        for p in range(PAIRS):
            rows = source[p].reshape(BLOCK, HALF)
            dest[p] = matmul(perm[t], rows).astype(BF16).reshape(dest.shape[1:])

    arrived(0, r1a, True)
    swap(s2a, r1a, ZX_TO_Y)
    send(1, s2a, r2a, False)
    arrived(0, r1b, False)
    swap(s2b, r1b, Y_TO_ZX)
    send(1, s2b, r2b, True)

    forward.wait()
    row_attention(xr, kv, row_pattern, me, orow, total)
    back[...] = total[:, :CW, :].astype(BF16)
    backward = pltpu.make_async_remote_copy(
        src_ref=back,
        dst_ref=backr,
        send_sem=ring_sem.at[2],
        recv_sem=ring_sem.at[3],
        device_id=before,
        device_id_type=MESH,
    )
    backward.start()

    arrived(1, r2a, False)
    pieces = [r2a[i // 2, :, i % 2].reshape(ROWS, HALF) for i in range(PIECES)]
    for i, result in enumerate(column_attention(*pieces, bias[...])):
        found[0, i] = result.astype(BF16)
    arrived(1, r2b, True)
    pieces = []
    for p in range(PAIRS):
        rows = matmul(perm[UNPACK], r2b[p].reshape(BLOCK, HALF)).astype(BF16)
        pieces += [rows[:ROWS], rows[ROWS:]]
    for i, result in enumerate(column_attention(*pieces, bias[...])):
        found[1, i] = result.astype(BF16)

    for k in range(ROWS // PART):
        part = pl.ds(k * PART, PART)
        rows = found[:, :, part, :].reshape(BLOCK, HALF)
        s3[part] = matmul(perm[SPREAD], rows).astype(BF16).reshape(PART, 2 * PIECES, HALF)

    mine = back_recv_sem.at[me // PART]

    def send_back(i):
        other = lax.rem(me + i * STRIDE, ROWS)
        pltpu.make_async_remote_copy(
            src_ref=s3.at[other],
            dst_ref=r3.at[me],
            send_sem=back_send_sem,
            recv_sem=mine,
            device_id={"seq": other, **place_here},
            device_id_type=MESH,
        ).start()

    @pl.loop(0, (ROWS - 2) // UNROLL)
    def _(j):
        for u in range(UNROLL):
            send_back(1 + j * UNROLL + u)

    send_back(ROWS - 1)
    pltpu.make_async_copy(s3.at[me], r3.at[me], mine).start()

    backward.wait()
    for i in range(2):
        orow[2 + i] = (total[i, CW:, :] + backr[i].astype(F32)).astype(BF16)

    for k in range(ROWS // PART):
        part = pl.ds(k * PART, PART)
        pltpu.make_async_copy(r3.at[part], r3.at[part], back_recv_sem.at[k]).wait()
        rows = matmul(perm[GATHER], r3[part].reshape(BLOCK, HALF)).astype(BF16)
        for c in range(2):
            for i in range(PIECES):
                start = (c * PIECES + i) * PART
                ocol[i // 2, i % 2, pl.ds(c * HALF + k * PART, PART), :] = rows[start : start + PART]

    for step, (over_zx, over_y) in enumerate(((r1a, r1b), (r2b, r2a))):
        sent(step, over_zx, True)
        sent(step, over_y, False)
    others = s3.at[pl.ds(0, ROWS - 1)]
    pltpu.make_async_copy(others, others, back_send_sem).wait()


def write_out(orow, ocol, o0, o1, o2, o3, sem):
    copies = [
        pltpu.make_async_copy(ref, o.at[0, :, pl.ds(part * HALF, HALF)], sem.at[part, i])
        for i, o in enumerate((o0, o1, o2, o3))
        for part, ref in enumerate((orow.at[i], ocol.at[i // 2, i % 2]))
    ]
    for copy in copies:
        copy.start()
    for copy in copies:
        copy.wait()


def per_device(queries, key_vectors, value_vectors, cotangent, row_pattern, column_pattern):
    by_zx = pltpu.VMEM((PAIRS, NZX, 2 * NY, HALF), BF16)
    by_y = pltpu.VMEM((PAIRS, NY, 2, NZX, HALF), BF16)
    direct = pltpu.VMEM((ROWS, 2 * PIECES, HALF), BF16)
    vmem = pl.BlockSpec(memory_space=pltpu.VMEM)
    hbm = pl.BlockSpec(memory_space=pltpu.HBM)
    halves = pltpu.VMEM((PAIRS, 2, CW, HALF), BF16)
    pair = pltpu.VMEM((2, CW, HALF), BF16)
    in_hbm = [
        pltpu.with_memory_space_constraint(x, pltpu.HBM)
        for x in (queries, key_vectors, value_vectors, cotangent, row_pattern, column_pattern)
    ]
    results = pl.pallas_call(
        kernel,
        out_shape=[pltpu.VMEM((PIECES, CW, HALF), BF16), halves],
        in_specs=[hbm] * 6,
        out_specs=[vmem] * 2,
        scratch_shapes=[
            halves, pair,
            pltpu.VMEM((2, 2 * CW, HALF), BF16),
            pair, pair,
            pltpu.VMEM((2, 2 * CW, HALF), F32),
            pltpu.VMEM((6, BLOCK, BLOCK), BF16),
            pltpu.VMEM((2 * ROWS, ROWS), F32),
            by_zx, by_zx, by_y,
            by_y, by_y, by_zx, by_zx,
            pltpu.VMEM((2, PIECES, ROWS, HALF), BF16),
            direct, direct,
            pltpu.SMEM(row_pattern.shape, jnp.int32),
            pltpu.SMEM(column_pattern.shape, jnp.int32),
            pltpu.SemaphoreType.DMA((2,)),
            pltpu.SemaphoreType.DMA((2, PIECES)),
            pltpu.SemaphoreType.DMA((4,)),
            pltpu.SemaphoreType.DMA((2, 2)),
            pltpu.SemaphoreType.DMA((2, 2)),
            pltpu.SemaphoreType.DMA,
            pltpu.SemaphoreType.DMA((ROWS // PART,)),
        ],
        compiler_params=pltpu.CompilerParams(
            collective_id=0, has_side_effects=True, vmem_limit_bytes=40 * 1024 * 1024
        ),
        cost_estimate=pl.CostEstimate(
            flops=800_000_000, bytes_accessed=1_050_000, transcendentals=200_000
        ),
        name="grid_attention",
    )(*in_hbm)
    return pl.pallas_call(
        write_out,
        out_shape=[jax.ShapeDtypeStruct(queries.shape, BF16)] * 4,
        in_specs=[vmem] * 2,
        out_specs=[hbm] * 4,
        scratch_shapes=[pltpu.SemaphoreType.DMA((2, PIECES))],
        cost_estimate=pl.CostEstimate(flops=0, bytes_accessed=1_050_000, transcendentals=0),
        compiler_params=pltpu.CompilerParams(vmem_limit_bytes=8 * 1024 * 1024),
        name="write_out",
    )(*[pltpu.with_memory_space_constraint(x, pltpu.VMEM) for x in results])


def solution(mesh):
    rows = P(("batch", "seq"), None, "mp")
    heads = P("mp", None, None)
    return jax.shard_map(
        per_device,
        mesh=mesh,
        in_specs=(rows, rows, rows, rows, heads, heads),
        out_specs=(rows, rows, rows, rows),
        check_vma=False,
    )
```

```python
import jax
import jax.numpy as jnp
from jax import lax
from jax.experimental import pallas as pl
from jax.experimental.pallas import tpu as pltpu
from jax.sharding import PartitionSpec as P

MESH = pl.DeviceIdType.MESH
F32 = jnp.float32
BF16 = jnp.bfloat16
NEG = -1e30

NY = 8
NZX = 16
ROWS = NY * NZX
CW = 256
HALF = 128
DH = 64
PIECES = 4
PAIRS = PIECES // 2
BLOCK = 2 * ROWS
PART = 32
PACK, UNPACK, ZX_TO_Y, Y_TO_ZX, SPREAD, GATHER = range(6)


def hops(offset, size):
    return min(offset, size - offset)


def far_first(count, distance):
    return sorted(range(1, count), key=lambda i: (-distance(i), i * 37 % count))


Y_ORDER = far_first(NY, lambda i: hops(i, NY))
ZX_ORDER = far_first(NZX, lambda i: hops(i // 2, NZX // 2) + i % 2)
ALL_ORDER = far_first(ROWS, lambda i: hops(i // NZX, NY) + hops(i % NZX // 2, NZX // 2) + i % 2)


def iota(shape, axis):
    return lax.broadcasted_iota(jnp.int32, shape, axis)


def matmul(a, b):
    return lax.dot_general(a, b, (((1,), (0,)), ((), ())), preferred_element_type=F32)


def matmul_nt(a, b):
    return lax.dot_general(a, b, (((1,), (1,)), ((), ())), preferred_element_type=F32)


def matmul_tn(a, b):
    return lax.dot_general(a, b, (((0,), (0,)), ((), ())), preferred_element_type=F32)


def per_head(x):
    first = iota(x.shape, 1) < DH
    zero = jnp.zeros_like(x)
    return jnp.concatenate([jnp.where(first, x, zero), jnp.where(first, zero, x)], axis=0)


def both_heads(stacked):
    half = stacked.shape[0] // 2
    top, bottom = stacked[:half], stacked[half:]
    return jnp.where(iota(top.shape, 1) < DH, top, bottom)


def softmax(blocks):
    highest = blocks[0].max(axis=-1, keepdims=True)
    for block in blocks[1:]:
        highest = jnp.maximum(highest, block.max(axis=-1, keepdims=True))
    powers = [jnp.exp(block - highest) for block in blocks]
    total = powers[0].sum(axis=-1, keepdims=True)
    for power in powers[1:]:
        total = total + power.sum(axis=-1, keepdims=True)
    return [power / total for power in powers]


def row_attention(x_ref, kv_ref, pattern_ref, row, out_ref, total_ref):
    total_ref[...] = jnp.zeros_like(total_ref)

    for b in range(2):
        start = b * HALF
        rows, window = pl.ds(start, HALF), pl.ds(start, 3 * HALF)
        shape = (2 * HALF, HALF)
        same = iota(shape, 1) <= lax.rem(iota(shape, 0), HALF)
        has_earlier = jnp.broadcast_to(row >= 1, shape)
        first, second = (
            pattern_ref[h, b, 1 - b] * jnp.minimum(row + b, 1)
            for h in range(2)
        )
        whole_open = jnp.where(iota(shape, 0) < HALF, first, second) > 0
        q = per_head(x_ref[0, rows, :]) * jnp.asarray(0.125, BF16)
        g = per_head(x_ref[1, rows, :])
        keys, values = kv_ref[0, window, :], kv_ref[1, window, :]
        scores, weight_grads = matmul_nt(q, keys), matmul_nt(g, values)

        def chosen(x, earlier_else):
            earlier, whole, this = (x[:, i * HALF : (i + 1) * HALF] for i in range(3))
            return jnp.where(same, this, earlier_else(earlier)), whole

        diag, whole = chosen(scores, lambda x: jnp.where(has_earlier, x, NEG))
        p_diag, p_whole = softmax([diag, jnp.where(whole_open, whole, NEG)])

        def spread(at_diag, at_whole):
            at_diag, at_whole = at_diag.astype(BF16), at_whole.astype(BF16)
            zero = jnp.zeros_like(at_diag)
            return jnp.concatenate(
                [jnp.where(same, zero, at_diag), at_whole, jnp.where(same, at_diag, zero)], axis=1
            )

        w = spread(p_diag, p_whole)
        attended = both_heads(matmul(w, values)).astype(BF16)
        out_ref[0, rows, :] = attended
        wide = attended.astype(F32)
        dots = (g.astype(F32) * jnp.concatenate([wide, wide], axis=0)).sum(-1, keepdims=True)
        d_diag, d_whole = chosen(weight_grads, lambda x: x)
        e = spread(p_diag * (d_diag - dots), p_whole * (d_whole - dots))
        out_ref[1, rows, :] = (both_heads(matmul(e, keys)) * 0.125).astype(BF16)
        total_ref[0, window, :] += matmul_tn(e, q)
        total_ref[1, window, :] += matmul_tn(w, g)


def column_attention(q, k, v, g, bias):
    q = per_head(q) * jnp.asarray(0.125, BF16)
    g = per_head(g)
    (p,) = softmax([matmul_nt(q, k) + bias])
    w = p.astype(BF16)
    attended = both_heads(matmul(w, v)).astype(BF16).astype(F32)
    dots = (g.astype(F32) * jnp.concatenate([attended, attended], axis=0)).sum(-1, keepdims=True)
    e = (p * (matmul_nt(g, v) - dots)).astype(BF16)
    return attended, both_heads(matmul(e, k)) * 0.125, matmul_tn(e, q), matmul_tn(w, g)


def column_bias(pattern_ref):
    shape = (2 * ROWS, ROWS)
    stacked, key = iota(shape, 0), iota(shape, 1)
    query = lax.rem(stacked, ROWS)
    which = query // 32 + jnp.where(stacked < ROWS, 0, 4)
    bits = jnp.zeros(shape, jnp.int32)
    for h in range(2):
        for b in range(4):
            code = sum(pattern_ref[h, b, j] * (1 << j) for j in range(4))
            bits = jnp.where(which == 4 * h + b, code, bits)
    allowed = (key <= query) & (((bits >> (key // 32)) & 1) > 0)
    return jnp.where(allowed, 0.0, NEG)


def reorder(source, target):
    order, size, row = {}, 1, iota((BLOCK, BLOCK), 1)
    for name in reversed(source):
        order[name] = lax.rem(row // size, source[name])
        size *= source[name]
    place = 0
    for name in target:
        place = place * source[name] + order[name]
    return jnp.where(place == iota((BLOCK, BLOCK), 0), 1.0, 0.0).astype(BF16)


def kernel(
    q_hbm, k_hbm, v_hbm, g_hbm, row_pattern_hbm, column_pattern_hbm,
    orow, ocol,
    xc, xr, kv, back, backr, total, perm, bias,
    s1a, r1a, r1b, s2a, r2a, s2b, r2b, found, s3, r3,
    row_pattern, column_pattern, pattern_sem, in_sem, ring_sem, send_sem, recv_sem, back_send_sem, back_recv_sem,
):
    me = lax.axis_index("seq")
    y, zx = me // NZX, lax.rem(me, NZX)
    place_here = {"mp": lax.axis_index("mp"), "batch": lax.axis_index("batch")}
    after = {"seq": lax.rem(me + 1, ROWS), **place_here}
    before = {"seq": lax.rem(me + ROWS - 1, ROWS), **place_here}

    zx_places = [lax.rem(zx + i, NZX) for i in range(NZX)]
    y_places = [lax.rem(y + i, NY) for i in range(NY)]

    def device(seq):
        return {"seq": seq, **place_here}

    zx_peers = [(zx_places[i], device(y * NZX + zx_places[i])) for i in ZX_ORDER]
    y_peers = [(y_places[i], device(y_places[i] * NZX + zx)) for i in Y_ORDER]

    inputs = (q_hbm, k_hbm, v_hbm, g_hbm)

    this_row = pl.ds(CW, CW)
    row_places = (xr.at[0], kv.at[0, this_row], kv.at[1, this_row], xr.at[1])

    def loads_of(part, places):
        return [
            pltpu.make_async_copy(h.at[0, :, pl.ds(part * HALF, HALF)], place, in_sem.at[part, i])
            for i, (h, place) in enumerate(zip(inputs, places))
        ]

    column_loads = loads_of(1, [xc.at[i // 2, i % 2] for i in range(PIECES)])
    row_loads = loads_of(0, row_places)
    patterns = [
        pltpu.make_async_copy(row_pattern_hbm, row_pattern, pattern_sem.at[0]),
        pltpu.make_async_copy(column_pattern_hbm, column_pattern, pattern_sem.at[1]),
    ]
    for load in column_loads:
        load.start()

    barrier = pltpu.get_barrier_semaphore()

    def greet(peer):
        pl.semaphore_signal(barrier, inc=1, device_id=peer, device_id_type=MESH)

    for _, peer in zx_peers + y_peers:
        greet(peer)
    greet(after)
    greet(before)
    for load in row_loads + patterns:
        load.start()

    def exchange(step, source, landing, over_zx):
        place = (step, 0 if over_zx else 1)
        peers, mine = (zx_peers, zx) if over_zx else (y_peers, y)
        for other, peer in peers:
            pltpu.make_async_remote_copy(
                src_ref=source(other),
                dst_ref=landing(mine),
                send_sem=send_sem.at[place],
                recv_sem=recv_sem.at[place],
                device_id=peer,
                device_id_type=MESH,
            ).start()
        pltpu.make_async_copy(source(mine), landing(mine), recv_sem.at[place]).start()

    def send(step, source, dest, over_zx):
        exchange(step, lambda j: source.at[:, j], lambda j: dest.at[:, j], over_zx)

    def arrived(step, whole, over_zx):
        pltpu.make_async_copy(whole, whole, recv_sem.at[step, 0 if over_zx else 1]).wait()

    def sent(step, dest, over_zx):
        part = dest.at[:, pl.ds(0, dest.shape[1] - 1)]
        pltpu.make_async_copy(part, part, send_sem.at[step, 0 if over_zx else 1]).wait()

    def last_columns(j=None):
        rows = pl.ds(HALF, HALF) if j is None else pl.ds(pl.multiple_of(HALF + j * NZX, NZX), NZX)
        return (slice(None), slice(None), rows, slice(None))

    grid_rows = {"piece": 2, "y": NY, "zx": NZX}
    by_zx = ("zx", "piece", "y")
    perm[PACK] = reorder(grid_rows, by_zx)
    for load in column_loads:
        load.wait()
    for p in range(PAIRS):
        rows = xc[p, :, :HALF, :].reshape(BLOCK, HALF)
        s1a[p] = matmul(perm[PACK], rows).astype(BF16).reshape(s1a.shape[1:])
    pl.semaphore_wait(barrier, (NZX - 1) + (NY - 1) + 2)

    send(0, s1a, r1a, True)
    exchange(0, lambda j: xc.at[last_columns(j)], lambda j: r1b.at[:, j], False)
    for load in row_loads:
        load.wait()
    forward = pltpu.make_async_remote_copy(
        src_ref=kv.at[:, this_row],
        dst_ref=kv.at[:, pl.ds(0, CW)],
        send_sem=ring_sem.at[0],
        recv_sem=ring_sem.at[1],
        device_id=after,
        device_id_type=MESH,
    )
    forward.start()

    for t, source, target in (
        (UNPACK, {"zx": NZX, "piece": 2, "y": NY}, ("piece", "y", "zx")),
        (ZX_TO_Y, {"zx": NZX, "piece": 2, "y": NY}, ("y", "piece", "zx")),
        (Y_TO_ZX, {"y": NY, "piece": 2, "zx": NZX}, ("zx", "piece", "y")),
        (SPREAD, {"piece": 2 * PIECES, "row": PART}, ("row", "piece")),
        (GATHER, {"row": PART, "piece": 2 * PIECES}, ("piece", "row")),
    ):
        perm[t] = reorder(source, target)
    for load in patterns:
        load.wait()
    bias[...] = column_bias(column_pattern)

    def swap(dest, source, t):
        for p in range(PAIRS):
            rows = source[p].reshape(BLOCK, HALF)
            dest[p] = matmul(perm[t], rows).astype(BF16).reshape(dest.shape[1:])

    arrived(0, r1a, True)
    swap(s2a, r1a, ZX_TO_Y)
    send(1, s2a, r2a, False)
    arrived(0, r1b, False)
    swap(s2b, r1b, Y_TO_ZX)
    send(1, s2b, r2b, True)

    forward.wait()
    row_attention(xr, kv, row_pattern, me, orow, total)
    back[...] = total[:, :CW, :].astype(BF16)
    backward = pltpu.make_async_remote_copy(
        src_ref=back,
        dst_ref=backr,
        send_sem=ring_sem.at[2],
        recv_sem=ring_sem.at[3],
        device_id=before,
        device_id_type=MESH,
    )
    backward.start()

    arrived(1, r2a, False)
    pieces = [r2a[i // 2, :, i % 2].reshape(ROWS, HALF) for i in range(PIECES)]
    for i, result in enumerate(column_attention(*pieces, bias[...])):
        found[0, i] = result.astype(BF16)
    arrived(1, r2b, True)
    pieces = []
    for p in range(PAIRS):
        rows = matmul(perm[UNPACK], r2b[p].reshape(BLOCK, HALF)).astype(BF16)
        pieces += [rows[:ROWS], rows[ROWS:]]
    for i, result in enumerate(column_attention(*pieces, bias[...])):
        found[1, i] = result.astype(BF16)

    for k in range(ROWS // PART):
        part = pl.ds(k * PART, PART)
        rows = found[:, :, part, :].reshape(BLOCK, HALF)
        s3[part] = matmul(perm[SPREAD], rows).astype(BF16).reshape(PART, 2 * PIECES, HALF)

    for i in ALL_ORDER:
        other = y_places[i // NZX] * NZX + zx_places[i % NZX]
        pltpu.make_async_remote_copy(
            src_ref=s3.at[other],
            dst_ref=r3.at[me],
            send_sem=back_send_sem,
            recv_sem=back_recv_sem,
            device_id=device(other),
            device_id_type=MESH,
        ).start()
    pltpu.make_async_copy(s3.at[me], r3.at[me], back_recv_sem).start()

    backward.wait()
    for i in range(2):
        orow[2 + i] = (total[i, CW:, :] + backr[i].astype(F32)).astype(BF16)

    pltpu.make_async_copy(r3, r3, back_recv_sem).wait()
    for k in range(ROWS // PART):
        part = pl.ds(k * PART, PART)
        rows = matmul(perm[GATHER], r3[part].reshape(BLOCK, HALF)).astype(BF16)
        for c in range(2):
            for i in range(PIECES):
                start = (c * PIECES + i) * PART
                ocol[i // 2, i % 2, pl.ds(c * HALF + k * PART, PART), :] = rows[start : start + PART]

    for step, (over_zx, over_y) in enumerate(((r1a, r1b), (r2b, r2a))):
        sent(step, over_zx, True)
        sent(step, over_y, False)
    others = s3.at[pl.ds(0, ROWS - 1)]
    pltpu.make_async_copy(others, others, back_send_sem).wait()


def write_out(orow, ocol, o0, o1, o2, o3, sem):
    copies = [
        pltpu.make_async_copy(ref, o.at[0, :, pl.ds(part * HALF, HALF)], sem.at[part, i])
        for i, o in enumerate((o0, o1, o2, o3))
        for part, ref in enumerate((orow.at[i], ocol.at[i // 2, i % 2]))
    ]
    for copy in copies:
        copy.start()
    for copy in copies:
        copy.wait()


def per_device(queries, key_vectors, value_vectors, cotangent, row_pattern, column_pattern):
    by_zx = pltpu.VMEM((PAIRS, NZX, 2 * NY, HALF), BF16)
    by_y = pltpu.VMEM((PAIRS, NY, 2, NZX, HALF), BF16)
    direct = pltpu.VMEM((ROWS, 2 * PIECES, HALF), BF16)
    vmem = pl.BlockSpec(memory_space=pltpu.VMEM)
    hbm = pl.BlockSpec(memory_space=pltpu.HBM)
    halves = pltpu.VMEM((PAIRS, 2, CW, HALF), BF16)
    pair = pltpu.VMEM((2, CW, HALF), BF16)
    in_hbm = [
        pltpu.with_memory_space_constraint(x, pltpu.HBM)
        for x in (queries, key_vectors, value_vectors, cotangent, row_pattern, column_pattern)
    ]
    results = pl.pallas_call(
        kernel,
        out_shape=[pltpu.VMEM((PIECES, CW, HALF), BF16), halves],
        in_specs=[hbm] * 6,
        out_specs=[vmem] * 2,
        scratch_shapes=[
            halves, pair,
            pltpu.VMEM((2, 2 * CW, HALF), BF16),
            pair, pair,
            pltpu.VMEM((2, 2 * CW, HALF), F32),
            pltpu.VMEM((6, BLOCK, BLOCK), BF16),
            pltpu.VMEM((2 * ROWS, ROWS), F32),
            by_zx, by_zx, by_y,
            by_y, by_y, by_zx, by_zx,
            pltpu.VMEM((2, PIECES, ROWS, HALF), BF16),
            direct, direct,
            pltpu.SMEM(row_pattern.shape, jnp.int32),
            pltpu.SMEM(column_pattern.shape, jnp.int32),
            pltpu.SemaphoreType.DMA((2,)),
            pltpu.SemaphoreType.DMA((2, PIECES)),
            pltpu.SemaphoreType.DMA((4,)),
            pltpu.SemaphoreType.DMA((2, 2)),
            pltpu.SemaphoreType.DMA((2, 2)),
            pltpu.SemaphoreType.DMA,
            pltpu.SemaphoreType.DMA,
        ],
        compiler_params=pltpu.CompilerParams(
            collective_id=0, has_side_effects=True, vmem_limit_bytes=40 * 1024 * 1024
        ),
        cost_estimate=pl.CostEstimate(
            flops=800_000_000, bytes_accessed=1_050_000, transcendentals=200_000
        ),
        name="grid_attention",
    )(*in_hbm)
    return pl.pallas_call(
        write_out,
        out_shape=[jax.ShapeDtypeStruct(queries.shape, BF16)] * 4,
        in_specs=[vmem] * 2,
        out_specs=[hbm] * 4,
        scratch_shapes=[pltpu.SemaphoreType.DMA((2, PIECES))],
        cost_estimate=pl.CostEstimate(flops=0, bytes_accessed=1_050_000, transcendentals=0),
        compiler_params=pltpu.CompilerParams(vmem_limit_bytes=8 * 1024 * 1024),
        name="write_out",
    )(*[pltpu.with_memory_space_constraint(x, pltpu.VMEM) for x in results])


def solution(mesh):
    rows = P(("batch", "seq"), None, "mp")
    heads = P("mp", None, None)
    return jax.shard_map(
        per_device,
        mesh=mesh,
        in_specs=(rows, rows, rows, rows, heads, heads),
        out_specs=(rows, rows, rows, rows),
        check_vma=False,
    )
```

```python
import jax
import jax.numpy as jnp
from jax import lax
from jax.experimental import pallas as pl
from jax.experimental.pallas import tpu as pltpu
from jax.sharding import PartitionSpec as P

MESH = pl.DeviceIdType.MESH
F32 = jnp.float32
BF16 = jnp.bfloat16
NEG = -1e30

NY = 8
NZX = 16
ROWS = NY * NZX
CW = 256
HALF = 128
DH = 64
PIECES = 4
PAIRS = PIECES // 2
BLOCK = 2 * ROWS
PART = 32
PACK, UNPACK, ZX_TO_Y, Y_TO_ZX, SPREAD, GATHER = range(6)


def hops(offset, size):
    return min(offset, size - offset)


def far_first(count, distance):
    return sorted(range(1, count), key=lambda i: (-distance(i), i * 37 % count))


Y_ORDER = far_first(NY, lambda i: hops(i, NY))
ZX_ORDER = far_first(NZX, lambda i: hops(i // 2, NZX // 2) + i % 2)
ALL_ORDER = far_first(ROWS, lambda i: hops(i // NZX, NY) + hops(i % NZX // 2, NZX // 2) + i % 2)


def iota(shape, axis):
    return lax.broadcasted_iota(jnp.int32, shape, axis)


def matmul(a, b):
    return lax.dot_general(a, b, (((1,), (0,)), ((), ())), preferred_element_type=F32)


def matmul_nt(a, b):
    return lax.dot_general(a, b, (((1,), (1,)), ((), ())), preferred_element_type=F32)


def matmul_tn(a, b):
    return lax.dot_general(a, b, (((0,), (0,)), ((), ())), preferred_element_type=F32)


def per_head(x):
    first = iota(x.shape, 1) < DH
    zero = jnp.zeros_like(x)
    return jnp.concatenate([jnp.where(first, x, zero), jnp.where(first, zero, x)], axis=0)


def both_heads(stacked):
    half = stacked.shape[0] // 2
    top, bottom = stacked[:half], stacked[half:]
    return jnp.where(iota(top.shape, 1) < DH, top, bottom)


def softmax(blocks):
    highest = blocks[0].max(axis=-1, keepdims=True)
    for block in blocks[1:]:
        highest = jnp.maximum(highest, block.max(axis=-1, keepdims=True))
    powers = [jnp.exp(block - highest) for block in blocks]
    total = powers[0].sum(axis=-1, keepdims=True)
    for power in powers[1:]:
        total = total + power.sum(axis=-1, keepdims=True)
    return [power / total for power in powers]


def row_attention(x_ref, kv_ref, pattern_ref, row, out_ref, total_ref):
    total_ref[...] = jnp.zeros_like(total_ref)

    for b in range(2):
        start = b * HALF
        rows, window = pl.ds(start, HALF), pl.ds(start, 3 * HALF)
        shape = (2 * HALF, HALF)
        same = iota(shape, 1) <= lax.rem(iota(shape, 0), HALF)
        has_earlier = jnp.broadcast_to(row >= 1, shape)
        first, second = (
            pattern_ref[h, b, 1 - b] * jnp.minimum(row + b, 1)
            for h in range(2)
        )
        whole_open = jnp.where(iota(shape, 0) < HALF, first, second) > 0
        q = per_head(x_ref[0, rows, :]) * jnp.asarray(0.125, BF16)
        g = per_head(x_ref[1, rows, :])
        keys, values = kv_ref[0, window, :], kv_ref[1, window, :]
        scores, weight_grads = matmul_nt(q, keys), matmul_nt(g, values)

        def chosen(x, earlier_else):
            earlier, whole, this = (x[:, i * HALF : (i + 1) * HALF] for i in range(3))
            return jnp.where(same, this, earlier_else(earlier)), whole

        diag, whole = chosen(scores, lambda x: jnp.where(has_earlier, x, NEG))
        p_diag, p_whole = softmax([diag, jnp.where(whole_open, whole, NEG)])

        def spread(at_diag, at_whole):
            at_diag, at_whole = at_diag.astype(BF16), at_whole.astype(BF16)
            zero = jnp.zeros_like(at_diag)
            return jnp.concatenate(
                [jnp.where(same, zero, at_diag), at_whole, jnp.where(same, at_diag, zero)], axis=1
            )

        w = spread(p_diag, p_whole)
        attended = both_heads(matmul(w, values)).astype(BF16)
        out_ref[0, rows, :] = attended
        wide = attended.astype(F32)
        dots = (g.astype(F32) * jnp.concatenate([wide, wide], axis=0)).sum(-1, keepdims=True)
        d_diag, d_whole = chosen(weight_grads, lambda x: x)
        e = spread(p_diag * (d_diag - dots), p_whole * (d_whole - dots))
        out_ref[1, rows, :] = (both_heads(matmul(e, keys)) * 0.125).astype(BF16)
        total_ref[0, window, :] += matmul_tn(e, q)
        total_ref[1, window, :] += matmul_tn(w, g)


def column_attention(q, k, v, g, bias):
    q = per_head(q) * jnp.asarray(0.125, BF16)
    g = per_head(g)
    (p,) = softmax([matmul_nt(q, k) + bias])
    w = p.astype(BF16)
    attended = both_heads(matmul(w, v)).astype(BF16).astype(F32)
    dots = (g.astype(F32) * jnp.concatenate([attended, attended], axis=0)).sum(-1, keepdims=True)
    e = (p * (matmul_nt(g, v) - dots)).astype(BF16)
    return attended, both_heads(matmul(e, k)) * 0.125, matmul_tn(e, q), matmul_tn(w, g)


def column_bias(pattern_ref):
    shape = (2 * ROWS, ROWS)
    stacked, key = iota(shape, 0), iota(shape, 1)
    query = lax.rem(stacked, ROWS)
    which = query // 32 + jnp.where(stacked < ROWS, 0, 4)
    bits = jnp.zeros(shape, jnp.int32)
    for h in range(2):
        for b in range(4):
            code = sum(pattern_ref[h, b, j] * (1 << j) for j in range(4))
            bits = jnp.where(which == 4 * h + b, code, bits)
    allowed = (key <= query) & (((bits >> (key // 32)) & 1) > 0)
    return jnp.where(allowed, 0.0, NEG)


def reorder(source, target):
    order, size, row = {}, 1, iota((BLOCK, BLOCK), 1)
    for name in reversed(source):
        order[name] = lax.rem(row // size, source[name])
        size *= source[name]
    place = 0
    for name in target:
        place = place * source[name] + order[name]
    return jnp.where(place == iota((BLOCK, BLOCK), 0), 1.0, 0.0).astype(BF16)


def kernel(
    q_hbm, k_hbm, v_hbm, g_hbm, row_pattern_hbm, column_pattern_hbm,
    orow, ocol,
    xc, xr, kv, back, backr, total, perm, bias,
    s1a, r1a, r1b, s2a, r2a, s2b, r2b, found, s3, r3,
    row_pattern, column_pattern, pattern_sem, in_sem, ring_sem, send_sem, recv_sem, back_send_sem, back_recv_sem,
):
    me = lax.axis_index("seq")
    y, zx = me // NZX, lax.rem(me, NZX)
    place_here = {"mp": lax.axis_index("mp"), "batch": lax.axis_index("batch")}
    after = {"seq": lax.rem(me + 1, ROWS), **place_here}
    before = {"seq": lax.rem(me + ROWS - 1, ROWS), **place_here}

    zx_places = [lax.rem(zx + i, NZX) for i in range(NZX)]
    y_places = [lax.rem(y + i, NY) for i in range(NY)]

    def device(seq):
        return {"seq": seq, **place_here}

    zx_peers = [(zx_places[i], device(y * NZX + zx_places[i])) for i in ZX_ORDER]
    y_peers = [(y_places[i], device(y_places[i] * NZX + zx)) for i in Y_ORDER]

    inputs = (q_hbm, k_hbm, v_hbm, g_hbm)

    this_row = pl.ds(CW, CW)
    row_places = (xr.at[0], kv.at[0, this_row], kv.at[1, this_row], xr.at[1])

    def loads_of(part, places):
        return [
            pltpu.make_async_copy(h.at[0, :, pl.ds(part * HALF, HALF)], place, in_sem.at[part, i])
            for i, (h, place) in enumerate(zip(inputs, places))
        ]

    column_loads = loads_of(1, [xc.at[i // 2, i % 2] for i in range(PIECES)])
    row_loads = loads_of(0, row_places)
    patterns = [
        pltpu.make_async_copy(row_pattern_hbm, row_pattern, pattern_sem.at[0]),
        pltpu.make_async_copy(column_pattern_hbm, column_pattern, pattern_sem.at[1]),
    ]
    for load in column_loads:
        load.start()

    barrier = pltpu.get_barrier_semaphore()

    def greet(peer):
        pl.semaphore_signal(barrier, inc=1, device_id=peer, device_id_type=MESH)

    for _, peer in zx_peers + y_peers:
        greet(peer)
    greet(after)
    greet(before)
    for load in row_loads + patterns:
        load.start()

    def exchange(step, source, landing, over_zx):
        place = (step, 0 if over_zx else 1)
        peers, mine = (zx_peers, zx) if over_zx else (y_peers, y)
        for other, peer in peers:
            pltpu.make_async_remote_copy(
                src_ref=source(other),
                dst_ref=landing(mine),
                send_sem=send_sem.at[place],
                recv_sem=recv_sem.at[place],
                device_id=peer,
                device_id_type=MESH,
            ).start()
        pltpu.make_async_copy(source(mine), landing(mine), recv_sem.at[place]).start()

    def send(step, source, dest, over_zx):
        exchange(step, lambda j: source.at[:, j], lambda j: dest.at[:, j], over_zx)

    def arrived(step, whole, over_zx):
        pltpu.make_async_copy(whole, whole, recv_sem.at[step, 0 if over_zx else 1]).wait()

    def sent(step, dest, over_zx):
        part = dest.at[:, pl.ds(0, dest.shape[1] - 1)]
        pltpu.make_async_copy(part, part, send_sem.at[step, 0 if over_zx else 1]).wait()

    def last_columns(j=None):
        rows = pl.ds(HALF, HALF) if j is None else pl.ds(pl.multiple_of(HALF + j * NZX, NZX), NZX)
        return (slice(None), slice(None), rows, slice(None))

    grid_rows = {"piece": 2, "y": NY, "zx": NZX}
    by_zx = ("zx", "piece", "y")
    perm[PACK] = reorder(grid_rows, by_zx)
    for load in column_loads:
        load.wait()
    for p in range(PAIRS):
        rows = xc[p, :, :HALF, :].reshape(BLOCK, HALF)
        s1a[p] = matmul(perm[PACK], rows).astype(BF16).reshape(s1a.shape[1:])
    pl.semaphore_wait(barrier, (NZX - 1) + (NY - 1) + 2)

    send(0, s1a, r1a, True)
    exchange(0, lambda j: xc.at[last_columns(j)], lambda j: r1b.at[:, j], False)
    for load in row_loads:
        load.wait()
    forward = pltpu.make_async_remote_copy(
        src_ref=kv.at[:, this_row],
        dst_ref=kv.at[:, pl.ds(0, CW)],
        send_sem=ring_sem.at[0],
        recv_sem=ring_sem.at[1],
        device_id=after,
        device_id_type=MESH,
    )
    forward.start()

    for t, source, target in (
        (UNPACK, {"zx": NZX, "piece": 2, "y": NY}, ("piece", "y", "zx")),
        (ZX_TO_Y, {"zx": NZX, "piece": 2, "y": NY}, ("y", "piece", "zx")),
        (Y_TO_ZX, {"y": NY, "piece": 2, "zx": NZX}, ("zx", "piece", "y")),
        (SPREAD, {"piece": 2 * PIECES, "row": PART}, ("row", "piece")),
        (GATHER, {"row": PART, "piece": 2 * PIECES}, ("piece", "row")),
    ):
        perm[t] = reorder(source, target)
    for load in patterns:
        load.wait()
    bias[...] = column_bias(column_pattern)

    def swap(dest, source, t):
        for p in range(PAIRS):
            rows = source[p].reshape(BLOCK, HALF)
            dest[p] = matmul(perm[t], rows).astype(BF16).reshape(dest.shape[1:])

    arrived(0, r1b, False)
    swap(s2b, r1b, Y_TO_ZX)
    send(1, s2b, r2b, True)
    arrived(0, r1a, True)
    swap(s2a, r1a, ZX_TO_Y)
    send(1, s2a, r2a, False)

    forward.wait()
    row_attention(xr, kv, row_pattern, me, orow, total)
    back[...] = total[:, :CW, :].astype(BF16)
    backward = pltpu.make_async_remote_copy(
        src_ref=back,
        dst_ref=backr,
        send_sem=ring_sem.at[2],
        recv_sem=ring_sem.at[3],
        device_id=before,
        device_id_type=MESH,
    )
    backward.start()

    arrived(1, r2b, True)
    pieces = []
    for p in range(PAIRS):
        rows = matmul(perm[UNPACK], r2b[p].reshape(BLOCK, HALF)).astype(BF16)
        pieces += [rows[:ROWS], rows[ROWS:]]
    for i, result in enumerate(column_attention(*pieces, bias[...])):
        found[1, i] = result.astype(BF16)
    arrived(1, r2a, False)
    pieces = [r2a[i // 2, :, i % 2].reshape(ROWS, HALF) for i in range(PIECES)]
    for i, result in enumerate(column_attention(*pieces, bias[...])):
        found[0, i] = result.astype(BF16)

    for k in range(ROWS // PART):
        part = pl.ds(k * PART, PART)
        rows = found[:, :, part, :].reshape(BLOCK, HALF)
        s3[part] = matmul(perm[SPREAD], rows).astype(BF16).reshape(PART, 2 * PIECES, HALF)

    for i in ALL_ORDER:
        other = y_places[i // NZX] * NZX + zx_places[i % NZX]
        pltpu.make_async_remote_copy(
            src_ref=s3.at[other],
            dst_ref=r3.at[me],
            send_sem=back_send_sem,
            recv_sem=back_recv_sem,
            device_id=device(other),
            device_id_type=MESH,
        ).start()
    pltpu.make_async_copy(s3.at[me], r3.at[me], back_recv_sem).start()

    backward.wait()
    for i in range(2):
        orow[2 + i] = (total[i, CW:, :] + backr[i].astype(F32)).astype(BF16)

    pltpu.make_async_copy(r3, r3, back_recv_sem).wait()
    for k in range(ROWS // PART):
        part = pl.ds(k * PART, PART)
        rows = matmul(perm[GATHER], r3[part].reshape(BLOCK, HALF)).astype(BF16)
        for c in range(2):
            for i in range(PIECES):
                start = (c * PIECES + i) * PART
                ocol[i // 2, i % 2, pl.ds(c * HALF + k * PART, PART), :] = rows[start : start + PART]

    for step, (over_zx, over_y) in enumerate(((r1a, r1b), (r2b, r2a))):
        sent(step, over_zx, True)
        sent(step, over_y, False)
    others = s3.at[pl.ds(0, ROWS - 1)]
    pltpu.make_async_copy(others, others, back_send_sem).wait()


def write_out(orow, ocol, o0, o1, o2, o3, sem):
    copies = [
        pltpu.make_async_copy(ref, o.at[0, :, pl.ds(part * HALF, HALF)], sem.at[part, i])
        for i, o in enumerate((o0, o1, o2, o3))
        for part, ref in enumerate((orow.at[i], ocol.at[i // 2, i % 2]))
    ]
    for copy in copies:
        copy.start()
    for copy in copies:
        copy.wait()


def per_device(queries, key_vectors, value_vectors, cotangent, row_pattern, column_pattern):
    by_zx = pltpu.VMEM((PAIRS, NZX, 2 * NY, HALF), BF16)
    by_y = pltpu.VMEM((PAIRS, NY, 2, NZX, HALF), BF16)
    direct = pltpu.VMEM((ROWS, 2 * PIECES, HALF), BF16)
    vmem = pl.BlockSpec(memory_space=pltpu.VMEM)
    hbm = pl.BlockSpec(memory_space=pltpu.HBM)
    halves = pltpu.VMEM((PAIRS, 2, CW, HALF), BF16)
    pair = pltpu.VMEM((2, CW, HALF), BF16)
    in_hbm = [
        pltpu.with_memory_space_constraint(x, pltpu.HBM)
        for x in (queries, key_vectors, value_vectors, cotangent, row_pattern, column_pattern)
    ]
    results = pl.pallas_call(
        kernel,
        out_shape=[pltpu.VMEM((PIECES, CW, HALF), BF16), halves],
        in_specs=[hbm] * 6,
        out_specs=[vmem] * 2,
        scratch_shapes=[
            halves, pair,
            pltpu.VMEM((2, 2 * CW, HALF), BF16),
            pair, pair,
            pltpu.VMEM((2, 2 * CW, HALF), F32),
            pltpu.VMEM((6, BLOCK, BLOCK), BF16),
            pltpu.VMEM((2 * ROWS, ROWS), F32),
            by_zx, by_zx, by_y,
            by_y, by_y, by_zx, by_zx,
            pltpu.VMEM((2, PIECES, ROWS, HALF), BF16),
            direct, direct,
            pltpu.SMEM(row_pattern.shape, jnp.int32),
            pltpu.SMEM(column_pattern.shape, jnp.int32),
            pltpu.SemaphoreType.DMA((2,)),
            pltpu.SemaphoreType.DMA((2, PIECES)),
            pltpu.SemaphoreType.DMA((4,)),
            pltpu.SemaphoreType.DMA((2, 2)),
            pltpu.SemaphoreType.DMA((2, 2)),
            pltpu.SemaphoreType.DMA,
            pltpu.SemaphoreType.DMA,
        ],
        compiler_params=pltpu.CompilerParams(
            collective_id=0, has_side_effects=True, vmem_limit_bytes=40 * 1024 * 1024
        ),
        cost_estimate=pl.CostEstimate(
            flops=800_000_000, bytes_accessed=1_050_000, transcendentals=200_000
        ),
        name="grid_attention",
    )(*in_hbm)
    return pl.pallas_call(
        write_out,
        out_shape=[jax.ShapeDtypeStruct(queries.shape, BF16)] * 4,
        in_specs=[vmem] * 2,
        out_specs=[hbm] * 4,
        scratch_shapes=[pltpu.SemaphoreType.DMA((2, PIECES))],
        cost_estimate=pl.CostEstimate(flops=0, bytes_accessed=1_050_000, transcendentals=0),
        compiler_params=pltpu.CompilerParams(vmem_limit_bytes=8 * 1024 * 1024),
        name="write_out",
    )(*[pltpu.with_memory_space_constraint(x, pltpu.VMEM) for x in results])


def solution(mesh):
    rows = P(("batch", "seq"), None, "mp")
    heads = P("mp", None, None)
    return jax.shard_map(
        per_device,
        mesh=mesh,
        in_specs=(rows, rows, rows, rows, heads, heads),
        out_specs=(rows, rows, rows, rows),
        check_vma=False,
    )
```

```python
import jax
import jax.numpy as jnp
from jax import lax
from jax.experimental import pallas as pl
from jax.experimental.pallas import tpu as pltpu
from jax.sharding import PartitionSpec as P

MESH = pl.DeviceIdType.MESH
F32 = jnp.float32
BF16 = jnp.bfloat16
NEG = -1e30

NY = 8
NZX = 16
ROWS = NY * NZX
CW = 256
HALF = 128
DH = 64
PIECES = 4
PAIRS = PIECES // 2
BLOCK = 2 * ROWS
PART = 32
PACK, UNPACK, ZX_TO_Y, Y_TO_ZX, SPREAD, GATHER = range(6)


def hops(offset, size):
    return min(offset, size - offset)


def far_first(count, distance):
    return sorted(range(1, count), key=lambda i: (-distance(i), i * 37 % count))


Y_ORDER = far_first(NY, lambda i: hops(i, NY))
ZX_ORDER = far_first(NZX, lambda i: hops(i // 2, NZX // 2) + i % 2)
ALL_ORDER = far_first(ROWS, lambda i: hops(i // NZX, NY) + hops(i % NZX // 2, NZX // 2) + i % 2)


def iota(shape, axis):
    return lax.broadcasted_iota(jnp.int32, shape, axis)


def matmul(a, b):
    return lax.dot_general(a, b, (((1,), (0,)), ((), ())), preferred_element_type=F32)


def matmul_nt(a, b):
    return lax.dot_general(a, b, (((1,), (1,)), ((), ())), preferred_element_type=F32)


def matmul_tn(a, b):
    return lax.dot_general(a, b, (((0,), (0,)), ((), ())), preferred_element_type=F32)


def per_head(x):
    first = iota(x.shape, 1) < DH
    zero = jnp.zeros_like(x)
    return jnp.concatenate([jnp.where(first, x, zero), jnp.where(first, zero, x)], axis=0)


def both_heads(stacked):
    half = stacked.shape[0] // 2
    top, bottom = stacked[:half], stacked[half:]
    return jnp.where(iota(top.shape, 1) < DH, top, bottom)


def softmax(blocks):
    highest = blocks[0].max(axis=-1, keepdims=True)
    for block in blocks[1:]:
        highest = jnp.maximum(highest, block.max(axis=-1, keepdims=True))
    powers = [jnp.exp(block - highest) for block in blocks]
    total = powers[0].sum(axis=-1, keepdims=True)
    for power in powers[1:]:
        total = total + power.sum(axis=-1, keepdims=True)
    share = 1.0 / total
    return [power * share for power in powers]


def row_attention(x_ref, kv_ref, pattern_ref, row, out_ref, total_ref):
    total_ref[...] = jnp.zeros_like(total_ref)

    for b in range(2):
        start = b * HALF
        rows, window = pl.ds(start, HALF), pl.ds(start, 3 * HALF)
        shape = (2 * HALF, HALF)
        same = iota(shape, 1) <= lax.rem(iota(shape, 0), HALF)
        has_earlier = jnp.broadcast_to(row >= 1, shape)
        first, second = (
            pattern_ref[h, b, 1 - b] * jnp.minimum(row + b, 1)
            for h in range(2)
        )
        whole_open = jnp.where(iota(shape, 0) < HALF, first, second) > 0
        q = per_head(x_ref[0, rows, :]) * jnp.asarray(0.125, BF16)
        g = per_head(x_ref[1, rows, :])
        keys, values = kv_ref[0, window, :], kv_ref[1, window, :]
        scores, weight_grads = matmul_nt(q, keys), matmul_nt(g, values)

        def chosen(x, earlier_else):
            earlier, whole, this = (x[:, i * HALF : (i + 1) * HALF] for i in range(3))
            return jnp.where(same, this, earlier_else(earlier)), whole

        diag, whole = chosen(scores, lambda x: jnp.where(has_earlier, x, NEG))
        p_diag, p_whole = softmax([diag, jnp.where(whole_open, whole, NEG)])

        def spread(at_diag, at_whole):
            at_diag, at_whole = at_diag.astype(BF16), at_whole.astype(BF16)
            zero = jnp.zeros_like(at_diag)
            return jnp.concatenate(
                [jnp.where(same, zero, at_diag), at_whole, jnp.where(same, at_diag, zero)], axis=1
            )

        w = spread(p_diag, p_whole)
        attended = both_heads(matmul(w, values)).astype(BF16)
        out_ref[0, rows, :HALF] = attended
        wide = attended.astype(F32)
        dots = (g.astype(F32) * jnp.concatenate([wide, wide], axis=0)).sum(-1, keepdims=True)
        d_diag, d_whole = chosen(weight_grads, lambda x: x)
        e = spread(p_diag * (d_diag - dots), p_whole * (d_whole - dots))
        out_ref[1, rows, :HALF] = (both_heads(matmul(e, keys)) * 0.125).astype(BF16)
        total_ref[0, window, :] += matmul_tn(e, q)
        total_ref[1, window, :] += matmul_tn(w, g)


def column_attention(q, k, v, g, bias):
    q = per_head(q) * jnp.asarray(0.125, BF16)
    g = per_head(g)
    (p,) = softmax([matmul_nt(q, k) + bias])
    w = p.astype(BF16)
    attended = both_heads(matmul(w, v)).astype(BF16).astype(F32)
    dots = (g.astype(F32) * jnp.concatenate([attended, attended], axis=0)).sum(-1, keepdims=True)
    e = (p * (matmul_nt(g, v) - dots)).astype(BF16)
    return attended, both_heads(matmul(e, k)) * 0.125, matmul_tn(e, q), matmul_tn(w, g)


def column_bias(pattern_ref):
    shape = (2 * ROWS, ROWS)
    stacked, key = iota(shape, 0), iota(shape, 1)
    query = lax.rem(stacked, ROWS)
    which = query // 32 + jnp.where(stacked < ROWS, 0, 4)
    bits = jnp.zeros(shape, jnp.int32)
    for h in range(2):
        for b in range(4):
            code = sum(pattern_ref[h, b, j] * (1 << j) for j in range(4))
            bits = jnp.where(which == 4 * h + b, code, bits)
    allowed = (key <= query) & (((bits >> (key // 32)) & 1) > 0)
    return jnp.where(allowed, 0.0, NEG)


def reorder(source, target):
    order, size, row = {}, 1, iota((BLOCK, BLOCK), 1)
    for name in reversed(source):
        order[name] = lax.rem(row // size, source[name])
        size *= source[name]
    place = 0
    for name in target:
        place = place * source[name] + order[name]
    return jnp.where(place == iota((BLOCK, BLOCK), 0), 1.0, 0.0).astype(BF16)


def kernel(
    q_hbm, k_hbm, v_hbm, g_hbm, row_pattern_hbm, column_pattern_hbm,
    result,
    xc, xr, kv, back, backr, total, perm, bias,
    s1a, r1a, r1b, s2a, r2a, s2b, r2b, found, s3, r3,
    row_pattern, column_pattern, pattern_sem, in_sem, ring_sem, send_sem, recv_sem, back_send_sem, back_recv_sem,
):
    me = lax.axis_index("seq")
    y, zx = me // NZX, lax.rem(me, NZX)
    place_here = {"mp": lax.axis_index("mp"), "batch": lax.axis_index("batch")}
    after = {"seq": lax.rem(me + 1, ROWS), **place_here}
    before = {"seq": lax.rem(me + ROWS - 1, ROWS), **place_here}

    zx_places = [lax.rem(zx + i, NZX) for i in range(NZX)]
    y_places = [lax.rem(y + i, NY) for i in range(NY)]

    def device(seq):
        return {"seq": seq, **place_here}

    zx_peers = [(zx_places[i], device(y * NZX + zx_places[i])) for i in ZX_ORDER]
    y_peers = [(y_places[i], device(y_places[i] * NZX + zx)) for i in Y_ORDER]

    inputs = (q_hbm, k_hbm, v_hbm, g_hbm)

    this_row = pl.ds(CW, CW)
    row_places = (xr.at[0], kv.at[0, this_row], kv.at[1, this_row], xr.at[1])

    def loads_of(part, places):
        return [
            pltpu.make_async_copy(h.at[0, :, pl.ds(part * HALF, HALF)], place, in_sem.at[part, i])
            for i, (h, place) in enumerate(zip(inputs, places))
        ]

    column_loads = loads_of(1, [xc.at[i // 2, i % 2] for i in range(PIECES)])
    row_loads = loads_of(0, row_places)
    patterns = [
        pltpu.make_async_copy(row_pattern_hbm, row_pattern, pattern_sem.at[0]),
        pltpu.make_async_copy(column_pattern_hbm, column_pattern, pattern_sem.at[1]),
    ]
    for load in column_loads:
        load.start()

    barrier = pltpu.get_barrier_semaphore()

    def greet(peer):
        pl.semaphore_signal(barrier, inc=1, device_id=peer, device_id_type=MESH)

    for _, peer in zx_peers + y_peers:
        greet(peer)
    greet(after)
    greet(before)
    for load in row_loads + patterns:
        load.start()

    def exchange(step, source, landing, over_zx):
        place = (step, 0 if over_zx else 1)
        peers, mine = (zx_peers, zx) if over_zx else (y_peers, y)
        for other, peer in peers:
            pltpu.make_async_remote_copy(
                src_ref=source(other),
                dst_ref=landing(mine),
                send_sem=send_sem.at[place],
                recv_sem=recv_sem.at[place],
                device_id=peer,
                device_id_type=MESH,
            ).start()
        pltpu.make_async_copy(source(mine), landing(mine), recv_sem.at[place]).start()

    def send(step, source, dest, over_zx):
        exchange(step, lambda j: source.at[j], lambda j: dest.at[j], over_zx)

    def arrived(step, whole, over_zx):
        pltpu.make_async_copy(whole, whole, recv_sem.at[step, 0 if over_zx else 1]).wait()

    def sent(step, dest, over_zx):
        part = dest.at[pl.ds(0, dest.shape[0] - 1)]
        pltpu.make_async_copy(part, part, send_sem.at[step, 0 if over_zx else 1]).wait()

    def last_columns(j=None):
        rows = pl.ds(HALF, HALF) if j is None else pl.ds(pl.multiple_of(HALF + j * NZX, NZX), NZX)
        return (slice(None), slice(None), rows, slice(None))

    grid_rows = {"piece": 2, "y": NY, "zx": NZX}
    by_zx = ("zx", "piece", "y")
    perm[PACK] = reorder(grid_rows, by_zx)
    for load in column_loads:
        load.wait()
    for p in range(PAIRS):
        rows = xc[p, :, :HALF, :].reshape(BLOCK, HALF)
        packed = matmul(perm[PACK], rows).astype(BF16)
        s1a[:, p] = packed.reshape(NZX, 2 * NY, HALF)
    pl.semaphore_wait(barrier, (NZX - 1) + (NY - 1) + 2)

    send(0, s1a, r1a, True)
    exchange(0, lambda j: xc.at[last_columns(j)], lambda j: r1b.at[j], False)
    for load in row_loads:
        load.wait()
    forward = pltpu.make_async_remote_copy(
        src_ref=kv.at[:, this_row],
        dst_ref=kv.at[:, pl.ds(0, CW)],
        send_sem=ring_sem.at[0],
        recv_sem=ring_sem.at[1],
        device_id=after,
        device_id_type=MESH,
    )
    forward.start()

    for t, source, target in (
        (UNPACK, {"zx": NZX, "piece": 2, "y": NY}, ("piece", "y", "zx")),
        (ZX_TO_Y, {"zx": NZX, "piece": 2, "y": NY}, ("y", "piece", "zx")),
        (Y_TO_ZX, {"y": NY, "piece": 2, "zx": NZX}, ("zx", "piece", "y")),
        (SPREAD, {"piece": 2 * PIECES, "row": PART}, ("row", "piece")),
        (GATHER, {"row": PART, "piece": 2 * PIECES}, ("piece", "row")),
    ):
        perm[t] = reorder(source, target)
    for load in patterns:
        load.wait()
    bias[...] = column_bias(column_pattern)

    def swap(dest, source, t):
        for p in range(PAIRS):
            rows = matmul(perm[t], source[:, p].reshape(BLOCK, HALF)).astype(BF16)
            dest[:, p] = rows.reshape(dest.shape[:1] + dest.shape[2:])

    arrived(0, r1a, True)
    swap(s2a, r1a, ZX_TO_Y)
    send(1, s2a, r2a, False)
    arrived(0, r1b, False)
    swap(s2b, r1b, Y_TO_ZX)
    send(1, s2b, r2b, True)

    forward.wait()
    row_attention(xr, kv, row_pattern, me, result, total)
    back[...] = total[:, :CW, :].astype(BF16)
    backward = pltpu.make_async_remote_copy(
        src_ref=back,
        dst_ref=backr,
        send_sem=ring_sem.at[2],
        recv_sem=ring_sem.at[3],
        device_id=before,
        device_id_type=MESH,
    )
    backward.start()

    arrived(1, r2a, False)
    pieces = [r2a[:, i // 2, i % 2].reshape(ROWS, HALF) for i in range(PIECES)]
    for i, found_here in enumerate(column_attention(*pieces, bias[...])):
        found[0, i] = found_here.astype(BF16)
    arrived(1, r2b, True)
    pieces = []
    for p in range(PAIRS):
        rows = matmul(perm[UNPACK], r2b[:, p].reshape(BLOCK, HALF)).astype(BF16)
        pieces += [rows[:ROWS], rows[ROWS:]]
    for i, found_here in enumerate(column_attention(*pieces, bias[...])):
        found[1, i] = found_here.astype(BF16)

    for k in range(ROWS // PART):
        part = pl.ds(k * PART, PART)
        rows = found[:, :, part, :].reshape(BLOCK, HALF)
        s3[part] = matmul(perm[SPREAD], rows).astype(BF16).reshape(PART, 2 * PIECES, HALF)

    for i in ALL_ORDER:
        other = y_places[i // NZX] * NZX + zx_places[i % NZX]
        pltpu.make_async_remote_copy(
            src_ref=s3.at[other],
            dst_ref=r3.at[me],
            send_sem=back_send_sem,
            recv_sem=back_recv_sem,
            device_id=device(other),
            device_id_type=MESH,
        ).start()
    pltpu.make_async_copy(s3.at[me], r3.at[me], back_recv_sem).start()

    backward.wait()
    for i in range(2):
        result[2 + i, :, :HALF] = (total[i, CW:, :] + backr[i].astype(F32)).astype(BF16)

    pltpu.make_async_copy(r3, r3, back_recv_sem).wait()
    for k in range(ROWS // PART):
        part = pl.ds(k * PART, PART)
        rows = matmul(perm[GATHER], r3[part].reshape(BLOCK, HALF)).astype(BF16)
        for c in range(2):
            for i in range(PIECES):
                start = (c * PIECES + i) * PART
                place = pl.ds(c * HALF + k * PART, PART)
                result[i, place, HALF:] = rows[start : start + PART]

    for step, (over_zx, over_y) in enumerate(((r1a, r1b), (r2b, r2a))):
        sent(step, over_zx, True)
        sent(step, over_y, False)
    others = s3.at[pl.ds(0, ROWS - 1)]
    pltpu.make_async_copy(others, others, back_send_sem).wait()


def write_out(result, o0, o1, o2, o3, sem):
    copies = [
        pltpu.make_async_copy(result.at[i], o.at[0], sem.at[i])
        for i, o in enumerate((o0, o1, o2, o3))
    ]
    for copy in copies:
        copy.start()
    for copy in copies:
        copy.wait()


def per_device(queries, key_vectors, value_vectors, cotangent, row_pattern, column_pattern):
    by_zx = pltpu.VMEM((NZX, PAIRS, 2 * NY, HALF), BF16)
    by_y = pltpu.VMEM((NY, PAIRS, 2, NZX, HALF), BF16)
    direct = pltpu.VMEM((ROWS, 2 * PIECES, HALF), BF16)
    vmem = pl.BlockSpec(memory_space=pltpu.VMEM)
    hbm = pl.BlockSpec(memory_space=pltpu.HBM)
    halves = pltpu.VMEM((PAIRS, 2, CW, HALF), BF16)
    pair = pltpu.VMEM((2, CW, HALF), BF16)
    in_hbm = [
        pltpu.with_memory_space_constraint(x, pltpu.HBM)
        for x in (queries, key_vectors, value_vectors, cotangent, row_pattern, column_pattern)
    ]
    result = pl.pallas_call(
        kernel,
        out_shape=pltpu.VMEM((PIECES, CW, 2 * HALF), BF16),
        in_specs=[hbm] * 6,
        out_specs=vmem,
        scratch_shapes=[
            halves, pair,
            pltpu.VMEM((2, 2 * CW, HALF), BF16),
            pair, pair,
            pltpu.VMEM((2, 2 * CW, HALF), F32),
            pltpu.VMEM((6, BLOCK, BLOCK), BF16),
            pltpu.VMEM((2 * ROWS, ROWS), F32),
            by_zx, by_zx, by_y,
            by_y, by_y, by_zx, by_zx,
            pltpu.VMEM((2, PIECES, ROWS, HALF), BF16),
            direct, direct,
            pltpu.SMEM(row_pattern.shape, jnp.int32),
            pltpu.SMEM(column_pattern.shape, jnp.int32),
            pltpu.SemaphoreType.DMA((2,)),
            pltpu.SemaphoreType.DMA((2, PIECES)),
            pltpu.SemaphoreType.DMA((4,)),
            pltpu.SemaphoreType.DMA((2, 2)),
            pltpu.SemaphoreType.DMA((2, 2)),
            pltpu.SemaphoreType.DMA,
            pltpu.SemaphoreType.DMA,
        ],
        compiler_params=pltpu.CompilerParams(
            collective_id=0, has_side_effects=True, vmem_limit_bytes=40 * 1024 * 1024
        ),
        cost_estimate=pl.CostEstimate(
            flops=800_000_000, bytes_accessed=1_050_000, transcendentals=200_000
        ),
        name="grid_attention",
    )(*in_hbm)
    return pl.pallas_call(
        write_out,
        out_shape=[jax.ShapeDtypeStruct(queries.shape, BF16)] * 4,
        in_specs=[vmem],
        out_specs=[hbm] * 4,
        scratch_shapes=[pltpu.SemaphoreType.DMA((PIECES,))],
        cost_estimate=pl.CostEstimate(flops=0, bytes_accessed=1_050_000, transcendentals=0),
        compiler_params=pltpu.CompilerParams(vmem_limit_bytes=8 * 1024 * 1024),
        name="write_out",
    )(pltpu.with_memory_space_constraint(result, pltpu.VMEM))


def solution(mesh):
    rows = P(("batch", "seq"), None, "mp")
    heads = P("mp", None, None)
    return jax.shard_map(
        per_device,
        mesh=mesh,
        in_specs=(rows, rows, rows, rows, heads, heads),
        out_specs=(rows, rows, rows, rows),
        check_vma=False,
    )
```

```python
import jax
import jax.numpy as jnp
from jax import lax
from jax.experimental import pallas as pl
from jax.experimental.pallas import tpu as pltpu
from jax.sharding import PartitionSpec as P

MESH = pl.DeviceIdType.MESH
F32 = jnp.float32
BF16 = jnp.bfloat16
NEG = -1e30

NY = 8
NZX = 16
ROWS = NY * NZX
CW = 256
HALF = 128
DH = 64
PIECES = 4
PAIRS = PIECES // 2
BLOCK = 2 * ROWS
PART = 32
PACK, UNPACK, ZX_TO_Y, Y_TO_ZX, SPREAD, GATHER = range(6)


def hops(offset, size):
    return min(offset, size - offset)


def far_first(count, distance):
    return sorted(range(1, count), key=lambda i: (-distance(i), i * 37 % count))


Y_ORDER = far_first(NY, lambda i: hops(i, NY))
ZX_ORDER = far_first(NZX, lambda i: hops(i // 2, NZX // 2) + i % 2)
ALL_ORDER = far_first(ROWS, lambda i: hops(i // NZX, NY) + hops(i % NZX // 2, NZX // 2) + i % 2)


def iota(shape, axis):
    return lax.broadcasted_iota(jnp.int32, shape, axis)


def matmul(a, b):
    return lax.dot_general(a, b, (((1,), (0,)), ((), ())), preferred_element_type=F32)


def matmul_nt(a, b):
    return lax.dot_general(a, b, (((1,), (1,)), ((), ())), preferred_element_type=F32)


def matmul_tn(a, b):
    return lax.dot_general(a, b, (((0,), (0,)), ((), ())), preferred_element_type=F32)


def per_head(x):
    first = iota(x.shape, 1) < DH
    zero = jnp.zeros_like(x)
    return jnp.concatenate([jnp.where(first, x, zero), jnp.where(first, zero, x)], axis=0)


def both_heads(stacked):
    half = stacked.shape[0] // 2
    top, bottom = stacked[:half], stacked[half:]
    return jnp.where(iota(top.shape, 1) < DH, top, bottom)


def softmax(blocks):
    highest = blocks[0].max(axis=-1, keepdims=True)
    for block in blocks[1:]:
        highest = jnp.maximum(highest, block.max(axis=-1, keepdims=True))
    powers = [jnp.exp(block - highest) for block in blocks]
    total = powers[0].sum(axis=-1, keepdims=True)
    for power in powers[1:]:
        total = total + power.sum(axis=-1, keepdims=True)
    share = 1.0 / total
    return [power * share for power in powers]


def row_attention(x_ref, kv_ref, pattern_ref, row, out_ref, total_ref):
    total_ref[...] = jnp.zeros_like(total_ref)

    for b in range(2):
        start = b * HALF
        rows, window = pl.ds(start, HALF), pl.ds(start, 3 * HALF)
        shape = (2 * HALF, HALF)
        same = iota(shape, 1) <= lax.rem(iota(shape, 0), HALF)
        has_earlier = jnp.broadcast_to(row >= 1, shape)
        first, second = (
            pattern_ref[h, b, 1 - b] * jnp.minimum(row + b, 1)
            for h in range(2)
        )
        whole_open = jnp.where(iota(shape, 0) < HALF, first, second) > 0
        q = per_head(x_ref[0, rows, :]) * jnp.asarray(0.125, BF16)
        g = per_head(x_ref[1, rows, :])
        keys, values = kv_ref[0, window, :], kv_ref[1, window, :]
        scores, weight_grads = matmul_nt(q, keys), matmul_nt(g, values)

        def chosen(x, earlier_else):
            earlier, whole, this = (x[:, i * HALF : (i + 1) * HALF] for i in range(3))
            return jnp.where(same, this, earlier_else(earlier)), whole

        diag, whole = chosen(scores, lambda x: jnp.where(has_earlier, x, NEG))
        p_diag, p_whole = softmax([diag, jnp.where(whole_open, whole, NEG)])

        def spread(at_diag, at_whole):
            at_diag, at_whole = at_diag.astype(BF16), at_whole.astype(BF16)
            zero = jnp.zeros_like(at_diag)
            return jnp.concatenate(
                [jnp.where(same, zero, at_diag), at_whole, jnp.where(same, at_diag, zero)], axis=1
            )

        w = spread(p_diag, p_whole)
        attended = both_heads(matmul(w, values)).astype(BF16)
        out_ref[0, rows, :HALF] = attended
        wide = attended.astype(F32)
        dots = (g.astype(F32) * jnp.concatenate([wide, wide], axis=0)).sum(-1, keepdims=True)
        d_diag, d_whole = chosen(weight_grads, lambda x: x)
        e = spread(p_diag * (d_diag - dots), p_whole * (d_whole - dots))
        out_ref[1, rows, :HALF] = (both_heads(matmul(e, keys)) * 0.125).astype(BF16)
        total_ref[0, window, :] += matmul_tn(e, q)
        total_ref[1, window, :] += matmul_tn(w, g)


def column_attention(q, k, v, g, bias):
    q = per_head(q) * jnp.asarray(0.125, BF16)
    g = per_head(g)
    (p,) = softmax([matmul_nt(q, k) + bias])
    w = p.astype(BF16)
    attended = both_heads(matmul(w, v)).astype(BF16).astype(F32)
    dots = (g.astype(F32) * jnp.concatenate([attended, attended], axis=0)).sum(-1, keepdims=True)
    e = (p * (matmul_nt(g, v) - dots)).astype(BF16)
    return attended, both_heads(matmul(e, k)) * 0.125, matmul_tn(e, q), matmul_tn(w, g)


def column_bias(pattern_ref):
    shape = (2 * ROWS, ROWS)
    stacked, key = iota(shape, 0), iota(shape, 1)
    query = lax.rem(stacked, ROWS)
    which = query // 32 + jnp.where(stacked < ROWS, 0, 4)
    bits = jnp.zeros(shape, jnp.int32)
    for h in range(2):
        for b in range(4):
            code = sum(pattern_ref[h, b, j] * (1 << j) for j in range(4))
            bits = jnp.where(which == 4 * h + b, code, bits)
    allowed = (key <= query) & (((bits >> (key // 32)) & 1) > 0)
    return jnp.where(allowed, 0.0, NEG)


def reorder(source, target):
    order, size, row = {}, 1, iota((BLOCK, BLOCK), 1)
    for name in reversed(source):
        order[name] = lax.rem(row // size, source[name])
        size *= source[name]
    place = 0
    for name in target:
        place = place * source[name] + order[name]
    return jnp.where(place == iota((BLOCK, BLOCK), 0), 1.0, 0.0).astype(BF16)


def kernel(
    q_hbm, k_hbm, v_hbm, g_hbm, row_pattern_hbm, column_pattern_hbm,
    result,
    xc, xr, kv, back, backr, total, perm, bias,
    s1a, r1a, r1b, s2a, r2a, s2b, r2b, found, s3, r3,
    row_pattern, column_pattern, pattern_sem, in_sem, ring_sem, send_sem, recv_sem, back_send_sem, back_recv_sem,
):
    me = lax.axis_index("seq")
    y, zx = me // NZX, lax.rem(me, NZX)
    place_here = {"mp": lax.axis_index("mp"), "batch": lax.axis_index("batch")}
    after = {"seq": lax.rem(me + 1, ROWS), **place_here}
    before = {"seq": lax.rem(me + ROWS - 1, ROWS), **place_here}

    turn = 1 - 2 * lax.axis_index("batch")
    zx_places = [lax.rem(zx + NZX + turn * i, NZX) for i in range(NZX)]
    y_places = [lax.rem(y + NY + turn * i, NY) for i in range(NY)]

    def device(seq):
        return {"seq": seq, **place_here}

    zx_peers = [(zx_places[i], device(y * NZX + zx_places[i])) for i in ZX_ORDER]
    y_peers = [(y_places[i], device(y_places[i] * NZX + zx)) for i in Y_ORDER]

    inputs = (q_hbm, k_hbm, v_hbm, g_hbm)

    this_row = pl.ds(CW, CW)
    row_places = (xr.at[0], kv.at[0, this_row], kv.at[1, this_row], xr.at[1])

    row_loads = [
        pltpu.make_async_copy(h.at[0, :, pl.ds(0, HALF)], place, in_sem.at[0, i])
        for i, (h, place) in enumerate(zip(inputs, row_places))
    ]
    first_loads, last_loads = (
        [
            pltpu.make_async_copy(
                h.at[0, pl.ds(start, HALF), pl.ds(HALF, HALF)],
                xc.at[i // 2, i % 2, pl.ds(start, HALF), :],
                in_sem.at[1 + start // HALF, i],
            )
            for i, h in enumerate(inputs)
        ]
        for start in (0, HALF)
    )
    patterns = [
        pltpu.make_async_copy(row_pattern_hbm, row_pattern, pattern_sem.at[0]),
        pltpu.make_async_copy(column_pattern_hbm, column_pattern, pattern_sem.at[1]),
    ]
    for load in first_loads + last_loads:
        load.start()

    barrier = pltpu.get_barrier_semaphore()

    def greet(peer):
        pl.semaphore_signal(barrier, inc=1, device_id=peer, device_id_type=MESH)

    for _, peer in zx_peers + y_peers:
        greet(peer)
    greet(after)
    greet(before)
    for load in row_loads + patterns:
        load.start()

    def exchange(step, source, landing, over_zx):
        place = (step, 0 if over_zx else 1)
        peers, mine = (zx_peers, zx) if over_zx else (y_peers, y)
        for other, peer in peers:
            pltpu.make_async_remote_copy(
                src_ref=source(other),
                dst_ref=landing(mine),
                send_sem=send_sem.at[place],
                recv_sem=recv_sem.at[place],
                device_id=peer,
                device_id_type=MESH,
            ).start()
        pltpu.make_async_copy(source(mine), landing(mine), recv_sem.at[place]).start()

    def send(step, source, dest, over_zx):
        exchange(step, lambda j: source.at[j], lambda j: dest.at[j], over_zx)

    def arrived(step, whole, over_zx):
        pltpu.make_async_copy(whole, whole, recv_sem.at[step, 0 if over_zx else 1]).wait()

    def sent(step, dest, over_zx):
        part = dest.at[pl.ds(0, dest.shape[0] - 1)]
        pltpu.make_async_copy(part, part, send_sem.at[step, 0 if over_zx else 1]).wait()

    def last_columns(j=None):
        rows = pl.ds(HALF, HALF) if j is None else pl.ds(pl.multiple_of(HALF + j * NZX, NZX), NZX)
        return (slice(None), slice(None), rows, slice(None))

    grid_rows = {"piece": 2, "y": NY, "zx": NZX}
    by_zx = ("zx", "piece", "y")
    perm[PACK] = reorder(grid_rows, by_zx)
    for load in first_loads:
        load.wait()
    for p in range(PAIRS):
        rows = xc[p, :, :HALF, :].reshape(BLOCK, HALF)
        packed = matmul(perm[PACK], rows).astype(BF16)
        s1a[:, p] = packed.reshape(NZX, 2 * NY, HALF)
    pl.semaphore_wait(barrier, (NZX - 1) + (NY - 1) + 2)

    send(0, s1a, r1a, True)
    for load in last_loads:
        load.wait()
    exchange(0, lambda j: xc.at[last_columns(j)], lambda j: r1b.at[j], False)
    for load in row_loads:
        load.wait()
    forward = pltpu.make_async_remote_copy(
        src_ref=kv.at[:, this_row],
        dst_ref=kv.at[:, pl.ds(0, CW)],
        send_sem=ring_sem.at[0],
        recv_sem=ring_sem.at[1],
        device_id=after,
        device_id_type=MESH,
    )
    forward.start()

    for t, source, target in (
        (UNPACK, {"zx": NZX, "piece": 2, "y": NY}, ("piece", "y", "zx")),
        (ZX_TO_Y, {"zx": NZX, "piece": 2, "y": NY}, ("y", "piece", "zx")),
        (Y_TO_ZX, {"y": NY, "piece": 2, "zx": NZX}, ("zx", "piece", "y")),
        (SPREAD, {"piece": 2 * PIECES, "row": PART}, ("row", "piece")),
        (GATHER, {"row": PART, "piece": 2 * PIECES}, ("piece", "row")),
    ):
        perm[t] = reorder(source, target)
    for load in patterns:
        load.wait()
    bias[...] = column_bias(column_pattern)

    def swap(dest, source, t):
        for p in range(PAIRS):
            rows = matmul(perm[t], source[:, p].reshape(BLOCK, HALF)).astype(BF16)
            dest[:, p] = rows.reshape(dest.shape[:1] + dest.shape[2:])

    arrived(0, r1a, True)
    swap(s2a, r1a, ZX_TO_Y)
    send(1, s2a, r2a, False)
    arrived(0, r1b, False)
    swap(s2b, r1b, Y_TO_ZX)
    send(1, s2b, r2b, True)

    forward.wait()
    row_attention(xr, kv, row_pattern, me, result, total)
    back[...] = total[:, :CW, :].astype(BF16)
    backward = pltpu.make_async_remote_copy(
        src_ref=back,
        dst_ref=backr,
        send_sem=ring_sem.at[2],
        recv_sem=ring_sem.at[3],
        device_id=before,
        device_id_type=MESH,
    )
    backward.start()

    arrived(1, r2a, False)
    pieces = [r2a[:, i // 2, i % 2].reshape(ROWS, HALF) for i in range(PIECES)]
    for i, found_here in enumerate(column_attention(*pieces, bias[...])):
        found[0, i] = found_here.astype(BF16)
    arrived(1, r2b, True)
    pieces = []
    for p in range(PAIRS):
        rows = matmul(perm[UNPACK], r2b[:, p].reshape(BLOCK, HALF)).astype(BF16)
        pieces += [rows[:ROWS], rows[ROWS:]]
    for i, found_here in enumerate(column_attention(*pieces, bias[...])):
        found[1, i] = found_here.astype(BF16)

    for k in range(ROWS // PART):
        part = pl.ds(k * PART, PART)
        rows = found[:, :, part, :].reshape(BLOCK, HALF)
        s3[part] = matmul(perm[SPREAD], rows).astype(BF16).reshape(PART, 2 * PIECES, HALF)

    for i in ALL_ORDER:
        other = y_places[i // NZX] * NZX + zx_places[i % NZX]
        pltpu.make_async_remote_copy(
            src_ref=s3.at[other],
            dst_ref=r3.at[me],
            send_sem=back_send_sem,
            recv_sem=back_recv_sem,
            device_id=device(other),
            device_id_type=MESH,
        ).start()
    pltpu.make_async_copy(s3.at[me], r3.at[me], back_recv_sem).start()

    backward.wait()
    for i in range(2):
        result[2 + i, :, :HALF] = (total[i, CW:, :] + backr[i].astype(F32)).astype(BF16)

    pltpu.make_async_copy(r3, r3, back_recv_sem).wait()
    for k in range(ROWS // PART):
        part = pl.ds(k * PART, PART)
        rows = matmul(perm[GATHER], r3[part].reshape(BLOCK, HALF)).astype(BF16)
        for c in range(2):
            for i in range(PIECES):
                start = (c * PIECES + i) * PART
                place = pl.ds(c * HALF + k * PART, PART)
                result[i, place, HALF:] = rows[start : start + PART]

    for step, (over_zx, over_y) in enumerate(((r1a, r1b), (r2b, r2a))):
        sent(step, over_zx, True)
        sent(step, over_y, False)
    others = s3.at[pl.ds(0, ROWS - 1)]
    pltpu.make_async_copy(others, others, back_send_sem).wait()


def write_out(result, o0, o1, o2, o3, sem):
    copies = [
        pltpu.make_async_copy(result.at[i], o.at[0], sem.at[i])
        for i, o in enumerate((o0, o1, o2, o3))
    ]
    for copy in copies:
        copy.start()
    for copy in copies:
        copy.wait()


def per_device(queries, key_vectors, value_vectors, cotangent, row_pattern, column_pattern):
    by_zx = pltpu.VMEM((NZX, PAIRS, 2 * NY, HALF), BF16)
    by_y = pltpu.VMEM((NY, PAIRS, 2, NZX, HALF), BF16)
    direct = pltpu.VMEM((ROWS, 2 * PIECES, HALF), BF16)
    vmem = pl.BlockSpec(memory_space=pltpu.VMEM)
    hbm = pl.BlockSpec(memory_space=pltpu.HBM)
    halves = pltpu.VMEM((PAIRS, 2, CW, HALF), BF16)
    pair = pltpu.VMEM((2, CW, HALF), BF16)
    in_hbm = [
        pltpu.with_memory_space_constraint(x, pltpu.HBM)
        for x in (queries, key_vectors, value_vectors, cotangent, row_pattern, column_pattern)
    ]
    result = pl.pallas_call(
        kernel,
        out_shape=pltpu.VMEM((PIECES, CW, 2 * HALF), BF16),
        in_specs=[hbm] * 6,
        out_specs=vmem,
        scratch_shapes=[
            halves, pair,
            pltpu.VMEM((2, 2 * CW, HALF), BF16),
            pair, pair,
            pltpu.VMEM((2, 2 * CW, HALF), F32),
            pltpu.VMEM((6, BLOCK, BLOCK), BF16),
            pltpu.VMEM((2 * ROWS, ROWS), F32),
            by_zx, by_zx, by_y,
            by_y, by_y, by_zx, by_zx,
            pltpu.VMEM((2, PIECES, ROWS, HALF), BF16),
            direct, direct,
            pltpu.SMEM(row_pattern.shape, jnp.int32),
            pltpu.SMEM(column_pattern.shape, jnp.int32),
            pltpu.SemaphoreType.DMA((2,)),
            pltpu.SemaphoreType.DMA((3, PIECES)),
            pltpu.SemaphoreType.DMA((4,)),
            pltpu.SemaphoreType.DMA((2, 2)),
            pltpu.SemaphoreType.DMA((2, 2)),
            pltpu.SemaphoreType.DMA,
            pltpu.SemaphoreType.DMA,
        ],
        compiler_params=pltpu.CompilerParams(
            collective_id=0, has_side_effects=True, vmem_limit_bytes=40 * 1024 * 1024
        ),
        cost_estimate=pl.CostEstimate(
            flops=800_000_000, bytes_accessed=1_050_000, transcendentals=200_000
        ),
        name="grid_attention",
    )(*in_hbm)
    return pl.pallas_call(
        write_out,
        out_shape=[jax.ShapeDtypeStruct(queries.shape, BF16)] * 4,
        in_specs=[vmem],
        out_specs=[hbm] * 4,
        scratch_shapes=[pltpu.SemaphoreType.DMA((PIECES,))],
        cost_estimate=pl.CostEstimate(flops=0, bytes_accessed=1_050_000, transcendentals=0),
        compiler_params=pltpu.CompilerParams(vmem_limit_bytes=8 * 1024 * 1024),
        name="write_out",
    )(pltpu.with_memory_space_constraint(result, pltpu.VMEM))


def solution(mesh):
    rows = P(("batch", "seq"), None, "mp")
    heads = P("mp", None, None)
    return jax.shard_map(
        per_device,
        mesh=mesh,
        in_specs=(rows, rows, rows, rows, heads, heads),
        out_specs=(rows, rows, rows, rows),
        check_vma=False,
    )
```

```python
import jax
import jax.numpy as jnp
from jax import lax
from jax.experimental import pallas as pl
from jax.experimental.pallas import tpu as pltpu
from jax.sharding import PartitionSpec as P

MESH = pl.DeviceIdType.MESH
F32 = jnp.float32
BF16 = jnp.bfloat16
NEG = -1e30

NY = 8
NZX = 16
ROWS = NY * NZX
CW = 256
HALF = 128
DH = 64
PIECES = 4
PAIRS = PIECES // 2
BLOCK = 2 * ROWS
PART = 32
PACK, UNPACK, ZX_TO_Y, Y_TO_ZX, SPREAD, GATHER = range(6)


def hops(offset, size):
    return min(offset, size - offset)


def far_first(count, distance):
    return sorted(range(1, count), key=lambda i: (-distance(i), i * 37 % count))


Y_ORDER = far_first(NY, lambda i: hops(i, NY))
ZX_ORDER = far_first(NZX, lambda i: hops(i // 2, NZX // 2) + i % 2)
ALL_ORDER = far_first(ROWS, lambda i: hops(i // NZX, NY) + hops(i % NZX // 2, NZX // 2) + i % 2)


def iota(shape, axis):
    return lax.broadcasted_iota(jnp.int32, shape, axis)


def matmul(a, b):
    return lax.dot_general(a, b, (((1,), (0,)), ((), ())), preferred_element_type=F32)


def matmul_nt(a, b):
    return lax.dot_general(a, b, (((1,), (1,)), ((), ())), preferred_element_type=F32)


def per_head(x):
    first = iota(x.shape, 1) < DH
    zero = jnp.zeros_like(x)
    return jnp.concatenate([jnp.where(first, x, zero), jnp.where(first, zero, x)], axis=0)


def both_heads(wide):
    first = iota((HALF, HALF), 0) < DH
    return jnp.where(first, wide[:, :HALF], wide[:, HALF:])


def head_sums(x):
    return jnp.concatenate(
        [x[:DH].sum(0, keepdims=True), x[DH:].sum(0, keepdims=True)], axis=1
    )


def softmax(blocks):
    highest = blocks[0].max(axis=0, keepdims=True)
    for block in blocks[1:]:
        highest = jnp.maximum(highest, block.max(axis=0, keepdims=True))
    powers = [jnp.exp(block - highest) for block in blocks]
    total = powers[0].sum(axis=0, keepdims=True)
    for power in powers[1:]:
        total = total + power.sum(axis=0, keepdims=True)
    share = 1.0 / total
    return [power * share for power in powers]


def row_attention(x_ref, kv_ref, pattern_ref, row, out_ref, total_ref):
    total_ref[...] = jnp.zeros_like(total_ref)
    shape = (HALF, 2 * HALF)
    same = iota(shape, 0) <= lax.rem(iota(shape, 1), HALF)
    has_earlier = jnp.broadcast_to(row >= 1, shape)
    keys_t, values_t = kv_ref[0].T, kv_ref[1].T
    for b in range(2):
        start = b * HALF
        rows, window = pl.ds(start, HALF), pl.ds(start, 3 * HALF)
        first, second = (pattern_ref[h, b, 1 - b] * jnp.minimum(row + b, 1) for h in range(2))
        whole_open = jnp.where(iota(shape, 1) < HALF, first, second) > 0
        q = per_head(x_ref[0, rows, :]) * jnp.asarray(0.125, BF16)
        g = per_head(x_ref[1, rows, :])
        keys, values = kv_ref[0, window, :], kv_ref[1, window, :]
        scores, weight_grads = matmul_nt(keys, q), matmul_nt(values, g)

        def chosen(x, earlier_else):
            earlier, whole, this = (x[i * HALF : (i + 1) * HALF] for i in range(3))
            return jnp.where(same, this, earlier_else(earlier)), whole

        diag, whole = chosen(scores, lambda x: jnp.where(has_earlier, x, NEG))
        p_diag, p_whole = softmax([diag, jnp.where(whole_open, whole, NEG)])

        def spread(at_diag, at_whole):
            at_diag, at_whole = at_diag.astype(BF16), at_whole.astype(BF16)
            zero = jnp.zeros_like(at_diag)
            return jnp.concatenate(
                [jnp.where(same, zero, at_diag), at_whole, jnp.where(same, at_diag, zero)], axis=0
            )

        w = spread(p_diag, p_whole)
        attended = both_heads(matmul(values_t[:, start : start + 3 * HALF], w)).astype(BF16)
        out_ref[0, rows, :HALF] = attended.T
        dots = head_sums(x_ref[1, rows, :].T.astype(F32) * attended.astype(F32))
        d_diag, d_whole = chosen(weight_grads, lambda x: x)
        e = spread(p_diag * (d_diag - dots), p_whole * (d_whole - dots))
        grad = both_heads(matmul(keys_t[:, start : start + 3 * HALF], e)) * 0.125
        out_ref[1, rows, :HALF] = grad.astype(BF16).T
        total_ref[0, window, :] += matmul(e, q)
        total_ref[1, window, :] += matmul(w, g)


def column_attention(q, k, v, g, bias):
    g_t = g.T.astype(F32)
    q = per_head(q) * jnp.asarray(0.125, BF16)
    g = per_head(g)
    (p,) = softmax([matmul_nt(k, q) + bias])
    w = p.astype(BF16)
    attended = both_heads(matmul(v.T, w)).astype(BF16)
    dots = head_sums(g_t * attended.astype(F32))
    e = (p * (matmul_nt(v, g) - dots)).astype(BF16)
    grad = (both_heads(matmul(k.T, e)) * 0.125).astype(BF16)
    return attended.T, grad.T, matmul(e, q).astype(BF16), matmul(w, g).astype(BF16)


def column_bias(pattern_ref):
    shape = (ROWS, 2 * ROWS)
    key, stacked = iota(shape, 0), iota(shape, 1)
    query = lax.rem(stacked, ROWS)
    which = query // 32 + jnp.where(stacked < ROWS, 0, 4)
    bits = jnp.zeros(shape, jnp.int32)
    for h in range(2):
        for b in range(4):
            code = sum(pattern_ref[h, b, j] * (1 << j) for j in range(4))
            bits = jnp.where(which == 4 * h + b, code, bits)
    allowed = (key <= query) & (((bits >> (key // 32)) & 1) > 0)
    return jnp.where(allowed, 0.0, NEG)


def reorder(source, target):
    order, size, row = {}, 1, iota((BLOCK, BLOCK), 1)
    for name in reversed(source):
        order[name] = lax.rem(row // size, source[name])
        size *= source[name]
    place = 0
    for name in target:
        place = place * source[name] + order[name]
    return jnp.where(place == iota((BLOCK, BLOCK), 0), 1.0, 0.0).astype(BF16)


def kernel(
    q_hbm, k_hbm, v_hbm, g_hbm, row_pattern_hbm, column_pattern_hbm,
    result,
    xc, xr, kv, back, backr, total, perm, bias,
    s1a, r1a, r1b, s2a, r2a, s2b, r2b, found, s3, r3,
    row_pattern, column_pattern, pattern_sem, in_sem, ring_sem, send_sem, recv_sem, back_send_sem, back_recv_sem,
):
    me = lax.axis_index("seq")
    y, zx = me // NZX, lax.rem(me, NZX)
    place_here = {"mp": lax.axis_index("mp"), "batch": lax.axis_index("batch")}
    after = {"seq": lax.rem(me + 1, ROWS), **place_here}
    before = {"seq": lax.rem(me + ROWS - 1, ROWS), **place_here}

    zx_places = [lax.rem(zx + i, NZX) for i in range(NZX)]
    y_places = [lax.rem(y + i, NY) for i in range(NY)]

    def device(seq):
        return {"seq": seq, **place_here}

    zx_peers = [(zx_places[i], device(y * NZX + zx_places[i])) for i in ZX_ORDER]
    y_peers = [(y_places[i], device(y_places[i] * NZX + zx)) for i in Y_ORDER]

    inputs = (q_hbm, k_hbm, v_hbm, g_hbm)

    this_row = pl.ds(CW, CW)
    row_places = (xr.at[0], kv.at[0, this_row], kv.at[1, this_row], xr.at[1])

    def loads_of(part, places):
        return [
            pltpu.make_async_copy(h.at[0, :, pl.ds(part * HALF, HALF)], place, in_sem.at[part, i])
            for i, (h, place) in enumerate(zip(inputs, places))
        ]

    column_loads = loads_of(1, [xc.at[i // 2, i % 2] for i in range(PIECES)])
    row_loads = loads_of(0, row_places)
    patterns = [
        pltpu.make_async_copy(row_pattern_hbm, row_pattern, pattern_sem.at[0]),
        pltpu.make_async_copy(column_pattern_hbm, column_pattern, pattern_sem.at[1]),
    ]
    for load in column_loads:
        load.start()

    barrier = pltpu.get_barrier_semaphore()

    def greet(peer):
        pl.semaphore_signal(barrier, inc=1, device_id=peer, device_id_type=MESH)

    for _, peer in zx_peers + y_peers:
        greet(peer)
    greet(after)
    greet(before)
    for load in row_loads + patterns:
        load.start()

    def exchange(step, source, landing, over_zx):
        place = (step, 0 if over_zx else 1)
        peers, mine = (zx_peers, zx) if over_zx else (y_peers, y)
        for other, peer in peers:
            pltpu.make_async_remote_copy(
                src_ref=source(other),
                dst_ref=landing(mine),
                send_sem=send_sem.at[place],
                recv_sem=recv_sem.at[place],
                device_id=peer,
                device_id_type=MESH,
            ).start()
        pltpu.make_async_copy(source(mine), landing(mine), recv_sem.at[place]).start()

    def send(step, source, dest, over_zx):
        exchange(step, lambda j: source.at[j], lambda j: dest.at[j], over_zx)

    def arrived(step, whole, over_zx):
        pltpu.make_async_copy(whole, whole, recv_sem.at[step, 0 if over_zx else 1]).wait()

    def sent(step, dest, over_zx):
        part = dest.at[pl.ds(0, dest.shape[0] - 1)]
        pltpu.make_async_copy(part, part, send_sem.at[step, 0 if over_zx else 1]).wait()

    def last_columns(j=None):
        rows = pl.ds(HALF, HALF) if j is None else pl.ds(pl.multiple_of(HALF + j * NZX, NZX), NZX)
        return (slice(None), slice(None), rows, slice(None))

    grid_rows = {"piece": 2, "y": NY, "zx": NZX}
    by_zx = ("zx", "piece", "y")
    perm[PACK] = reorder(grid_rows, by_zx)
    for load in column_loads:
        load.wait()
    for p in range(PAIRS):
        rows = xc[p, :, :HALF, :].reshape(BLOCK, HALF)
        packed = matmul(perm[PACK], rows).astype(BF16)
        s1a[:, p] = packed.reshape(NZX, 2 * NY, HALF)
    pl.semaphore_wait(barrier, (NZX - 1) + (NY - 1) + 2)

    send(0, s1a, r1a, True)
    exchange(0, lambda j: xc.at[last_columns(j)], lambda j: r1b.at[j], False)
    for load in row_loads:
        load.wait()
    forward = pltpu.make_async_remote_copy(
        src_ref=kv.at[:, this_row],
        dst_ref=kv.at[:, pl.ds(0, CW)],
        send_sem=ring_sem.at[0],
        recv_sem=ring_sem.at[1],
        device_id=after,
        device_id_type=MESH,
    )
    forward.start()

    for t, source, target in (
        (UNPACK, {"zx": NZX, "piece": 2, "y": NY}, ("piece", "y", "zx")),
        (ZX_TO_Y, {"zx": NZX, "piece": 2, "y": NY}, ("y", "piece", "zx")),
        (Y_TO_ZX, {"y": NY, "piece": 2, "zx": NZX}, ("zx", "piece", "y")),
        (SPREAD, {"piece": 2 * PIECES, "row": PART}, ("row", "piece")),
        (GATHER, {"row": PART, "piece": 2 * PIECES}, ("piece", "row")),
    ):
        perm[t] = reorder(source, target)
    for load in patterns:
        load.wait()
    bias[...] = column_bias(column_pattern)

    def swap(dest, source, t):
        for p in range(PAIRS):
            rows = matmul(perm[t], source[:, p].reshape(BLOCK, HALF)).astype(BF16)
            dest[:, p] = rows.reshape(dest.shape[:1] + dest.shape[2:])

    arrived(0, r1a, True)
    swap(s2a, r1a, ZX_TO_Y)
    send(1, s2a, r2a, False)
    arrived(0, r1b, False)
    swap(s2b, r1b, Y_TO_ZX)
    send(1, s2b, r2b, True)

    forward.wait()
    row_attention(xr, kv, row_pattern, me, result, total)
    back[...] = total[:, :CW, :].astype(BF16)
    backward = pltpu.make_async_remote_copy(
        src_ref=back,
        dst_ref=backr,
        send_sem=ring_sem.at[2],
        recv_sem=ring_sem.at[3],
        device_id=before,
        device_id_type=MESH,
    )
    backward.start()

    arrived(1, r2a, False)
    pieces = [r2a[:, i // 2, i % 2].reshape(ROWS, HALF) for i in range(PIECES)]
    for i, found_here in enumerate(column_attention(*pieces, bias[...])):
        found[0, i] = found_here
    arrived(1, r2b, True)
    pieces = []
    for p in range(PAIRS):
        rows = matmul(perm[UNPACK], r2b[:, p].reshape(BLOCK, HALF)).astype(BF16)
        pieces += [rows[:ROWS], rows[ROWS:]]
    for i, found_here in enumerate(column_attention(*pieces, bias[...])):
        found[1, i] = found_here

    for k in range(ROWS // PART):
        part = pl.ds(k * PART, PART)
        rows = found[:, :, part, :].reshape(BLOCK, HALF)
        s3[part] = matmul(perm[SPREAD], rows).astype(BF16).reshape(PART, 2 * PIECES, HALF)

    for i in ALL_ORDER:
        other = y_places[i // NZX] * NZX + zx_places[i % NZX]
        pltpu.make_async_remote_copy(
            src_ref=s3.at[other],
            dst_ref=r3.at[me],
            send_sem=back_send_sem,
            recv_sem=back_recv_sem,
            device_id=device(other),
            device_id_type=MESH,
        ).start()
    pltpu.make_async_copy(s3.at[me], r3.at[me], back_recv_sem).start()

    backward.wait()
    for i in range(2):
        result[2 + i, :, :HALF] = (total[i, CW:, :] + backr[i].astype(F32)).astype(BF16)

    pltpu.make_async_copy(r3, r3, back_recv_sem).wait()
    for k in range(ROWS // PART):
        part = pl.ds(k * PART, PART)
        rows = matmul(perm[GATHER], r3[part].reshape(BLOCK, HALF)).astype(BF16)
        for c in range(2):
            for i in range(PIECES):
                start = (c * PIECES + i) * PART
                place = pl.ds(c * HALF + k * PART, PART)
                result[i, place, HALF:] = rows[start : start + PART]

    for step, (over_zx, over_y) in enumerate(((r1a, r1b), (r2b, r2a))):
        sent(step, over_zx, True)
        sent(step, over_y, False)
    others = s3.at[pl.ds(0, ROWS - 1)]
    pltpu.make_async_copy(others, others, back_send_sem).wait()


def write_out(result, o0, o1, o2, o3, sem):
    copies = [
        pltpu.make_async_copy(result.at[i], o.at[0], sem.at[i])
        for i, o in enumerate((o0, o1, o2, o3))
    ]
    for copy in copies:
        copy.start()
    for copy in copies:
        copy.wait()


def per_device(queries, key_vectors, value_vectors, cotangent, row_pattern, column_pattern):
    by_zx = pltpu.VMEM((NZX, PAIRS, 2 * NY, HALF), BF16)
    by_y = pltpu.VMEM((NY, PAIRS, 2, NZX, HALF), BF16)
    direct = pltpu.VMEM((ROWS, 2 * PIECES, HALF), BF16)
    vmem = pl.BlockSpec(memory_space=pltpu.VMEM)
    hbm = pl.BlockSpec(memory_space=pltpu.HBM)
    halves = pltpu.VMEM((PAIRS, 2, CW, HALF), BF16)
    pair = pltpu.VMEM((2, CW, HALF), BF16)
    in_hbm = [
        pltpu.with_memory_space_constraint(x, pltpu.HBM)
        for x in (queries, key_vectors, value_vectors, cotangent, row_pattern, column_pattern)
    ]
    result = pl.pallas_call(
        kernel,
        out_shape=pltpu.VMEM((PIECES, CW, 2 * HALF), BF16),
        in_specs=[hbm] * 6,
        out_specs=vmem,
        scratch_shapes=[
            halves, pair,
            pltpu.VMEM((2, 2 * CW, HALF), BF16),
            pair, pair,
            pltpu.VMEM((2, 2 * CW, HALF), F32),
            pltpu.VMEM((6, BLOCK, BLOCK), BF16),
            pltpu.VMEM((ROWS, 2 * ROWS), F32),
            by_zx, by_zx, by_y,
            by_y, by_y, by_zx, by_zx,
            pltpu.VMEM((2, PIECES, ROWS, HALF), BF16),
            direct, direct,
            pltpu.SMEM(row_pattern.shape, jnp.int32),
            pltpu.SMEM(column_pattern.shape, jnp.int32),
            pltpu.SemaphoreType.DMA((2,)),
            pltpu.SemaphoreType.DMA((2, PIECES)),
            pltpu.SemaphoreType.DMA((4,)),
            pltpu.SemaphoreType.DMA((2, 2)),
            pltpu.SemaphoreType.DMA((2, 2)),
            pltpu.SemaphoreType.DMA,
            pltpu.SemaphoreType.DMA,
        ],
        compiler_params=pltpu.CompilerParams(
            collective_id=0, has_side_effects=True, vmem_limit_bytes=40 * 1024 * 1024
        ),
        cost_estimate=pl.CostEstimate(
            flops=800_000_000, bytes_accessed=1_050_000, transcendentals=200_000
        ),
        name="grid_attention",
    )(*in_hbm)
    return pl.pallas_call(
        write_out,
        out_shape=[jax.ShapeDtypeStruct(queries.shape, BF16)] * 4,
        in_specs=[vmem],
        out_specs=[hbm] * 4,
        scratch_shapes=[pltpu.SemaphoreType.DMA((PIECES,))],
        cost_estimate=pl.CostEstimate(flops=0, bytes_accessed=1_050_000, transcendentals=0),
        compiler_params=pltpu.CompilerParams(vmem_limit_bytes=8 * 1024 * 1024),
        name="write_out",
    )(pltpu.with_memory_space_constraint(result, pltpu.VMEM))


def solution(mesh):
    rows = P(("batch", "seq"), None, "mp")
    heads = P("mp", None, None)
    return jax.shard_map(
        per_device,
        mesh=mesh,
        in_specs=(rows, rows, rows, rows, heads, heads),
        out_specs=(rows, rows, rows, rows),
        check_vma=False,
    )
```

```python
import jax
import jax.numpy as jnp
from jax import lax
from jax.experimental import pallas as pl
from jax.experimental.pallas import tpu as pltpu
from jax.sharding import PartitionSpec as P

MESH = pl.DeviceIdType.MESH
F32 = jnp.float32
BF16 = jnp.bfloat16
NEG = -1e30

NY = 8
NZX = 16
ROWS = NY * NZX
CW = 256
HALF = 128
DH = 64
PIECES = 4
PAIRS = PIECES // 2
BLOCK = 2 * ROWS
PART = 32
PACK, UNPACK, ZX_TO_Y, Y_TO_ZX, SPREAD, GATHER = range(6)


def hops(offset, size):
    return min(offset, size - offset)


def far_first(count, distance):
    return sorted(range(1, count), key=lambda i: (-distance(i), i * 37 % count))


Y_ORDER = far_first(NY, lambda i: hops(i, NY))
ZX_ORDER = far_first(NZX, lambda i: hops(i // 2, NZX // 2) + i % 2)
ALL_ORDER = far_first(ROWS, lambda i: hops(i // NZX, NY) + hops(i % NZX // 2, NZX // 2) + i % 2)


def iota(shape, axis):
    return lax.broadcasted_iota(jnp.int32, shape, axis)


def matmul(a, b):
    return lax.dot_general(a, b, (((1,), (0,)), ((), ())), preferred_element_type=F32)


def matmul_nt(a, b):
    return lax.dot_general(a, b, (((1,), (1,)), ((), ())), preferred_element_type=F32)


def per_head(x):
    first = iota(x.shape, 1) < DH
    zero = jnp.zeros_like(x)
    return jnp.concatenate([jnp.where(first, x, zero), jnp.where(first, zero, x)], axis=0)


def both_heads(wide):
    first = iota((HALF, HALF), 0) < DH
    return jnp.where(first, wide[:, :HALF], wide[:, HALF:])


def head_sums(x):
    return jnp.concatenate(
        [x[:DH].sum(0, keepdims=True), x[DH:].sum(0, keepdims=True)], axis=1
    )


def softmax(blocks):
    highest = blocks[0].max(axis=0, keepdims=True)
    for block in blocks[1:]:
        highest = jnp.maximum(highest, block.max(axis=0, keepdims=True))
    powers = [jnp.exp(block - highest) for block in blocks]
    total = powers[0].sum(axis=0, keepdims=True)
    for power in powers[1:]:
        total = total + power.sum(axis=0, keepdims=True)
    share = 1.0 / total
    return [power * share for power in powers]


def row_attention(x_ref, kv_ref, pattern_ref, row, out_ref, total_ref):
    total_ref[...] = jnp.zeros_like(total_ref)
    shape = (HALF, 2 * HALF)
    same = iota(shape, 0) <= lax.rem(iota(shape, 1), HALF)
    has_earlier = jnp.broadcast_to(row >= 1, shape)
    keys_t, values_t = kv_ref[0].T, kv_ref[1].T
    for b in range(2):
        start = b * HALF
        rows, window = pl.ds(start, HALF), pl.ds(start, 3 * HALF)
        first, second = (pattern_ref[h, b, 1 - b] * jnp.minimum(row + b, 1) for h in range(2))
        whole_open = jnp.where(iota(shape, 1) < HALF, first, second) > 0
        q = per_head(x_ref[0, rows, :]) * jnp.asarray(0.125, BF16)
        g = per_head(x_ref[1, rows, :])
        keys, values = kv_ref[0, window, :], kv_ref[1, window, :]
        scores, weight_grads = matmul_nt(keys, q), matmul_nt(values, g)

        def chosen(x, earlier_else):
            earlier, whole, this = (x[i * HALF : (i + 1) * HALF] for i in range(3))
            return jnp.where(same, this, earlier_else(earlier)), whole

        diag, whole = chosen(scores, lambda x: jnp.where(has_earlier, x, NEG))
        p_diag, p_whole = softmax([diag, jnp.where(whole_open, whole, NEG)])

        def spread(at_diag, at_whole):
            at_diag, at_whole = at_diag.astype(BF16), at_whole.astype(BF16)
            zero = jnp.zeros_like(at_diag)
            return jnp.concatenate(
                [jnp.where(same, zero, at_diag), at_whole, jnp.where(same, at_diag, zero)], axis=0
            )

        w = spread(p_diag, p_whole)
        attended = both_heads(matmul(values_t[:, start : start + 3 * HALF], w)).astype(BF16)
        out_ref[0, rows, :HALF] = attended.T
        dots = head_sums(x_ref[1, rows, :].T.astype(F32) * attended.astype(F32))
        d_diag, d_whole = chosen(weight_grads, lambda x: x)
        e = spread(p_diag * (d_diag - dots), p_whole * (d_whole - dots))
        grad = both_heads(matmul(keys_t[:, start : start + 3 * HALF], e)) * 0.125
        out_ref[1, rows, :HALF] = grad.astype(BF16).T
        total_ref[0, window, :] += matmul(e, q)
        total_ref[1, window, :] += matmul(w, g)


def column_attention(q, k, v, g, bias):
    g_t = g.T.astype(F32)
    q = per_head(q) * jnp.asarray(0.125, BF16)
    g = per_head(g)
    (p,) = softmax([matmul_nt(k, q) + bias])
    w = p.astype(BF16)
    attended = both_heads(matmul(v.T, w)).astype(BF16)
    dots = head_sums(g_t * attended.astype(F32))
    e = (p * (matmul_nt(v, g) - dots)).astype(BF16)
    grad = (both_heads(matmul(k.T, e)) * 0.125).astype(BF16)
    return attended.T, grad.T, matmul(e, q).astype(BF16), matmul(w, g).astype(BF16)


def column_bias(pattern_ref):
    shape = (ROWS, 2 * ROWS)
    key, stacked = iota(shape, 0), iota(shape, 1)
    query = lax.rem(stacked, ROWS)
    which = query // 32 + jnp.where(stacked < ROWS, 0, 4)
    bits = jnp.zeros(shape, jnp.int32)
    for h in range(2):
        for b in range(4):
            code = sum(pattern_ref[h, b, j] * (1 << j) for j in range(4))
            bits = jnp.where(which == 4 * h + b, code, bits)
    allowed = (key <= query) & (((bits >> (key // 32)) & 1) > 0)
    return jnp.where(allowed, 0.0, NEG)


def reorder(source, target):
    order, size, row = {}, 1, iota((BLOCK, BLOCK), 1)
    for name in reversed(source):
        order[name] = lax.rem(row // size, source[name])
        size *= source[name]
    place = 0
    for name in target:
        place = place * source[name] + order[name]
    return jnp.where(place == iota((BLOCK, BLOCK), 0), 1.0, 0.0).astype(BF16)


def kernel(
    q_hbm, k_hbm, v_hbm, g_hbm, row_pattern_hbm, column_pattern_hbm,
    result,
    xc, xr, kv, back, backr, total, perm, bias,
    s1a, r1a, r1b, s2a, r2a, s2b, r2b, found, s3, r3,
    row_pattern, column_pattern, pattern_sem, in_sem, ring_sem, send_sem, recv_sem, back_send_sem, back_recv_sem,
):
    me = lax.axis_index("seq")
    y, zx = me // NZX, lax.rem(me, NZX)
    batch = lax.axis_index("batch")
    place_here = {"mp": lax.axis_index("mp"), "batch": batch}
    after = {"seq": lax.rem(me + 1, ROWS), **place_here}
    before = {"seq": lax.rem(me + ROWS - 1, ROWS), **place_here}

    zx_places = [lax.rem(zx + i, NZX) for i in range(NZX)]
    y_places = [lax.rem(y + i, NY) for i in range(NY)]

    def device(seq):
        return {"seq": seq, **place_here}

    zx_peers = [(zx_places[i], device(y * NZX + zx_places[i])) for i in ZX_ORDER]
    y_peers = [(y_places[i], device(y_places[i] * NZX + zx)) for i in Y_ORDER]

    inputs = (q_hbm, k_hbm, v_hbm, g_hbm)

    this_row = pl.ds(CW, CW)
    row_places = (xr.at[0], kv.at[0, this_row], kv.at[1, this_row], xr.at[1])

    def loads_of(part, places):
        return [
            pltpu.make_async_copy(h.at[0, :, pl.ds(part * HALF, HALF)], place, in_sem.at[part, i])
            for i, (h, place) in enumerate(zip(inputs, places))
        ]

    column_loads = loads_of(1, [xc.at[i // 2, i % 2] for i in range(PIECES)])
    row_loads = loads_of(0, row_places)
    patterns = [
        pltpu.make_async_copy(row_pattern_hbm, row_pattern, pattern_sem.at[0]),
        pltpu.make_async_copy(column_pattern_hbm, column_pattern, pattern_sem.at[1]),
    ]
    for load in column_loads:
        load.start()

    barrier = pltpu.get_barrier_semaphore()

    def greet(peer):
        pl.semaphore_signal(barrier, inc=1, device_id=peer, device_id_type=MESH)

    for _, peer in zx_peers + y_peers:
        greet(peer)
    greet(after)
    greet(before)
    for load in row_loads + patterns:
        load.start()

    def exchange(step, source, landing, over_zx):
        place = (step, 0 if over_zx else 1)
        peers, mine = (zx_peers, zx) if over_zx else (y_peers, y)
        for other, peer in peers:
            pltpu.make_async_remote_copy(
                src_ref=source(other),
                dst_ref=landing(mine),
                send_sem=send_sem.at[place],
                recv_sem=recv_sem.at[place],
                device_id=peer,
                device_id_type=MESH,
            ).start()
        pltpu.make_async_copy(source(mine), landing(mine), recv_sem.at[place]).start()

    def send(step, source, dest, over_zx):
        exchange(step, lambda j: source.at[j], lambda j: dest.at[j], over_zx)

    def arrived(step, whole, over_zx):
        pltpu.make_async_copy(whole, whole, recv_sem.at[step, 0 if over_zx else 1]).wait()

    def sent(step, dest, over_zx):
        part = dest.at[pl.ds(0, dest.shape[0] - 1)]
        pltpu.make_async_copy(part, part, send_sem.at[step, 0 if over_zx else 1]).wait()

    def last_columns(j=None):
        rows = pl.ds(HALF, HALF) if j is None else pl.ds(pl.multiple_of(HALF + j * NZX, NZX), NZX)
        return (slice(None), slice(None), rows, slice(None))

    grid_rows = {"piece": 2, "y": NY, "zx": NZX}
    by_zx = ("zx", "piece", "y")
    perm[PACK] = reorder(grid_rows, by_zx)
    for load in column_loads:
        load.wait()
    pl.semaphore_wait(barrier, (NZX - 1) + (NY - 1) + 2)

    def over_y():
        exchange(0, lambda j: xc.at[last_columns(j)], lambda j: r1b.at[j], False)

    pl.when(batch == 1)(over_y)
    for p in range(PAIRS):
        rows = xc[p, :, :HALF, :].reshape(BLOCK, HALF)
        packed = matmul(perm[PACK], rows).astype(BF16)
        s1a[:, p] = packed.reshape(NZX, 2 * NY, HALF)
    send(0, s1a, r1a, True)
    pl.when(batch == 0)(over_y)
    for load in row_loads:
        load.wait()
    forward = pltpu.make_async_remote_copy(
        src_ref=kv.at[:, this_row],
        dst_ref=kv.at[:, pl.ds(0, CW)],
        send_sem=ring_sem.at[0],
        recv_sem=ring_sem.at[1],
        device_id=after,
        device_id_type=MESH,
    )
    forward.start()

    for t, source, target in (
        (UNPACK, {"zx": NZX, "piece": 2, "y": NY}, ("piece", "y", "zx")),
        (ZX_TO_Y, {"zx": NZX, "piece": 2, "y": NY}, ("y", "piece", "zx")),
        (Y_TO_ZX, {"y": NY, "piece": 2, "zx": NZX}, ("zx", "piece", "y")),
        (SPREAD, {"piece": 2 * PIECES, "row": PART}, ("row", "piece")),
        (GATHER, {"row": PART, "piece": 2 * PIECES}, ("piece", "row")),
    ):
        perm[t] = reorder(source, target)
    for load in patterns:
        load.wait()
    bias[...] = column_bias(column_pattern)

    def swap(dest, source, t):
        for p in range(PAIRS):
            rows = matmul(perm[t], source[:, p].reshape(BLOCK, HALF)).astype(BF16)
            dest[:, p] = rows.reshape(dest.shape[:1] + dest.shape[2:])

    arrived(0, r1a, True)
    swap(s2a, r1a, ZX_TO_Y)
    send(1, s2a, r2a, False)
    arrived(0, r1b, False)
    swap(s2b, r1b, Y_TO_ZX)
    send(1, s2b, r2b, True)

    forward.wait()
    row_attention(xr, kv, row_pattern, me, result, total)
    back[...] = total[:, :CW, :].astype(BF16)
    backward = pltpu.make_async_remote_copy(
        src_ref=back,
        dst_ref=backr,
        send_sem=ring_sem.at[2],
        recv_sem=ring_sem.at[3],
        device_id=before,
        device_id_type=MESH,
    )
    backward.start()

    arrived(1, r2a, False)
    pieces = [r2a[:, i // 2, i % 2].reshape(ROWS, HALF) for i in range(PIECES)]
    for i, found_here in enumerate(column_attention(*pieces, bias[...])):
        found[0, i] = found_here
    arrived(1, r2b, True)
    pieces = []
    for p in range(PAIRS):
        rows = matmul(perm[UNPACK], r2b[:, p].reshape(BLOCK, HALF)).astype(BF16)
        pieces += [rows[:ROWS], rows[ROWS:]]
    for i, found_here in enumerate(column_attention(*pieces, bias[...])):
        found[1, i] = found_here

    for k in range(ROWS // PART):
        part = pl.ds(k * PART, PART)
        rows = found[:, :, part, :].reshape(BLOCK, HALF)
        s3[part] = matmul(perm[SPREAD], rows).astype(BF16).reshape(PART, 2 * PIECES, HALF)

    for i in ALL_ORDER:
        other = y_places[i // NZX] * NZX + zx_places[i % NZX]
        pltpu.make_async_remote_copy(
            src_ref=s3.at[other],
            dst_ref=r3.at[me],
            send_sem=back_send_sem,
            recv_sem=back_recv_sem,
            device_id=device(other),
            device_id_type=MESH,
        ).start()
    pltpu.make_async_copy(s3.at[me], r3.at[me], back_recv_sem).start()

    backward.wait()
    for i in range(2):
        result[2 + i, :, :HALF] = (total[i, CW:, :] + backr[i].astype(F32)).astype(BF16)

    pltpu.make_async_copy(r3, r3, back_recv_sem).wait()
    for k in range(ROWS // PART):
        part = pl.ds(k * PART, PART)
        rows = matmul(perm[GATHER], r3[part].reshape(BLOCK, HALF)).astype(BF16)
        for c in range(2):
            for i in range(PIECES):
                start = (c * PIECES + i) * PART
                place = pl.ds(c * HALF + k * PART, PART)
                result[i, place, HALF:] = rows[start : start + PART]

    for step, (over_zx, over_y) in enumerate(((r1a, r1b), (r2b, r2a))):
        sent(step, over_zx, True)
        sent(step, over_y, False)
    others = s3.at[pl.ds(0, ROWS - 1)]
    pltpu.make_async_copy(others, others, back_send_sem).wait()


def write_out(result, o0, o1, o2, o3, sem):
    copies = [
        pltpu.make_async_copy(result.at[i], o.at[0], sem.at[i])
        for i, o in enumerate((o0, o1, o2, o3))
    ]
    for copy in copies:
        copy.start()
    for copy in copies:
        copy.wait()


def per_device(queries, key_vectors, value_vectors, cotangent, row_pattern, column_pattern):
    by_zx = pltpu.VMEM((NZX, PAIRS, 2 * NY, HALF), BF16)
    by_y = pltpu.VMEM((NY, PAIRS, 2, NZX, HALF), BF16)
    direct = pltpu.VMEM((ROWS, 2 * PIECES, HALF), BF16)
    vmem = pl.BlockSpec(memory_space=pltpu.VMEM)
    hbm = pl.BlockSpec(memory_space=pltpu.HBM)
    halves = pltpu.VMEM((PAIRS, 2, CW, HALF), BF16)
    pair = pltpu.VMEM((2, CW, HALF), BF16)
    in_hbm = [
        pltpu.with_memory_space_constraint(x, pltpu.HBM)
        for x in (queries, key_vectors, value_vectors, cotangent, row_pattern, column_pattern)
    ]
    result = pl.pallas_call(
        kernel,
        out_shape=pltpu.VMEM((PIECES, CW, 2 * HALF), BF16),
        in_specs=[hbm] * 6,
        out_specs=vmem,
        scratch_shapes=[
            halves, pair,
            pltpu.VMEM((2, 2 * CW, HALF), BF16),
            pair, pair,
            pltpu.VMEM((2, 2 * CW, HALF), F32),
            pltpu.VMEM((6, BLOCK, BLOCK), BF16),
            pltpu.VMEM((ROWS, 2 * ROWS), F32),
            by_zx, by_zx, by_y,
            by_y, by_y, by_zx, by_zx,
            pltpu.VMEM((2, PIECES, ROWS, HALF), BF16),
            direct, direct,
            pltpu.SMEM(row_pattern.shape, jnp.int32),
            pltpu.SMEM(column_pattern.shape, jnp.int32),
            pltpu.SemaphoreType.DMA((2,)),
            pltpu.SemaphoreType.DMA((2, PIECES)),
            pltpu.SemaphoreType.DMA((4,)),
            pltpu.SemaphoreType.DMA((2, 2)),
            pltpu.SemaphoreType.DMA((2, 2)),
            pltpu.SemaphoreType.DMA,
            pltpu.SemaphoreType.DMA,
        ],
        compiler_params=pltpu.CompilerParams(
            collective_id=0, has_side_effects=True, vmem_limit_bytes=40 * 1024 * 1024
        ),
        cost_estimate=pl.CostEstimate(
            flops=800_000_000, bytes_accessed=1_050_000, transcendentals=200_000
        ),
        name="grid_attention",
    )(*in_hbm)
    return pl.pallas_call(
        write_out,
        out_shape=[jax.ShapeDtypeStruct(queries.shape, BF16)] * 4,
        in_specs=[vmem],
        out_specs=[hbm] * 4,
        scratch_shapes=[pltpu.SemaphoreType.DMA((PIECES,))],
        cost_estimate=pl.CostEstimate(flops=0, bytes_accessed=1_050_000, transcendentals=0),
        compiler_params=pltpu.CompilerParams(vmem_limit_bytes=8 * 1024 * 1024),
        name="write_out",
    )(pltpu.with_memory_space_constraint(result, pltpu.VMEM))


def solution(mesh):
    rows = P(("batch", "seq"), None, "mp")
    heads = P("mp", None, None)
    return jax.shard_map(
        per_device,
        mesh=mesh,
        in_specs=(rows, rows, rows, rows, heads, heads),
        out_specs=(rows, rows, rows, rows),
        check_vma=False,
    )
```

```python
import jax
import jax.numpy as jnp
from jax import lax
from jax.experimental import pallas as pl
from jax.experimental.pallas import tpu as pltpu
from jax.sharding import PartitionSpec as P

MESH = pl.DeviceIdType.MESH
F32 = jnp.float32
BF16 = jnp.bfloat16
NEG = -1e30

NY = 8
NZX = 16
ROWS = NY * NZX
CW = 256
HALF = 128
DH = 64
PIECES = 4
PAIRS = PIECES // 2
BLOCK = 2 * ROWS
PART = 32
PACK, UNPACK, ZX_TO_Y, Y_TO_ZX, SPREAD, GATHER = range(6)


def hops(offset, size):
    return min(offset, size - offset)


def far_first(count, distance):
    return sorted(range(1, count), key=lambda i: (-distance(i), i * 37 % count))


Y_ORDER = far_first(NY, lambda i: hops(i, NY))
ZX_ORDER = far_first(NZX, lambda i: hops(i // 2, NZX // 2) + i % 2)
ALL_ORDER = far_first(ROWS, lambda i: hops(i // NZX, NY) + hops(i % NZX // 2, NZX // 2) + i % 2)


def iota(shape, axis):
    return lax.broadcasted_iota(jnp.int32, shape, axis)


def matmul(a, b):
    return lax.dot_general(a, b, (((1,), (0,)), ((), ())), preferred_element_type=F32)


def matmul_nt(a, b):
    return lax.dot_general(a, b, (((1,), (1,)), ((), ())), preferred_element_type=F32)


def per_head(x):
    first = iota(x.shape, 1) < DH
    zero = jnp.zeros_like(x)
    return jnp.concatenate([jnp.where(first, x, zero), jnp.where(first, zero, x)], axis=0)


def both_heads(wide):
    first = iota((HALF, HALF), 0) < DH
    return jnp.where(first, wide[:, :HALF], wide[:, HALF:])


def head_sums(x):
    return jnp.concatenate(
        [x[:DH].sum(0, keepdims=True), x[DH:].sum(0, keepdims=True)], axis=1
    )


def softmax(blocks):
    highest = blocks[0].max(axis=0, keepdims=True)
    for block in blocks[1:]:
        highest = jnp.maximum(highest, block.max(axis=0, keepdims=True))
    powers = [jnp.exp(block - highest) for block in blocks]
    total = powers[0].sum(axis=0, keepdims=True)
    for power in powers[1:]:
        total = total + power.sum(axis=0, keepdims=True)
    share = 1.0 / total
    return [power * share for power in powers]


def row_attention(x_ref, kv_ref, pattern_ref, row, out_ref, total_ref):
    shape = (HALF, 2 * HALF)
    same = iota(shape, 0) <= (iota((1, 2 * HALF), 1) & (HALF - 1))
    has_earlier = jnp.broadcast_to(row >= 1, shape)
    keys_t, values_t = kv_ref[0].T, kv_ref[1].T
    for b in range(2):
        start = b * HALF
        rows, window = pl.ds(start, HALF), pl.ds(start, 3 * HALF)
        first, second = (pattern_ref[h, b, 1 - b] * jnp.minimum(row + b, 1) for h in range(2))
        whole_open = jnp.where(iota((1, 2 * HALF), 1) < HALF, first, second) > 0
        q = per_head(x_ref[0, rows, :]) * jnp.asarray(0.125, BF16)
        g = per_head(x_ref[1, rows, :])
        keys, values = kv_ref[0, window, :], kv_ref[1, window, :]
        scores, weight_grads = matmul_nt(keys, q), matmul_nt(values, g)

        def chosen(x, earlier_else):
            earlier, whole, this = (x[i * HALF : (i + 1) * HALF] for i in range(3))
            return jnp.where(same, this, earlier_else(earlier)), whole

        diag, whole = chosen(scores, lambda x: jnp.where(has_earlier, x, NEG))
        p_diag, p_whole = softmax([diag, jnp.where(whole_open, whole, NEG)])

        def spread(at_diag, at_whole):
            at_diag, at_whole = at_diag.astype(BF16), at_whole.astype(BF16)
            zero = jnp.zeros_like(at_diag)
            return jnp.concatenate(
                [jnp.where(same, zero, at_diag), at_whole, jnp.where(same, at_diag, zero)], axis=0
            )

        w = spread(p_diag, p_whole)
        attended = both_heads(matmul(values_t[:, start : start + 3 * HALF], w)).astype(BF16)
        out_ref[0, rows, :HALF] = attended.T
        dots = head_sums(x_ref[1, rows, :].T.astype(F32) * attended.astype(F32))
        d_diag, d_whole = chosen(weight_grads, lambda x: x)
        e = spread(p_diag * (d_diag - dots), p_whole * (d_whole - dots))
        grad = both_heads(matmul(keys_t[:, start : start + 3 * HALF], e)) * 0.125
        out_ref[1, rows, :HALF] = grad.astype(BF16).T
        for i, term in enumerate((matmul(e, q), matmul(w, g))):
            if b == 0:
                total_ref[i, window, :] = term
            else:
                total_ref[i, HALF : 3 * HALF, :] += term[: 2 * HALF]
                total_ref[i, 3 * HALF :, :] = term[2 * HALF :]


def column_attention(q, k, v, g, bias):
    g_t = g.T.astype(F32)
    q = per_head(q) * jnp.asarray(0.125, BF16)
    g = per_head(g)
    (p,) = softmax([matmul_nt(k, q) + bias])
    w = p.astype(BF16)
    attended = both_heads(matmul(v.T, w)).astype(BF16)
    dots = head_sums(g_t * attended.astype(F32))
    e = (p * (matmul_nt(v, g) - dots)).astype(BF16)
    grad = (both_heads(matmul(k.T, e)) * 0.125).astype(BF16)
    return attended.T, grad.T, matmul(e, q).astype(BF16), matmul(w, g).astype(BF16)


def column_bias(pattern_ref):
    key, stacked = iota((ROWS, 1), 0), iota((1, 2 * ROWS), 1)
    query = stacked & (ROWS - 1)
    bits = jnp.zeros(stacked.shape, jnp.int32)
    for h in range(2):
        for b in range(4):
            code = sum(pattern_ref[h, b, j] * (1 << j) for j in range(4))
            bits = jnp.where(stacked // 32 == 4 * h + b, code, bits)
    seen = jnp.zeros((ROWS, 2 * ROWS), jnp.int32)
    for j in range(4):
        seen = jnp.where(key // 32 == j, (bits >> j) & 1, seen)
    allowed = (key <= query) & (seen > 0)
    return jnp.where(allowed, 0.0, NEG)


def reorder(source, target):
    order, size, row = {}, 1, iota((1, BLOCK), 1)
    for name in reversed(source):
        order[name] = (row // size) & (source[name] - 1)
        size *= source[name]
    place = 0
    for name in target:
        place = place * source[name] + order[name]
    return jnp.where(place == iota((BLOCK, BLOCK), 0), 1.0, 0.0).astype(BF16)


def kernel(
    q_hbm, k_hbm, v_hbm, g_hbm, row_pattern_hbm, column_pattern_hbm,
    result,
    xc, xr, kv, back, backr, total, perm, bias,
    s1a, r1a, r1b, s2a, r2a, s2b, r2b, found, s3, r3,
    row_pattern, column_pattern, pattern_sem, in_sem, ring_sem, send_sem, recv_sem, back_send_sem, back_recv_sem,
):
    me = lax.axis_index("seq")
    y, zx = me // NZX, lax.rem(me, NZX)
    place_here = {"mp": lax.axis_index("mp"), "batch": lax.axis_index("batch")}
    after = {"seq": lax.rem(me + 1, ROWS), **place_here}
    before = {"seq": lax.rem(me + ROWS - 1, ROWS), **place_here}

    zx_places = [lax.rem(zx + i, NZX) for i in range(NZX)]
    y_places = [lax.rem(y + i, NY) for i in range(NY)]

    def device(seq):
        return {"seq": seq, **place_here}

    zx_peers = [(zx_places[i], device(y * NZX + zx_places[i])) for i in ZX_ORDER]
    y_peers = [(y_places[i], device(y_places[i] * NZX + zx)) for i in Y_ORDER]

    inputs = (q_hbm, k_hbm, v_hbm, g_hbm)

    this_row = pl.ds(CW, CW)
    row_places = (xr.at[0], kv.at[0, this_row], kv.at[1, this_row], xr.at[1])

    def loads_of(part, places):
        return [
            pltpu.make_async_copy(h.at[0, :, pl.ds(part * HALF, HALF)], place, in_sem.at[part, i])
            for i, (h, place) in enumerate(zip(inputs, places))
        ]

    column_loads = loads_of(1, [xc.at[i // 2, i % 2] for i in range(PIECES)])
    row_loads = loads_of(0, row_places)
    patterns = [
        pltpu.make_async_copy(row_pattern_hbm, row_pattern, pattern_sem.at[0]),
        pltpu.make_async_copy(column_pattern_hbm, column_pattern, pattern_sem.at[1]),
    ]
    for load in column_loads:
        load.start()

    barrier = pltpu.get_barrier_semaphore()

    def greet(peer):
        pl.semaphore_signal(barrier, inc=1, device_id=peer, device_id_type=MESH)

    for _, peer in zx_peers + y_peers:
        greet(peer)
    greet(after)
    greet(before)
    for load in row_loads + patterns:
        load.start()

    def exchange(step, source, landing, over_zx):
        place = (step, 0 if over_zx else 1)
        peers, mine = (zx_peers, zx) if over_zx else (y_peers, y)
        for other, peer in peers:
            pltpu.make_async_remote_copy(
                src_ref=source(other),
                dst_ref=landing(mine),
                send_sem=send_sem.at[place],
                recv_sem=recv_sem.at[place],
                device_id=peer,
                device_id_type=MESH,
            ).start()
        pltpu.make_async_copy(source(mine), landing(mine), recv_sem.at[place]).start()

    def send(step, source, dest, over_zx):
        exchange(step, lambda j: source.at[j], lambda j: dest.at[j], over_zx)

    def arrived(step, whole, over_zx):
        pltpu.make_async_copy(whole, whole, recv_sem.at[step, 0 if over_zx else 1]).wait()

    def sent(step, dest, over_zx):
        part = dest.at[pl.ds(0, dest.shape[0] - 1)]
        pltpu.make_async_copy(part, part, send_sem.at[step, 0 if over_zx else 1]).wait()

    def last_columns(j=None):
        rows = pl.ds(HALF, HALF) if j is None else pl.ds(pl.multiple_of(HALF + j * NZX, NZX), NZX)
        return (slice(None), slice(None), rows, slice(None))

    grid_rows = {"piece": 2, "y": NY, "zx": NZX}
    by_zx = ("zx", "piece", "y")
    perm[PACK] = reorder(grid_rows, by_zx)
    for load in column_loads:
        load.wait()
    for p in range(PAIRS):
        rows = xc[p, :, :HALF, :].reshape(BLOCK, HALF)
        packed = matmul(perm[PACK], rows).astype(BF16)
        s1a[:, p] = packed.reshape(NZX, 2 * NY, HALF)
    pl.semaphore_wait(barrier, (NZX - 1) + (NY - 1) + 2)

    send(0, s1a, r1a, True)
    exchange(0, lambda j: xc.at[last_columns(j)], lambda j: r1b.at[j], False)
    for load in row_loads:
        load.wait()
    forward = pltpu.make_async_remote_copy(
        src_ref=kv.at[:, this_row],
        dst_ref=kv.at[:, pl.ds(0, CW)],
        send_sem=ring_sem.at[0],
        recv_sem=ring_sem.at[1],
        device_id=after,
        device_id_type=MESH,
    )
    forward.start()

    for t, source, target in (
        (UNPACK, {"zx": NZX, "piece": 2, "y": NY}, ("piece", "y", "zx")),
        (ZX_TO_Y, {"zx": NZX, "piece": 2, "y": NY}, ("y", "piece", "zx")),
        (Y_TO_ZX, {"y": NY, "piece": 2, "zx": NZX}, ("zx", "piece", "y")),
        (SPREAD, {"piece": 2 * PIECES, "row": PART}, ("row", "piece")),
        (GATHER, {"row": PART, "piece": 2 * PIECES}, ("piece", "row")),
    ):
        perm[t] = reorder(source, target)
    for load in patterns:
        load.wait()
    bias[...] = column_bias(column_pattern)

    def swap(dest, source, t):
        for p in range(PAIRS):
            rows = matmul(perm[t], source[:, p].reshape(BLOCK, HALF)).astype(BF16)
            dest[:, p] = rows.reshape(dest.shape[:1] + dest.shape[2:])

    arrived(0, r1a, True)
    swap(s2a, r1a, ZX_TO_Y)
    send(1, s2a, r2a, False)
    arrived(0, r1b, False)
    swap(s2b, r1b, Y_TO_ZX)
    send(1, s2b, r2b, True)

    forward.wait()
    row_attention(xr, kv, row_pattern, me, result, total)
    back[...] = total[:, :CW, :].astype(BF16)
    backward = pltpu.make_async_remote_copy(
        src_ref=back,
        dst_ref=backr,
        send_sem=ring_sem.at[2],
        recv_sem=ring_sem.at[3],
        device_id=before,
        device_id_type=MESH,
    )
    backward.start()

    arrived(1, r2a, False)
    pieces = [r2a[:, i // 2, i % 2].reshape(ROWS, HALF) for i in range(PIECES)]
    for i, found_here in enumerate(column_attention(*pieces, bias[...])):
        found[0, i] = found_here
    arrived(1, r2b, True)
    pieces = []
    for p in range(PAIRS):
        rows = matmul(perm[UNPACK], r2b[:, p].reshape(BLOCK, HALF)).astype(BF16)
        pieces += [rows[:ROWS], rows[ROWS:]]
    for i, found_here in enumerate(column_attention(*pieces, bias[...])):
        found[1, i] = found_here

    for k in range(ROWS // PART):
        part = pl.ds(k * PART, PART)
        rows = found[:, :, part, :].reshape(BLOCK, HALF)
        s3[part] = matmul(perm[SPREAD], rows).astype(BF16).reshape(PART, 2 * PIECES, HALF)

    for i in ALL_ORDER:
        other = y_places[i // NZX] * NZX + zx_places[i % NZX]
        pltpu.make_async_remote_copy(
            src_ref=s3.at[other],
            dst_ref=r3.at[me],
            send_sem=back_send_sem,
            recv_sem=back_recv_sem,
            device_id=device(other),
            device_id_type=MESH,
        ).start()
    pltpu.make_async_copy(s3.at[me], r3.at[me], back_recv_sem).start()

    backward.wait()
    for i in range(2):
        result[2 + i, :, :HALF] = (total[i, CW:, :] + backr[i].astype(F32)).astype(BF16)

    pltpu.make_async_copy(r3, r3, back_recv_sem).wait()
    for k in range(ROWS // PART):
        part = pl.ds(k * PART, PART)
        rows = matmul(perm[GATHER], r3[part].reshape(BLOCK, HALF)).astype(BF16)
        for c in range(2):
            for i in range(PIECES):
                start = (c * PIECES + i) * PART
                place = pl.ds(c * HALF + k * PART, PART)
                result[i, place, HALF:] = rows[start : start + PART]

    for step, (over_zx, over_y) in enumerate(((r1a, r1b), (r2b, r2a))):
        sent(step, over_zx, True)
        sent(step, over_y, False)
    others = s3.at[pl.ds(0, ROWS - 1)]
    pltpu.make_async_copy(others, others, back_send_sem).wait()


def write_out(result, o0, o1, o2, o3, sem):
    copies = [
        pltpu.make_async_copy(result.at[i], o.at[0], sem.at[i])
        for i, o in enumerate((o0, o1, o2, o3))
    ]
    for copy in copies:
        copy.start()
    for copy in copies:
        copy.wait()


def per_device(queries, key_vectors, value_vectors, cotangent, row_pattern, column_pattern):
    by_zx = pltpu.VMEM((NZX, PAIRS, 2 * NY, HALF), BF16)
    by_y = pltpu.VMEM((NY, PAIRS, 2, NZX, HALF), BF16)
    direct = pltpu.VMEM((ROWS, 2 * PIECES, HALF), BF16)
    vmem = pl.BlockSpec(memory_space=pltpu.VMEM)
    hbm = pl.BlockSpec(memory_space=pltpu.HBM)
    halves = pltpu.VMEM((PAIRS, 2, CW, HALF), BF16)
    pair = pltpu.VMEM((2, CW, HALF), BF16)
    in_hbm = [
        pltpu.with_memory_space_constraint(x, pltpu.HBM)
        for x in (queries, key_vectors, value_vectors, cotangent, row_pattern, column_pattern)
    ]
    result = pl.pallas_call(
        kernel,
        out_shape=pltpu.VMEM((PIECES, CW, 2 * HALF), BF16),
        in_specs=[hbm] * 6,
        out_specs=vmem,
        scratch_shapes=[
            halves, pair,
            pltpu.VMEM((2, 2 * CW, HALF), BF16),
            pair, pair,
            pltpu.VMEM((2, 2 * CW, HALF), F32),
            pltpu.VMEM((6, BLOCK, BLOCK), BF16),
            pltpu.VMEM((ROWS, 2 * ROWS), F32),
            by_zx, by_zx, by_y,
            by_y, by_y, by_zx, by_zx,
            pltpu.VMEM((2, PIECES, ROWS, HALF), BF16),
            direct, direct,
            pltpu.SMEM(row_pattern.shape, jnp.int32),
            pltpu.SMEM(column_pattern.shape, jnp.int32),
            pltpu.SemaphoreType.DMA((2,)),
            pltpu.SemaphoreType.DMA((2, PIECES)),
            pltpu.SemaphoreType.DMA((4,)),
            pltpu.SemaphoreType.DMA((2, 2)),
            pltpu.SemaphoreType.DMA((2, 2)),
            pltpu.SemaphoreType.DMA,
            pltpu.SemaphoreType.DMA,
        ],
        compiler_params=pltpu.CompilerParams(
            collective_id=0, has_side_effects=True, vmem_limit_bytes=40 * 1024 * 1024
        ),
        cost_estimate=pl.CostEstimate(
            flops=800_000_000, bytes_accessed=1_050_000, transcendentals=200_000
        ),
        name="grid_attention",
    )(*in_hbm)
    return pl.pallas_call(
        write_out,
        out_shape=[jax.ShapeDtypeStruct(queries.shape, BF16)] * 4,
        in_specs=[vmem],
        out_specs=[hbm] * 4,
        scratch_shapes=[pltpu.SemaphoreType.DMA((PIECES,))],
        cost_estimate=pl.CostEstimate(flops=0, bytes_accessed=1_050_000, transcendentals=0),
        compiler_params=pltpu.CompilerParams(vmem_limit_bytes=8 * 1024 * 1024),
        name="write_out",
    )(pltpu.with_memory_space_constraint(result, pltpu.VMEM))


def solution(mesh):
    rows = P(("batch", "seq"), None, "mp")
    heads = P("mp", None, None)
    return jax.shard_map(
        per_device,
        mesh=mesh,
        in_specs=(rows, rows, rows, rows, heads, heads),
        out_specs=(rows, rows, rows, rows),
        check_vma=False,
    )
```

```python
import jax
import jax.numpy as jnp
from jax import lax
from jax.experimental import pallas as pl
from jax.experimental.pallas import tpu as pltpu
from jax.sharding import PartitionSpec as P

MESH = pl.DeviceIdType.MESH
F32 = jnp.float32
BF16 = jnp.bfloat16
NEG = -1e30

NY = 8
NZX = 16
ROWS = NY * NZX
CW = 256
HALF = 128
DH = 64
PIECES = 4
PAIRS = PIECES // 2
BLOCK = 2 * ROWS
PART = 32
PACK, UNPACK, ZX_TO_Y, Y_TO_ZX, SPREAD, GATHER = range(6)


def hops(offset, size):
    return min(offset, size - offset)


def far_first(count, distance):
    return sorted(range(1, count), key=lambda i: (-distance(i), i * 37 % count))


Y_ORDER = far_first(NY, lambda i: hops(i, NY))
ZX_ORDER = far_first(NZX, lambda i: hops(i // 2, NZX // 2) + i % 2)
ALL_ORDER = far_first(ROWS, lambda i: hops(i // NZX, NY) + hops(i % NZX // 2, NZX // 2) + i % 2)


def iota(shape, axis):
    return lax.broadcasted_iota(jnp.int32, shape, axis)


def matmul(a, b):
    return lax.dot_general(a, b, (((1,), (0,)), ((), ())), preferred_element_type=F32)


def matmul_nt(a, b):
    return lax.dot_general(a, b, (((1,), (1,)), ((), ())), preferred_element_type=F32)


def per_head(x):
    first = iota(x.shape, 1) < DH
    zero = jnp.zeros_like(x)
    return jnp.concatenate([jnp.where(first, x, zero), jnp.where(first, zero, x)], axis=0)


def both_heads(wide):
    first = iota((HALF, HALF), 0) < DH
    return jnp.where(first, wide[:, :HALF], wide[:, HALF:])


def head_sums(x):
    return jnp.concatenate(
        [x[:DH].sum(0, keepdims=True), x[DH:].sum(0, keepdims=True)], axis=1
    )


def softmax(blocks):
    highest = blocks[0].max(axis=0, keepdims=True)
    for block in blocks[1:]:
        highest = jnp.maximum(highest, block.max(axis=0, keepdims=True))
    powers = [jnp.exp(block - highest) for block in blocks]
    total = powers[0].sum(axis=0, keepdims=True)
    for power in powers[1:]:
        total = total + power.sum(axis=0, keepdims=True)
    share = 1.0 / total
    return [power * share for power in powers]


def row_attention(x_ref, kv_ref, pattern_ref, row, out_ref, total_ref):
    shape = (HALF, 2 * HALF)
    same = iota(shape, 0) <= (iota((1, 2 * HALF), 1) & (HALF - 1))
    has_earlier = jnp.broadcast_to(row >= 1, shape)
    keys_t, values_t = kv_ref[0].T, kv_ref[1].T
    for b in range(2):
        start = b * HALF
        rows, window = pl.ds(start, HALF), pl.ds(start, 3 * HALF)
        first, second = (pattern_ref[h, b, 1 - b] * jnp.minimum(row + b, 1) for h in range(2))
        whole_open = jnp.where(iota((1, 2 * HALF), 1) < HALF, first, second) > 0
        q = per_head(x_ref[0, rows, :]) * jnp.asarray(0.125, BF16)
        g = per_head(x_ref[1, rows, :])
        keys, values = kv_ref[0, window, :], kv_ref[1, window, :]
        scores, weight_grads = matmul_nt(keys, q), matmul_nt(values, g)

        def chosen(x, earlier_else):
            earlier, whole, this = (x[i * HALF : (i + 1) * HALF] for i in range(3))
            return jnp.where(same, this, earlier_else(earlier)), whole

        diag, whole = chosen(scores, lambda x: jnp.where(has_earlier, x, NEG))
        p_diag, p_whole = softmax([diag, jnp.where(whole_open, whole, NEG)])

        def spread(at_diag, at_whole):
            at_diag, at_whole = at_diag.astype(BF16), at_whole.astype(BF16)
            zero = jnp.zeros_like(at_diag)
            return jnp.concatenate(
                [jnp.where(same, zero, at_diag), at_whole, jnp.where(same, at_diag, zero)], axis=0
            )

        w = spread(p_diag, p_whole)
        attended = both_heads(matmul(values_t[:, start : start + 3 * HALF], w)).astype(BF16)
        out_ref[0, rows, :HALF] = attended.T
        dots = head_sums(x_ref[1, rows, :].T.astype(F32) * attended.astype(F32))
        d_diag, d_whole = chosen(weight_grads, lambda x: x)
        e = spread(p_diag * (d_diag - dots), p_whole * (d_whole - dots))
        grad = both_heads(matmul(keys_t[:, start : start + 3 * HALF], e)) * 0.125
        out_ref[1, rows, :HALF] = grad.astype(BF16).T
        for i, term in enumerate((matmul(e, q), matmul(w, g))):
            if b == 0:
                total_ref[i, window, :] = term
            else:
                total_ref[i, HALF : 3 * HALF, :] += term[: 2 * HALF]
                total_ref[i, 3 * HALF :, :] = term[2 * HALF :]


def column_attention(q, k, v, g, bias):
    g_t = g.T.astype(F32)
    q = per_head(q) * jnp.asarray(0.125, BF16)
    g = per_head(g)
    (p,) = softmax([matmul_nt(k, q) + bias])
    w = p.astype(BF16)
    attended = both_heads(matmul(v.T, w)).astype(BF16)
    dots = head_sums(g_t * attended.astype(F32))
    e = (p * (matmul_nt(v, g) - dots)).astype(BF16)
    grad = (both_heads(matmul(k.T, e)) * 0.125).astype(BF16)
    return attended.T, grad.T, matmul(e, q).astype(BF16), matmul(w, g).astype(BF16)


def column_bias(pattern_ref):
    key, stacked = iota((ROWS, 1), 0), iota((1, 2 * ROWS), 1)
    query = stacked & (ROWS - 1)
    bits = jnp.zeros(stacked.shape, jnp.int32)
    for h in range(2):
        for b in range(4):
            code = sum(pattern_ref[h, b, j] * (1 << j) for j in range(4))
            bits = jnp.where(stacked // 32 == 4 * h + b, code, bits)
    seen = jnp.zeros((ROWS, 2 * ROWS), jnp.int32)
    for j in range(4):
        seen = jnp.where(key // 32 == j, (bits >> j) & 1, seen)
    allowed = (key <= query) & (seen > 0)
    return jnp.where(allowed, 0.0, NEG)


def reorder(source, target):
    order, size, row = {}, 1, iota((1, BLOCK), 1)
    for name in reversed(source):
        order[name] = (row // size) & (source[name] - 1)
        size *= source[name]
    place = 0
    for name in target:
        place = place * source[name] + order[name]
    return jnp.where(place == iota((BLOCK, BLOCK), 0), 1.0, 0.0).astype(BF16)


def kernel(
    q_hbm, k_hbm, v_hbm, g_hbm, row_pattern_hbm, column_pattern_hbm,
    result,
    xc, xr, kv, back, backr, total, perm, bias,
    s1a, r1a, r1b, s2a, r2a, s2b, r2b, found, s3, r3,
    row_pattern, column_pattern, pattern_sem, in_sem, ring_sem, send_sem, recv_sem, back_send_sem, back_recv_sem,
):
    me = lax.axis_index("seq")
    y, zx = me // NZX, lax.rem(me, NZX)
    batch = lax.axis_index("batch")
    place_here = {"mp": lax.axis_index("mp"), "batch": batch}
    after = {"seq": lax.rem(me + 1, ROWS), **place_here}
    before = {"seq": lax.rem(me + ROWS - 1, ROWS), **place_here}

    zx_places = [lax.rem(zx + i, NZX) for i in range(NZX)]
    y_places = [lax.rem(y + i, NY) for i in range(NY)]

    def device(seq):
        return {"seq": seq, **place_here}

    zx_peers = [(zx_places[i], device(y * NZX + zx_places[i])) for i in ZX_ORDER]
    y_peers = [(y_places[i], device(y_places[i] * NZX + zx)) for i in Y_ORDER]

    inputs = (q_hbm, k_hbm, v_hbm, g_hbm)

    this_row = pl.ds(CW, CW)
    row_places = (xr.at[0], kv.at[0, this_row], kv.at[1, this_row], xr.at[1])

    def loads_of(part, places):
        return [
            pltpu.make_async_copy(h.at[0, :, pl.ds(part * HALF, HALF)], place, in_sem.at[part, i])
            for i, (h, place) in enumerate(zip(inputs, places))
        ]

    column_loads = loads_of(1, [xc.at[i // 2, i % 2] for i in range(PIECES)])
    row_loads = loads_of(0, row_places)
    patterns = [
        pltpu.make_async_copy(row_pattern_hbm, row_pattern, pattern_sem.at[0]),
        pltpu.make_async_copy(column_pattern_hbm, column_pattern, pattern_sem.at[1]),
    ]
    for load in column_loads:
        load.start()

    barrier = pltpu.get_barrier_semaphore()

    def greet(peer):
        pl.semaphore_signal(barrier, inc=1, device_id=peer, device_id_type=MESH)

    for _, peer in zx_peers + y_peers:
        greet(peer)
    greet(after)
    greet(before)
    for load in row_loads + patterns:
        load.start()

    def exchange(step, source, landing, over_zx):
        place = (step, 0 if over_zx else 1)
        peers, mine = (zx_peers, zx) if over_zx else (y_peers, y)
        for other, peer in peers:
            pltpu.make_async_remote_copy(
                src_ref=source(other),
                dst_ref=landing(mine),
                send_sem=send_sem.at[place],
                recv_sem=recv_sem.at[place],
                device_id=peer,
                device_id_type=MESH,
            ).start()
        pltpu.make_async_copy(source(mine), landing(mine), recv_sem.at[place]).start()

    def send(step, source, dest, over_zx):
        exchange(step, lambda j: source.at[j], lambda j: dest.at[j], over_zx)

    def arrived(step, whole, over_zx):
        pltpu.make_async_copy(whole, whole, recv_sem.at[step, 0 if over_zx else 1]).wait()

    def sent(step, dest, over_zx):
        part = dest.at[pl.ds(0, dest.shape[0] - 1)]
        pltpu.make_async_copy(part, part, send_sem.at[step, 0 if over_zx else 1]).wait()

    def last_columns(j=None):
        rows = pl.ds(HALF, HALF) if j is None else pl.ds(pl.multiple_of(HALF + j * NZX, NZX), NZX)
        return (slice(None), slice(None), rows, slice(None))

    grid_rows = {"piece": 2, "y": NY, "zx": NZX}
    by_zx = ("zx", "piece", "y")
    perm[PACK] = reorder(grid_rows, by_zx)
    for load in column_loads:
        load.wait()
    pl.semaphore_wait(barrier, (NZX - 1) + (NY - 1) + 2)

    def over_y():
        exchange(0, lambda j: xc.at[last_columns(j)], lambda j: r1b.at[j], False)

    pl.when(batch == 0)(over_y)
    for p in range(PAIRS):
        rows = xc[p, :, :HALF, :].reshape(BLOCK, HALF)
        packed = matmul(perm[PACK], rows).astype(BF16)
        s1a[:, p] = packed.reshape(NZX, 2 * NY, HALF)
    send(0, s1a, r1a, True)
    pl.when(batch == 1)(over_y)
    for load in row_loads:
        load.wait()
    forward = pltpu.make_async_remote_copy(
        src_ref=kv.at[:, this_row],
        dst_ref=kv.at[:, pl.ds(0, CW)],
        send_sem=ring_sem.at[0],
        recv_sem=ring_sem.at[1],
        device_id=after,
        device_id_type=MESH,
    )
    forward.start()

    for t, source, target in (
        (UNPACK, {"zx": NZX, "piece": 2, "y": NY}, ("piece", "y", "zx")),
        (ZX_TO_Y, {"zx": NZX, "piece": 2, "y": NY}, ("y", "piece", "zx")),
        (Y_TO_ZX, {"y": NY, "piece": 2, "zx": NZX}, ("zx", "piece", "y")),
        (SPREAD, {"piece": 2 * PIECES, "row": PART}, ("row", "piece")),
        (GATHER, {"row": PART, "piece": 2 * PIECES}, ("piece", "row")),
    ):
        perm[t] = reorder(source, target)
    for load in patterns:
        load.wait()
    bias[...] = column_bias(column_pattern)

    def swap(dest, source, t):
        for p in range(PAIRS):
            rows = matmul(perm[t], source[:, p].reshape(BLOCK, HALF)).astype(BF16)
            dest[:, p] = rows.reshape(dest.shape[:1] + dest.shape[2:])

    arrived(0, r1a, True)
    swap(s2a, r1a, ZX_TO_Y)
    send(1, s2a, r2a, False)
    arrived(0, r1b, False)
    swap(s2b, r1b, Y_TO_ZX)
    send(1, s2b, r2b, True)

    forward.wait()
    row_attention(xr, kv, row_pattern, me, result, total)
    back[...] = total[:, :CW, :].astype(BF16)
    backward = pltpu.make_async_remote_copy(
        src_ref=back,
        dst_ref=backr,
        send_sem=ring_sem.at[2],
        recv_sem=ring_sem.at[3],
        device_id=before,
        device_id_type=MESH,
    )
    backward.start()

    arrived(1, r2a, False)
    pieces = [r2a[:, i // 2, i % 2].reshape(ROWS, HALF) for i in range(PIECES)]
    for i, found_here in enumerate(column_attention(*pieces, bias[...])):
        found[0, i] = found_here
    arrived(1, r2b, True)
    pieces = []
    for p in range(PAIRS):
        rows = matmul(perm[UNPACK], r2b[:, p].reshape(BLOCK, HALF)).astype(BF16)
        pieces += [rows[:ROWS], rows[ROWS:]]
    for i, found_here in enumerate(column_attention(*pieces, bias[...])):
        found[1, i] = found_here

    for k in range(ROWS // PART):
        part = pl.ds(k * PART, PART)
        rows = found[:, :, part, :].reshape(BLOCK, HALF)
        s3[part] = matmul(perm[SPREAD], rows).astype(BF16).reshape(PART, 2 * PIECES, HALF)

    for i in ALL_ORDER:
        other = y_places[i // NZX] * NZX + zx_places[i % NZX]
        pltpu.make_async_remote_copy(
            src_ref=s3.at[other],
            dst_ref=r3.at[me],
            send_sem=back_send_sem,
            recv_sem=back_recv_sem,
            device_id=device(other),
            device_id_type=MESH,
        ).start()
    pltpu.make_async_copy(s3.at[me], r3.at[me], back_recv_sem).start()

    backward.wait()
    for i in range(2):
        result[2 + i, :, :HALF] = (total[i, CW:, :] + backr[i].astype(F32)).astype(BF16)

    pltpu.make_async_copy(r3, r3, back_recv_sem).wait()
    for k in range(ROWS // PART):
        part = pl.ds(k * PART, PART)
        rows = matmul(perm[GATHER], r3[part].reshape(BLOCK, HALF)).astype(BF16)
        for c in range(2):
            for i in range(PIECES):
                start = (c * PIECES + i) * PART
                place = pl.ds(c * HALF + k * PART, PART)
                result[i, place, HALF:] = rows[start : start + PART]

    for step, (over_zx, over_y) in enumerate(((r1a, r1b), (r2b, r2a))):
        sent(step, over_zx, True)
        sent(step, over_y, False)
    others = s3.at[pl.ds(0, ROWS - 1)]
    pltpu.make_async_copy(others, others, back_send_sem).wait()


def write_out(result, o0, o1, o2, o3, sem):
    copies = [
        pltpu.make_async_copy(result.at[i], o.at[0], sem.at[i])
        for i, o in enumerate((o0, o1, o2, o3))
    ]
    for copy in copies:
        copy.start()
    for copy in copies:
        copy.wait()


def per_device(queries, key_vectors, value_vectors, cotangent, row_pattern, column_pattern):
    by_zx = pltpu.VMEM((NZX, PAIRS, 2 * NY, HALF), BF16)
    by_y = pltpu.VMEM((NY, PAIRS, 2, NZX, HALF), BF16)
    direct = pltpu.VMEM((ROWS, 2 * PIECES, HALF), BF16)
    vmem = pl.BlockSpec(memory_space=pltpu.VMEM)
    hbm = pl.BlockSpec(memory_space=pltpu.HBM)
    halves = pltpu.VMEM((PAIRS, 2, CW, HALF), BF16)
    pair = pltpu.VMEM((2, CW, HALF), BF16)
    in_hbm = [
        pltpu.with_memory_space_constraint(x, pltpu.HBM)
        for x in (queries, key_vectors, value_vectors, cotangent, row_pattern, column_pattern)
    ]
    result = pl.pallas_call(
        kernel,
        out_shape=pltpu.VMEM((PIECES, CW, 2 * HALF), BF16),
        in_specs=[hbm] * 6,
        out_specs=vmem,
        scratch_shapes=[
            halves, pair,
            pltpu.VMEM((2, 2 * CW, HALF), BF16),
            pair, pair,
            pltpu.VMEM((2, 2 * CW, HALF), F32),
            pltpu.VMEM((6, BLOCK, BLOCK), BF16),
            pltpu.VMEM((ROWS, 2 * ROWS), F32),
            by_zx, by_zx, by_y,
            by_y, by_y, by_zx, by_zx,
            pltpu.VMEM((2, PIECES, ROWS, HALF), BF16),
            direct, direct,
            pltpu.SMEM(row_pattern.shape, jnp.int32),
            pltpu.SMEM(column_pattern.shape, jnp.int32),
            pltpu.SemaphoreType.DMA((2,)),
            pltpu.SemaphoreType.DMA((2, PIECES)),
            pltpu.SemaphoreType.DMA((4,)),
            pltpu.SemaphoreType.DMA((2, 2)),
            pltpu.SemaphoreType.DMA((2, 2)),
            pltpu.SemaphoreType.DMA,
            pltpu.SemaphoreType.DMA,
        ],
        compiler_params=pltpu.CompilerParams(
            collective_id=0, has_side_effects=True, vmem_limit_bytes=40 * 1024 * 1024
        ),
        cost_estimate=pl.CostEstimate(
            flops=800_000_000, bytes_accessed=1_050_000, transcendentals=200_000
        ),
        name="grid_attention",
    )(*in_hbm)
    return pl.pallas_call(
        write_out,
        out_shape=[jax.ShapeDtypeStruct(queries.shape, BF16)] * 4,
        in_specs=[vmem],
        out_specs=[hbm] * 4,
        scratch_shapes=[pltpu.SemaphoreType.DMA((PIECES,))],
        cost_estimate=pl.CostEstimate(flops=0, bytes_accessed=1_050_000, transcendentals=0),
        compiler_params=pltpu.CompilerParams(vmem_limit_bytes=8 * 1024 * 1024),
        name="write_out",
    )(pltpu.with_memory_space_constraint(result, pltpu.VMEM))


def solution(mesh):
    rows = P(("batch", "seq"), None, "mp")
    heads = P("mp", None, None)
    return jax.shard_map(
        per_device,
        mesh=mesh,
        in_specs=(rows, rows, rows, rows, heads, heads),
        out_specs=(rows, rows, rows, rows),
        check_vma=False,
    )
```

```python
import jax
import jax.numpy as jnp
from jax import lax
from jax.experimental import pallas as pl
from jax.experimental.pallas import tpu as pltpu
from jax.sharding import PartitionSpec as P

MESH = pl.DeviceIdType.MESH
F32 = jnp.float32
BF16 = jnp.bfloat16
NEG = -1e30

NY = 8
NZX = 16
ROWS = NY * NZX
CW = 256
HALF = 128
DH = 64
PIECES = 4
PAIRS = PIECES // 2
BLOCK = 2 * ROWS
PART = 32
PACK, UNPACK, ZX_TO_Y, Y_TO_ZX, SPREAD, GATHER = range(6)


def hops(offset, size):
    return min(offset, size - offset)


def far_first(count, distance):
    return sorted(range(1, count), key=lambda i: (-distance(i), i * 37 % count))


Y_ORDER = far_first(NY, lambda i: hops(i, NY))
ZX_ORDER = far_first(NZX, lambda i: hops(i // 2, NZX // 2) + i % 2)
ALL_ORDER = far_first(ROWS, lambda i: hops(i // NZX, NY) + hops(i % NZX // 2, NZX // 2) + i % 2)


def iota(shape, axis):
    return lax.broadcasted_iota(jnp.int32, shape, axis)


def matmul(a, b):
    return lax.dot_general(a, b, (((1,), (0,)), ((), ())), preferred_element_type=F32)


def matmul_nt(a, b):
    return lax.dot_general(a, b, (((1,), (1,)), ((), ())), preferred_element_type=F32)


def per_head(x):
    first = iota(x.shape, 1) < DH
    zero = jnp.zeros_like(x)
    return jnp.concatenate([jnp.where(first, x, zero), jnp.where(first, zero, x)], axis=0)


def both_heads(wide):
    first = iota((HALF, HALF), 0) < DH
    return jnp.where(first, wide[:, :HALF], wide[:, HALF:])


def head_sums(x):
    return jnp.concatenate(
        [x[:DH].sum(0, keepdims=True), x[DH:].sum(0, keepdims=True)], axis=1
    )


def softmax(blocks):
    highest = blocks[0].max(axis=0, keepdims=True)
    for block in blocks[1:]:
        highest = jnp.maximum(highest, block.max(axis=0, keepdims=True))
    powers = [jnp.exp(block - highest) for block in blocks]
    total = powers[0].sum(axis=0, keepdims=True)
    for power in powers[1:]:
        total = total + power.sum(axis=0, keepdims=True)
    share = 1.0 / total
    return [power * share for power in powers]


def row_attention(x_ref, kv_ref, pattern_ref, row, out_ref, total_ref, w_ref, e_ref):
    shape = (HALF, 2 * HALF)
    same = iota(shape, 0) <= (iota((1, 2 * HALF), 1) & (HALF - 1))
    has_earlier = jnp.broadcast_to(row >= 1, shape)
    values_t = kv_ref[1].T
    for b in range(2):
        start = b * HALF
        rows, window = pl.ds(start, HALF), pl.ds(start, 3 * HALF)
        first, second = (pattern_ref[h, b, 1 - b] * jnp.minimum(row + b, 1) for h in range(2))
        whole_open = jnp.where(iota((1, 2 * HALF), 1) < HALF, first, second) > 0
        q = per_head(x_ref[0, rows, :]) * jnp.asarray(0.125, BF16)
        g = per_head(x_ref[1, rows, :])
        keys, values = kv_ref[0, window, :], kv_ref[1, window, :]
        scores, weight_grads = matmul_nt(keys, q), matmul_nt(values, g)

        def chosen(x, earlier_else):
            earlier, whole, this = (x[i * HALF : (i + 1) * HALF] for i in range(3))
            return jnp.where(same, this, earlier_else(earlier)), whole

        diag, whole = chosen(scores, lambda x: jnp.where(has_earlier, x, NEG))
        p_diag, p_whole = softmax([diag, jnp.where(whole_open, whole, NEG)])

        def spread(at_diag, at_whole):
            at_diag, at_whole = at_diag.astype(BF16), at_whole.astype(BF16)
            zero = jnp.zeros_like(at_diag)
            return jnp.concatenate(
                [jnp.where(same, zero, at_diag), at_whole, jnp.where(same, at_diag, zero)], axis=0
            )

        w = spread(p_diag, p_whole)
        attended = both_heads(matmul(values_t[:, start : start + 3 * HALF], w)).astype(BF16)
        out_ref[0, rows, :HALF] = attended.T
        dots = head_sums(x_ref[1, rows, :].T.astype(F32) * attended.astype(F32))
        d_diag, d_whole = chosen(weight_grads, lambda x: x)
        e = spread(p_diag * (d_diag - dots), p_whole * (d_whole - dots))
        w_ref[b], e_ref[b] = w, e
        earlier = 2 * HALF - start
        for i, term in enumerate((matmul(e[:earlier], q), matmul(w[:earlier], g))):
            if b == 0:
                total_ref[i, : 2 * HALF, :] = term
            else:
                total_ref[i, HALF : 2 * HALF, :] += term


def row_gradients(x_ref, kv_ref, out_ref, total_ref, w_ref, e_ref):
    keys_t = kv_ref[0].T
    for b in range(2):
        start = b * HALF
        rows = pl.ds(start, HALF)
        q = per_head(x_ref[0, rows, :]) * jnp.asarray(0.125, BF16)
        g = per_head(x_ref[1, rows, :])
        w, e = w_ref[b], e_ref[b]
        grad = both_heads(matmul(keys_t[:, start : start + 3 * HALF], e)) * 0.125
        out_ref[1, rows, :HALF] = grad.astype(BF16).T
        earlier = 2 * HALF - start
        for i, term in enumerate((matmul(e[earlier:], q), matmul(w[earlier:], g))):
            if b == 0:
                total_ref[i, 2 * HALF : 3 * HALF, :] = term
            else:
                total_ref[i, 2 * HALF : 3 * HALF, :] += term[:HALF]
                total_ref[i, 3 * HALF :, :] = term[HALF:]


def column_attention(q, k, v, g, bias):
    g_t = g.T.astype(F32)
    q = per_head(q) * jnp.asarray(0.125, BF16)
    g = per_head(g)
    (p,) = softmax([matmul_nt(k, q) + bias])
    w = p.astype(BF16)
    attended = both_heads(matmul(v.T, w)).astype(BF16)
    dots = head_sums(g_t * attended.astype(F32))
    e = (p * (matmul_nt(v, g) - dots)).astype(BF16)
    grad = (both_heads(matmul(k.T, e)) * 0.125).astype(BF16)
    return attended.T, grad.T, matmul(e, q).astype(BF16), matmul(w, g).astype(BF16)


def column_bias(pattern_ref):
    key, stacked = iota((ROWS, 1), 0), iota((1, 2 * ROWS), 1)
    query = stacked & (ROWS - 1)
    bits = jnp.zeros(stacked.shape, jnp.int32)
    for h in range(2):
        for b in range(4):
            code = sum(pattern_ref[h, b, j] * (1 << j) for j in range(4))
            bits = jnp.where(stacked // 32 == 4 * h + b, code, bits)
    seen = jnp.zeros((ROWS, 2 * ROWS), jnp.int32)
    for j in range(4):
        seen = jnp.where(key // 32 == j, (bits >> j) & 1, seen)
    allowed = (key <= query) & (seen > 0)
    return jnp.where(allowed, 0.0, NEG)


def reorder(source, target):
    order, size, row = {}, 1, iota((1, BLOCK), 1)
    for name in reversed(source):
        order[name] = (row // size) & (source[name] - 1)
        size *= source[name]
    place = 0
    for name in target:
        place = place * source[name] + order[name]
    return jnp.where(place == iota((BLOCK, BLOCK), 0), 1.0, 0.0).astype(BF16)


def kernel(
    q_hbm, k_hbm, v_hbm, g_hbm, row_pattern_hbm, column_pattern_hbm,
    result,
    xc, xr, kv, back, backr, total, row_w, row_e, perm, bias,
    s1a, r1a, r1b, s2a, r2a, s2b, r2b, found, s3, r3,
    row_pattern, column_pattern, pattern_sem, in_sem, ring_sem, send_sem, recv_sem, back_send_sem, back_recv_sem,
):
    me = lax.axis_index("seq")
    y, zx = me // NZX, lax.rem(me, NZX)
    place_here = {"mp": lax.axis_index("mp"), "batch": lax.axis_index("batch")}
    after = {"seq": lax.rem(me + 1, ROWS), **place_here}
    before = {"seq": lax.rem(me + ROWS - 1, ROWS), **place_here}

    zx_places = [lax.rem(zx + i, NZX) for i in range(NZX)]
    y_places = [lax.rem(y + i, NY) for i in range(NY)]

    def device(seq):
        return {"seq": seq, **place_here}

    zx_peers = [(zx_places[i], device(y * NZX + zx_places[i])) for i in ZX_ORDER]
    y_peers = [(y_places[i], device(y_places[i] * NZX + zx)) for i in Y_ORDER]

    inputs = (q_hbm, k_hbm, v_hbm, g_hbm)

    this_row = pl.ds(CW, CW)
    row_places = (xr.at[0], kv.at[0, this_row], kv.at[1, this_row], xr.at[1])

    def loads_of(part, places):
        return [
            pltpu.make_async_copy(h.at[0, :, pl.ds(part * HALF, HALF)], place, in_sem.at[part, i])
            for i, (h, place) in enumerate(zip(inputs, places))
        ]

    column_loads = loads_of(1, [xc.at[i // 2, i % 2] for i in range(PIECES)])
    row_loads = loads_of(0, row_places)
    patterns = [
        pltpu.make_async_copy(row_pattern_hbm, row_pattern, pattern_sem.at[0]),
        pltpu.make_async_copy(column_pattern_hbm, column_pattern, pattern_sem.at[1]),
    ]
    for load in column_loads:
        load.start()

    barrier = pltpu.get_barrier_semaphore()

    def greet(peer):
        pl.semaphore_signal(barrier, inc=1, device_id=peer, device_id_type=MESH)

    for _, peer in zx_peers + y_peers:
        greet(peer)
    greet(after)
    greet(before)
    for load in row_loads + patterns:
        load.start()

    def exchange(step, source, landing, over_zx):
        place = (step, 0 if over_zx else 1)
        peers, mine = (zx_peers, zx) if over_zx else (y_peers, y)
        for other, peer in peers:
            pltpu.make_async_remote_copy(
                src_ref=source(other),
                dst_ref=landing(mine),
                send_sem=send_sem.at[place],
                recv_sem=recv_sem.at[place],
                device_id=peer,
                device_id_type=MESH,
            ).start()
        pltpu.make_async_copy(source(mine), landing(mine), recv_sem.at[place]).start()

    def send(step, source, dest, over_zx):
        exchange(step, lambda j: source.at[j], lambda j: dest.at[j], over_zx)

    def arrived(step, whole, over_zx):
        pltpu.make_async_copy(whole, whole, recv_sem.at[step, 0 if over_zx else 1]).wait()

    def sent(step, dest, over_zx):
        part = dest.at[pl.ds(0, dest.shape[0] - 1)]
        pltpu.make_async_copy(part, part, send_sem.at[step, 0 if over_zx else 1]).wait()

    def last_columns(j=None):
        rows = pl.ds(HALF, HALF) if j is None else pl.ds(pl.multiple_of(HALF + j * NZX, NZX), NZX)
        return (slice(None), slice(None), rows, slice(None))

    grid_rows = {"piece": 2, "y": NY, "zx": NZX}
    by_zx = ("zx", "piece", "y")
    perm[PACK] = reorder(grid_rows, by_zx)
    for load in column_loads:
        load.wait()
    for p in range(PAIRS):
        rows = xc[p, :, :HALF, :].reshape(BLOCK, HALF)
        packed = matmul(perm[PACK], rows).astype(BF16)
        s1a[:, p] = packed.reshape(NZX, 2 * NY, HALF)
    pl.semaphore_wait(barrier, (NZX - 1) + (NY - 1) + 2)

    send(0, s1a, r1a, True)
    exchange(0, lambda j: xc.at[last_columns(j)], lambda j: r1b.at[j], False)
    for load in row_loads:
        load.wait()
    forward = pltpu.make_async_remote_copy(
        src_ref=kv.at[:, this_row],
        dst_ref=kv.at[:, pl.ds(0, CW)],
        send_sem=ring_sem.at[0],
        recv_sem=ring_sem.at[1],
        device_id=after,
        device_id_type=MESH,
    )
    forward.start()

    for t, source, target in (
        (UNPACK, {"zx": NZX, "piece": 2, "y": NY}, ("piece", "y", "zx")),
        (ZX_TO_Y, {"zx": NZX, "piece": 2, "y": NY}, ("y", "piece", "zx")),
        (Y_TO_ZX, {"y": NY, "piece": 2, "zx": NZX}, ("zx", "piece", "y")),
        (SPREAD, {"piece": 2 * PIECES, "row": PART}, ("row", "piece")),
        (GATHER, {"row": PART, "piece": 2 * PIECES}, ("piece", "row")),
    ):
        perm[t] = reorder(source, target)
    for load in patterns:
        load.wait()
    bias[...] = column_bias(column_pattern)

    def swap(dest, source, t):
        for p in range(PAIRS):
            rows = matmul(perm[t], source[:, p].reshape(BLOCK, HALF)).astype(BF16)
            dest[:, p] = rows.reshape(dest.shape[:1] + dest.shape[2:])

    arrived(0, r1a, True)
    swap(s2a, r1a, ZX_TO_Y)
    send(1, s2a, r2a, False)
    arrived(0, r1b, False)
    swap(s2b, r1b, Y_TO_ZX)
    send(1, s2b, r2b, True)

    forward.wait()
    row_attention(xr, kv, row_pattern, me, result, total, row_w, row_e)
    back[...] = total[:, :CW, :].astype(BF16)
    backward = pltpu.make_async_remote_copy(
        src_ref=back,
        dst_ref=backr,
        send_sem=ring_sem.at[2],
        recv_sem=ring_sem.at[3],
        device_id=before,
        device_id_type=MESH,
    )
    backward.start()

    arrived(1, r2a, False)
    arrived(1, r2b, True)
    first = [r2a[:, i // 2, i % 2].reshape(ROWS, HALF) for i in range(PIECES)]
    second = []
    for p in range(PAIRS):
        rows = matmul(perm[UNPACK], r2b[:, p].reshape(BLOCK, HALF)).astype(BF16)
        second += [rows[:ROWS], rows[ROWS:]]
    results = [column_attention(*pieces, bias[...]) for pieces in (first, second)]
    for c in range(2):
        for i in range(PIECES):
            found[c, i] = results[c][i]

    for k in range(ROWS // PART):
        part = pl.ds(k * PART, PART)
        rows = found[:, :, part, :].reshape(BLOCK, HALF)
        s3[part] = matmul(perm[SPREAD], rows).astype(BF16).reshape(PART, 2 * PIECES, HALF)

    for i in ALL_ORDER:
        other = y_places[i // NZX] * NZX + zx_places[i % NZX]
        pltpu.make_async_remote_copy(
            src_ref=s3.at[other],
            dst_ref=r3.at[me],
            send_sem=back_send_sem,
            recv_sem=back_recv_sem,
            device_id=device(other),
            device_id_type=MESH,
        ).start()
    pltpu.make_async_copy(s3.at[me], r3.at[me], back_recv_sem).start()

    row_gradients(xr, kv, result, total, row_w, row_e)
    backward.wait()
    for i in range(2):
        result[2 + i, :, :HALF] = (total[i, CW:, :] + backr[i].astype(F32)).astype(BF16)

    pltpu.make_async_copy(r3, r3, back_recv_sem).wait()
    for k in range(ROWS // PART):
        part = pl.ds(k * PART, PART)
        rows = matmul(perm[GATHER], r3[part].reshape(BLOCK, HALF)).astype(BF16)
        for c in range(2):
            for i in range(PIECES):
                start = (c * PIECES + i) * PART
                place = pl.ds(c * HALF + k * PART, PART)
                result[i, place, HALF:] = rows[start : start + PART]

    for step, (over_zx, over_y) in enumerate(((r1a, r1b), (r2b, r2a))):
        sent(step, over_zx, True)
        sent(step, over_y, False)
    others = s3.at[pl.ds(0, ROWS - 1)]
    pltpu.make_async_copy(others, others, back_send_sem).wait()


def write_out(result, o0, o1, o2, o3, sem):
    copies = [
        pltpu.make_async_copy(result.at[i], o.at[0], sem.at[i])
        for i, o in enumerate((o0, o1, o2, o3))
    ]
    for copy in copies:
        copy.start()
    for copy in copies:
        copy.wait()


def per_device(queries, key_vectors, value_vectors, cotangent, row_pattern, column_pattern):
    by_zx = pltpu.VMEM((NZX, PAIRS, 2 * NY, HALF), BF16)
    by_y = pltpu.VMEM((NY, PAIRS, 2, NZX, HALF), BF16)
    weights = pltpu.VMEM((2, 3 * HALF, 2 * HALF), BF16)
    direct = pltpu.VMEM((ROWS, 2 * PIECES, HALF), BF16)
    vmem = pl.BlockSpec(memory_space=pltpu.VMEM)
    hbm = pl.BlockSpec(memory_space=pltpu.HBM)
    halves = pltpu.VMEM((PAIRS, 2, CW, HALF), BF16)
    pair = pltpu.VMEM((2, CW, HALF), BF16)
    in_hbm = [
        pltpu.with_memory_space_constraint(x, pltpu.HBM)
        for x in (queries, key_vectors, value_vectors, cotangent, row_pattern, column_pattern)
    ]
    result = pl.pallas_call(
        kernel,
        out_shape=pltpu.VMEM((PIECES, CW, 2 * HALF), BF16),
        in_specs=[hbm] * 6,
        out_specs=vmem,
        scratch_shapes=[
            halves, pair,
            pltpu.VMEM((2, 2 * CW, HALF), BF16),
            pair, pair,
            pltpu.VMEM((2, 2 * CW, HALF), F32),
            weights, weights,
            pltpu.VMEM((6, BLOCK, BLOCK), BF16),
            pltpu.VMEM((ROWS, 2 * ROWS), F32),
            by_zx, by_zx, by_y,
            by_y, by_y, by_zx, by_zx,
            pltpu.VMEM((2, PIECES, ROWS, HALF), BF16),
            direct, direct,
            pltpu.SMEM(row_pattern.shape, jnp.int32),
            pltpu.SMEM(column_pattern.shape, jnp.int32),
            pltpu.SemaphoreType.DMA((2,)),
            pltpu.SemaphoreType.DMA((2, PIECES)),
            pltpu.SemaphoreType.DMA((4,)),
            pltpu.SemaphoreType.DMA((2, 2)),
            pltpu.SemaphoreType.DMA((2, 2)),
            pltpu.SemaphoreType.DMA,
            pltpu.SemaphoreType.DMA,
        ],
        compiler_params=pltpu.CompilerParams(
            collective_id=0, has_side_effects=True, vmem_limit_bytes=40 * 1024 * 1024
        ),
        cost_estimate=pl.CostEstimate(
            flops=800_000_000, bytes_accessed=1_050_000, transcendentals=200_000
        ),
        name="grid_attention",
    )(*in_hbm)
    return pl.pallas_call(
        write_out,
        out_shape=[jax.ShapeDtypeStruct(queries.shape, BF16)] * 4,
        in_specs=[vmem],
        out_specs=[hbm] * 4,
        scratch_shapes=[pltpu.SemaphoreType.DMA((PIECES,))],
        cost_estimate=pl.CostEstimate(flops=0, bytes_accessed=1_050_000, transcendentals=0),
        compiler_params=pltpu.CompilerParams(vmem_limit_bytes=8 * 1024 * 1024),
        name="write_out",
    )(pltpu.with_memory_space_constraint(result, pltpu.VMEM))


def solution(mesh):
    rows = P(("batch", "seq"), None, "mp")
    heads = P("mp", None, None)
    return jax.shard_map(
        per_device,
        mesh=mesh,
        in_specs=(rows, rows, rows, rows, heads, heads),
        out_specs=(rows, rows, rows, rows),
        check_vma=False,
    )
```

```python
import jax
import jax.numpy as jnp
from jax import lax
from jax.experimental import pallas as pl
from jax.experimental.pallas import tpu as pltpu
from jax.sharding import PartitionSpec as P

MESH = pl.DeviceIdType.MESH
F32 = jnp.float32
BF16 = jnp.bfloat16
NEG = -1e30

NY = 8
NZX = 16
ROWS = NY * NZX
CW = 256
HALF = 128
DH = 64
PIECES = 4
PAIRS = PIECES // 2
BLOCK = 2 * ROWS
PART = 32
PACK, UNPACK, ZX_TO_Y, Y_TO_ZX, SPREAD, GATHER = range(6)


def hops(offset, size):
    return min(offset, size - offset)


def far_first(count, distance):
    return sorted(range(1, count), key=lambda i: (-distance(i), i * 37 % count))


Y_ORDER = far_first(NY, lambda i: hops(i, NY))
ZX_ORDER = far_first(NZX, lambda i: hops(i // 2, NZX // 2) + i % 2)
ALL_ORDER = far_first(ROWS, lambda i: hops(i // NZX, NY) + hops(i % NZX // 2, NZX // 2) + i % 2)


def iota(shape, axis):
    return lax.broadcasted_iota(jnp.int32, shape, axis)


def matmul(a, b):
    return lax.dot_general(a, b, (((1,), (0,)), ((), ())), preferred_element_type=F32)


def matmul_nt(a, b):
    return lax.dot_general(a, b, (((1,), (1,)), ((), ())), preferred_element_type=F32)


def per_head(x):
    first = iota(x.shape, 1) < DH
    zero = jnp.zeros_like(x)
    return jnp.concatenate([jnp.where(first, x, zero), jnp.where(first, zero, x)], axis=0)


def both_heads(wide):
    first = iota((HALF, HALF), 0) < DH
    return jnp.where(first, wide[:, :HALF], wide[:, HALF:])


def head_sums(x):
    return jnp.concatenate(
        [x[:DH].sum(0, keepdims=True), x[DH:].sum(0, keepdims=True)], axis=1
    )


def softmax(blocks):
    highest = blocks[0].max(axis=0, keepdims=True)
    for block in blocks[1:]:
        highest = jnp.maximum(highest, block.max(axis=0, keepdims=True))
    powers = [jnp.exp(block - highest) for block in blocks]
    total = powers[0].sum(axis=0, keepdims=True)
    for power in powers[1:]:
        total = total + power.sum(axis=0, keepdims=True)
    share = 1.0 / total
    return [power * share for power in powers]


def row_attention(x_ref, kv_ref, pattern_ref, row, out_ref, total_ref, w_ref, e_ref):
    shape = (HALF, 2 * HALF)
    same = iota(shape, 0) <= (iota((1, 2 * HALF), 1) & (HALF - 1))
    has_earlier = jnp.broadcast_to(row >= 1, shape)
    values_t = kv_ref[1].T
    for b in range(2):
        start = b * HALF
        rows, window = pl.ds(start, HALF), pl.ds(start, 3 * HALF)
        first, second = (pattern_ref[h, b, 1 - b] * jnp.minimum(row + b, 1) for h in range(2))
        whole_open = jnp.where(iota((1, 2 * HALF), 1) < HALF, first, second) > 0
        q = per_head(x_ref[0, rows, :]) * jnp.asarray(0.125, BF16)
        g = per_head(x_ref[1, rows, :])
        keys, values = kv_ref[0, window, :], kv_ref[1, window, :]
        scores, weight_grads = matmul_nt(keys, q), matmul_nt(values, g)

        def chosen(x, earlier_else):
            earlier, whole, this = (x[i * HALF : (i + 1) * HALF] for i in range(3))
            return jnp.where(same, this, earlier_else(earlier)), whole

        diag, whole = chosen(scores, lambda x: jnp.where(has_earlier, x, NEG))
        p_diag, p_whole = softmax([diag, jnp.where(whole_open, whole, NEG)])

        def spread(at_diag, at_whole):
            at_diag, at_whole = at_diag.astype(BF16), at_whole.astype(BF16)
            zero = jnp.zeros_like(at_diag)
            return jnp.concatenate(
                [jnp.where(same, zero, at_diag), at_whole, jnp.where(same, at_diag, zero)], axis=0
            )

        w = spread(p_diag, p_whole)
        attended = both_heads(matmul(values_t[:, start : start + 3 * HALF], w)).astype(BF16)
        out_ref[0, rows, :HALF] = attended.T
        dots = head_sums(x_ref[1, rows, :].T.astype(F32) * attended.astype(F32))
        d_diag, d_whole = chosen(weight_grads, lambda x: x)
        e = spread(p_diag * (d_diag - dots), p_whole * (d_whole - dots))
        w_ref[b], e_ref[b] = w, e
        earlier = 2 * HALF - start
        for i, term in enumerate((matmul(e[:earlier], q), matmul(w[:earlier], g))):
            if b == 0:
                total_ref[i, : 2 * HALF, :] = term
            else:
                total_ref[i, HALF : 2 * HALF, :] += term


def row_gradients(x_ref, kv_ref, out_ref, total_ref, w_ref, e_ref):
    keys_t = kv_ref[0].T
    for b in range(2):
        start = b * HALF
        rows = pl.ds(start, HALF)
        q = per_head(x_ref[0, rows, :]) * jnp.asarray(0.125, BF16)
        g = per_head(x_ref[1, rows, :])
        w, e = w_ref[b], e_ref[b]
        grad = both_heads(matmul(keys_t[:, start : start + 3 * HALF], e)) * 0.125
        out_ref[1, rows, :HALF] = grad.astype(BF16).T
        earlier = 2 * HALF - start
        for i, term in enumerate((matmul(e[earlier:], q), matmul(w[earlier:], g))):
            if b == 0:
                total_ref[i, 2 * HALF : 3 * HALF, :] = term
            else:
                total_ref[i, 2 * HALF : 3 * HALF, :] += term[:HALF]
                total_ref[i, 3 * HALF :, :] = term[HALF:]


def column_attention(q, k, v, g, bias):
    g_t = g.T.astype(F32)
    q = per_head(q) * jnp.asarray(0.125, BF16)
    g = per_head(g)
    (p,) = softmax([matmul_nt(k, q) + bias])
    w = p.astype(BF16)
    attended = both_heads(matmul(v.T, w)).astype(BF16)
    dots = head_sums(g_t * attended.astype(F32))
    e = (p * (matmul_nt(v, g) - dots)).astype(BF16)
    grad = (both_heads(matmul(k.T, e)) * 0.125).astype(BF16)
    return attended.T, grad.T, matmul(e, q).astype(BF16), matmul(w, g).astype(BF16)


def column_bias(pattern_ref):
    key, stacked = iota((ROWS, 1), 0), iota((1, 2 * ROWS), 1)
    query = stacked & (ROWS - 1)
    bits = jnp.zeros(stacked.shape, jnp.int32)
    for h in range(2):
        for b in range(4):
            code = sum(pattern_ref[h, b, j] * (1 << j) for j in range(4))
            bits = jnp.where(stacked // 32 == 4 * h + b, code, bits)
    seen = jnp.zeros((ROWS, 2 * ROWS), jnp.int32)
    for j in range(4):
        seen = jnp.where(key // 32 == j, (bits >> j) & 1, seen)
    allowed = (key <= query) & (seen > 0)
    return jnp.where(allowed, 0.0, NEG)


def reorder(source, target):
    order, size, row = {}, 1, iota((1, BLOCK), 1)
    for name in reversed(source):
        order[name] = (row // size) & (source[name] - 1)
        size *= source[name]
    place = 0
    for name in target:
        place = place * source[name] + order[name]
    return jnp.where(place == iota((BLOCK, BLOCK), 0), 1.0, 0.0).astype(BF16)


def kernel(
    q_hbm, k_hbm, v_hbm, g_hbm, row_pattern_hbm, column_pattern_hbm,
    result,
    xc, xr, kv, back, backr, total, row_w, row_e, perm, bias,
    s1a, r1a, r1b, s2a, r2a, s2b, r2b, found, s3, r3,
    row_pattern, column_pattern, pattern_sem, in_sem, ring_sem, send_sem, recv_sem, back_send_sem, back_recv_sem,
):
    me = lax.axis_index("seq")
    y, zx = me // NZX, lax.rem(me, NZX)
    place_here = {"mp": lax.axis_index("mp"), "batch": lax.axis_index("batch")}
    after = {"seq": lax.rem(me + 1, ROWS), **place_here}
    before = {"seq": lax.rem(me + ROWS - 1, ROWS), **place_here}

    zx_places = [lax.rem(zx + i, NZX) for i in range(NZX)]
    y_places = [lax.rem(y + i, NY) for i in range(NY)]

    def device(seq):
        return {"seq": seq, **place_here}

    zx_peers = [(zx_places[i], device(y * NZX + zx_places[i])) for i in ZX_ORDER]
    y_peers = [(y_places[i], device(y_places[i] * NZX + zx)) for i in Y_ORDER]

    inputs = (q_hbm, k_hbm, v_hbm, g_hbm)

    this_row = pl.ds(CW, CW)
    row_places = (xr.at[0], kv.at[0, this_row], kv.at[1, this_row], xr.at[1])

    def loads_of(part, places):
        return [
            pltpu.make_async_copy(h.at[0, :, pl.ds(part * HALF, HALF)], place, in_sem.at[part, i])
            for i, (h, place) in enumerate(zip(inputs, places))
        ]

    column_loads = loads_of(1, [xc.at[i // 2, i % 2] for i in range(PIECES)])
    row_loads = loads_of(0, row_places)
    patterns = [
        pltpu.make_async_copy(row_pattern_hbm, row_pattern, pattern_sem.at[0]),
        pltpu.make_async_copy(column_pattern_hbm, column_pattern, pattern_sem.at[1]),
    ]
    for load in column_loads:
        load.start()

    barrier = pltpu.get_barrier_semaphore()

    def greet(peer):
        pl.semaphore_signal(barrier, inc=1, device_id=peer, device_id_type=MESH)

    for _, peer in zx_peers + y_peers:
        greet(peer)
    greet(after)
    greet(before)
    for load in row_loads + patterns:
        load.start()

    def exchange(step, source, landing, over_zx):
        place = (step, 0 if over_zx else 1)
        peers, mine = (zx_peers, zx) if over_zx else (y_peers, y)
        for other, peer in peers:
            pltpu.make_async_remote_copy(
                src_ref=source(other),
                dst_ref=landing(mine),
                send_sem=send_sem.at[place],
                recv_sem=recv_sem.at[place],
                device_id=peer,
                device_id_type=MESH,
            ).start()
        pltpu.make_async_copy(source(mine), landing(mine), recv_sem.at[place]).start()

    def send(step, source, dest, over_zx):
        exchange(step, lambda j: source.at[j], lambda j: dest.at[j], over_zx)

    def arrived(step, whole, over_zx):
        pltpu.make_async_copy(whole, whole, recv_sem.at[step, 0 if over_zx else 1]).wait()

    def sent(step, dest, over_zx):
        part = dest.at[pl.ds(0, dest.shape[0] - 1)]
        pltpu.make_async_copy(part, part, send_sem.at[step, 0 if over_zx else 1]).wait()

    def last_columns(j=None):
        rows = pl.ds(HALF, HALF) if j is None else pl.ds(pl.multiple_of(HALF + j * NZX, NZX), NZX)
        return (slice(None), slice(None), rows, slice(None))

    grid_rows = {"piece": 2, "y": NY, "zx": NZX}
    by_zx = ("zx", "piece", "y")
    perm[PACK] = reorder(grid_rows, by_zx)
    for load in column_loads:
        load.wait()
    for p in range(PAIRS):
        rows = xc[p, :, :HALF, :].reshape(BLOCK, HALF)
        packed = matmul(perm[PACK], rows).astype(BF16)
        s1a[:, p] = packed.reshape(NZX, 2 * NY, HALF)
    pl.semaphore_wait(barrier, (NZX - 1) + (NY - 1) + 2)

    send(0, s1a, r1a, True)
    exchange(0, lambda j: xc.at[last_columns(j)], lambda j: r1b.at[j], False)
    for load in row_loads:
        load.wait()
    forward = pltpu.make_async_remote_copy(
        src_ref=kv.at[:, this_row],
        dst_ref=kv.at[:, pl.ds(0, CW)],
        send_sem=ring_sem.at[0],
        recv_sem=ring_sem.at[1],
        device_id=after,
        device_id_type=MESH,
    )
    forward.start()

    for t, source, target in (
        (UNPACK, {"zx": NZX, "piece": 2, "y": NY}, ("piece", "y", "zx")),
        (ZX_TO_Y, {"zx": NZX, "piece": 2, "y": NY}, ("y", "piece", "zx")),
        (Y_TO_ZX, {"y": NY, "piece": 2, "zx": NZX}, ("zx", "piece", "y")),
        (SPREAD, {"piece": 2 * PIECES, "row": PART}, ("row", "piece")),
        (GATHER, {"row": PART, "piece": 2 * PIECES}, ("piece", "row")),
    ):
        perm[t] = reorder(source, target)
    for load in patterns:
        load.wait()
    bias[...] = column_bias(column_pattern)

    def swap(dest, source, t):
        for p in range(PAIRS):
            rows = matmul(perm[t], source[:, p].reshape(BLOCK, HALF)).astype(BF16)
            dest[:, p] = rows.reshape(dest.shape[:1] + dest.shape[2:])

    arrived(0, r1a, True)
    arrived(0, r1b, False)
    swap(s2a, r1a, ZX_TO_Y)
    swap(s2b, r1b, Y_TO_ZX)
    send(1, s2a, r2a, False)
    send(1, s2b, r2b, True)

    forward.wait()
    row_attention(xr, kv, row_pattern, me, result, total, row_w, row_e)
    back[...] = total[:, :CW, :].astype(BF16)
    backward = pltpu.make_async_remote_copy(
        src_ref=back,
        dst_ref=backr,
        send_sem=ring_sem.at[2],
        recv_sem=ring_sem.at[3],
        device_id=before,
        device_id_type=MESH,
    )
    backward.start()

    arrived(1, r2a, False)
    pieces = [r2a[:, i // 2, i % 2].reshape(ROWS, HALF) for i in range(PIECES)]
    for i, found_here in enumerate(column_attention(*pieces, bias[...])):
        found[0, i] = found_here
    arrived(1, r2b, True)
    pieces = []
    for p in range(PAIRS):
        rows = matmul(perm[UNPACK], r2b[:, p].reshape(BLOCK, HALF)).astype(BF16)
        pieces += [rows[:ROWS], rows[ROWS:]]
    for i, found_here in enumerate(column_attention(*pieces, bias[...])):
        found[1, i] = found_here

    for k in range(ROWS // PART):
        part = pl.ds(k * PART, PART)
        rows = found[:, :, part, :].reshape(BLOCK, HALF)
        s3[part] = matmul(perm[SPREAD], rows).astype(BF16).reshape(PART, 2 * PIECES, HALF)

    for i in ALL_ORDER:
        other = y_places[i // NZX] * NZX + zx_places[i % NZX]
        pltpu.make_async_remote_copy(
            src_ref=s3.at[other],
            dst_ref=r3.at[me],
            send_sem=back_send_sem,
            recv_sem=back_recv_sem,
            device_id=device(other),
            device_id_type=MESH,
        ).start()
    pltpu.make_async_copy(s3.at[me], r3.at[me], back_recv_sem).start()

    row_gradients(xr, kv, result, total, row_w, row_e)
    backward.wait()
    for i in range(2):
        result[2 + i, :, :HALF] = (total[i, CW:, :] + backr[i].astype(F32)).astype(BF16)

    pltpu.make_async_copy(r3, r3, back_recv_sem).wait()
    for k in range(ROWS // PART):
        part = pl.ds(k * PART, PART)
        rows = matmul(perm[GATHER], r3[part].reshape(BLOCK, HALF)).astype(BF16)
        for c in range(2):
            for i in range(PIECES):
                start = (c * PIECES + i) * PART
                place = pl.ds(c * HALF + k * PART, PART)
                result[i, place, HALF:] = rows[start : start + PART]

    for step, (over_zx, over_y) in enumerate(((r1a, r1b), (r2b, r2a))):
        sent(step, over_zx, True)
        sent(step, over_y, False)
    others = s3.at[pl.ds(0, ROWS - 1)]
    pltpu.make_async_copy(others, others, back_send_sem).wait()


def write_out(result, o0, o1, o2, o3, sem):
    copies = [
        pltpu.make_async_copy(result.at[i], o.at[0], sem.at[i])
        for i, o in enumerate((o0, o1, o2, o3))
    ]
    for copy in copies:
        copy.start()
    for copy in copies:
        copy.wait()


def per_device(queries, key_vectors, value_vectors, cotangent, row_pattern, column_pattern):
    by_zx = pltpu.VMEM((NZX, PAIRS, 2 * NY, HALF), BF16)
    by_y = pltpu.VMEM((NY, PAIRS, 2, NZX, HALF), BF16)
    weights = pltpu.VMEM((2, 3 * HALF, 2 * HALF), BF16)
    direct = pltpu.VMEM((ROWS, 2 * PIECES, HALF), BF16)
    vmem = pl.BlockSpec(memory_space=pltpu.VMEM)
    hbm = pl.BlockSpec(memory_space=pltpu.HBM)
    halves = pltpu.VMEM((PAIRS, 2, CW, HALF), BF16)
    pair = pltpu.VMEM((2, CW, HALF), BF16)
    in_hbm = [
        pltpu.with_memory_space_constraint(x, pltpu.HBM)
        for x in (queries, key_vectors, value_vectors, cotangent, row_pattern, column_pattern)
    ]
    result = pl.pallas_call(
        kernel,
        out_shape=pltpu.VMEM((PIECES, CW, 2 * HALF), BF16),
        in_specs=[hbm] * 6,
        out_specs=vmem,
        scratch_shapes=[
            halves, pair,
            pltpu.VMEM((2, 2 * CW, HALF), BF16),
            pair, pair,
            pltpu.VMEM((2, 2 * CW, HALF), F32),
            weights, weights,
            pltpu.VMEM((6, BLOCK, BLOCK), BF16),
            pltpu.VMEM((ROWS, 2 * ROWS), F32),
            by_zx, by_zx, by_y,
            by_y, by_y, by_zx, by_zx,
            pltpu.VMEM((2, PIECES, ROWS, HALF), BF16),
            direct, direct,
            pltpu.SMEM(row_pattern.shape, jnp.int32),
            pltpu.SMEM(column_pattern.shape, jnp.int32),
            pltpu.SemaphoreType.DMA((2,)),
            pltpu.SemaphoreType.DMA((2, PIECES)),
            pltpu.SemaphoreType.DMA((4,)),
            pltpu.SemaphoreType.DMA((2, 2)),
            pltpu.SemaphoreType.DMA((2, 2)),
            pltpu.SemaphoreType.DMA,
            pltpu.SemaphoreType.DMA,
        ],
        compiler_params=pltpu.CompilerParams(
            collective_id=0, has_side_effects=True, vmem_limit_bytes=40 * 1024 * 1024
        ),
        cost_estimate=pl.CostEstimate(
            flops=800_000_000, bytes_accessed=1_050_000, transcendentals=200_000
        ),
        name="grid_attention",
    )(*in_hbm)
    return pl.pallas_call(
        write_out,
        out_shape=[jax.ShapeDtypeStruct(queries.shape, BF16)] * 4,
        in_specs=[vmem],
        out_specs=[hbm] * 4,
        scratch_shapes=[pltpu.SemaphoreType.DMA((PIECES,))],
        cost_estimate=pl.CostEstimate(flops=0, bytes_accessed=1_050_000, transcendentals=0),
        compiler_params=pltpu.CompilerParams(vmem_limit_bytes=8 * 1024 * 1024),
        name="write_out",
    )(pltpu.with_memory_space_constraint(result, pltpu.VMEM))


def solution(mesh):
    rows = P(("batch", "seq"), None, "mp")
    heads = P("mp", None, None)
    return jax.shard_map(
        per_device,
        mesh=mesh,
        in_specs=(rows, rows, rows, rows, heads, heads),
        out_specs=(rows, rows, rows, rows),
        check_vma=False,
    )
```

```python
import jax
import jax.numpy as jnp
from jax import lax
from jax.experimental import pallas as pl
from jax.experimental.pallas import tpu as pltpu
from jax.sharding import PartitionSpec as P

MESH = pl.DeviceIdType.MESH
F32 = jnp.float32
BF16 = jnp.bfloat16
NEG = -1e30

NY = 8
NZX = 16
ROWS = NY * NZX
CW = 256
HALF = 128
DH = 64
PIECES = 4
PAIRS = PIECES // 2
BLOCK = 2 * ROWS
PART = 32
PACK, UNPACK, ZX_TO_Y, Y_TO_ZX, SPREAD, GATHER = range(6)


def hops(offset, size):
    return min(offset, size - offset)


def far_first(count, distance):
    return sorted(range(1, count), key=lambda i: (-distance(i), i * 37 % count))


Y_ORDER = far_first(NY, lambda i: hops(i, NY))
ZX_ORDER = far_first(NZX, lambda i: hops(i // 2, NZX // 2) + i % 2)
ALL_ORDER = far_first(ROWS, lambda i: hops(i // NZX, NY) + hops(i % NZX // 2, NZX // 2) + i % 2)


def iota(shape, axis):
    return lax.broadcasted_iota(jnp.int32, shape, axis)


def matmul(a, b):
    return lax.dot_general(a, b, (((1,), (0,)), ((), ())), preferred_element_type=F32)


def matmul_nt(a, b):
    return lax.dot_general(a, b, (((1,), (1,)), ((), ())), preferred_element_type=F32)


def per_head(x):
    first = iota(x.shape, 1) < DH
    zero = jnp.zeros_like(x)
    return jnp.concatenate([jnp.where(first, x, zero), jnp.where(first, zero, x)], axis=0)


def both_heads(wide):
    first = iota((HALF, HALF), 0) < DH
    return jnp.where(first, wide[:, :HALF], wide[:, HALF:])


def head_sums(x):
    return jnp.concatenate(
        [x[:DH].sum(0, keepdims=True), x[DH:].sum(0, keepdims=True)], axis=1
    )


def softmax(blocks):
    highest = blocks[0].max(axis=0, keepdims=True)
    for block in blocks[1:]:
        highest = jnp.maximum(highest, block.max(axis=0, keepdims=True))
    powers = [jnp.exp(block - highest) for block in blocks]
    total = powers[0].sum(axis=0, keepdims=True)
    for power in powers[1:]:
        total = total + power.sum(axis=0, keepdims=True)
    share = 1.0 / total
    return [power * share for power in powers]


def row_attention(x_ref, kv_ref, pattern_ref, row, out_ref, total_ref, w_ref, e_ref):
    shape = (HALF, 2 * HALF)
    same = iota(shape, 0) <= (iota((1, 2 * HALF), 1) & (HALF - 1))
    has_earlier = jnp.broadcast_to(row >= 1, shape)
    values_t = kv_ref[1].T
    for b in range(2):
        start = b * HALF
        rows, window = pl.ds(start, HALF), pl.ds(start, 3 * HALF)
        first, second = (pattern_ref[h, b, 1 - b] * jnp.minimum(row + b, 1) for h in range(2))
        whole_open = jnp.where(iota((1, 2 * HALF), 1) < HALF, first, second) > 0
        q = per_head(x_ref[0, rows, :]) * jnp.asarray(0.125, BF16)
        g = per_head(x_ref[1, rows, :])
        keys, values = kv_ref[0, window, :], kv_ref[1, window, :]
        scores, weight_grads = matmul_nt(keys, q), matmul_nt(values, g)

        def chosen(x, earlier_else):
            earlier, whole, this = (x[i * HALF : (i + 1) * HALF] for i in range(3))
            return jnp.where(same, this, earlier_else(earlier)), whole

        diag, whole = chosen(scores, lambda x: jnp.where(has_earlier, x, NEG))
        p_diag, p_whole = softmax([diag, jnp.where(whole_open, whole, NEG)])

        def spread(at_diag, at_whole):
            at_diag, at_whole = at_diag.astype(BF16), at_whole.astype(BF16)
            zero = jnp.zeros_like(at_diag)
            return jnp.concatenate(
                [jnp.where(same, zero, at_diag), at_whole, jnp.where(same, at_diag, zero)], axis=0
            )

        w = spread(p_diag, p_whole)
        attended = both_heads(matmul(values_t[:, start : start + 3 * HALF], w)).astype(BF16)
        out_ref[0, rows, :HALF] = attended.T
        dots = head_sums(x_ref[1, rows, :].T.astype(F32) * attended.astype(F32))
        d_diag, d_whole = chosen(weight_grads, lambda x: x)
        e = spread(p_diag * (d_diag - dots), p_whole * (d_whole - dots))
        w_ref[b], e_ref[b] = w, e
        earlier = 2 * HALF - start
        for i, term in enumerate((matmul(e[:earlier], q), matmul(w[:earlier], g))):
            if b == 0:
                total_ref[i, : 2 * HALF, :] = term
            else:
                total_ref[i, HALF : 2 * HALF, :] += term


def row_gradients(x_ref, kv_ref, out_ref, total_ref, w_ref, e_ref):
    keys_t = kv_ref[0].T
    for b in range(2):
        start = b * HALF
        rows = pl.ds(start, HALF)
        q = per_head(x_ref[0, rows, :]) * jnp.asarray(0.125, BF16)
        g = per_head(x_ref[1, rows, :])
        w, e = w_ref[b], e_ref[b]
        grad = both_heads(matmul(keys_t[:, start : start + 3 * HALF], e)) * 0.125
        out_ref[1, rows, :HALF] = grad.astype(BF16).T
        earlier = 2 * HALF - start
        for i, term in enumerate((matmul(e[earlier:], q), matmul(w[earlier:], g))):
            if b == 0:
                total_ref[i, 2 * HALF : 3 * HALF, :] = term
            else:
                total_ref[i, 2 * HALF : 3 * HALF, :] += term[:HALF]
                total_ref[i, 3 * HALF :, :] = term[HALF:]


def column_attention(q, k, v, g, bias):
    g_t = g.T.astype(F32)
    q = per_head(q) * jnp.asarray(0.125, BF16)
    g = per_head(g)
    (p,) = softmax([matmul_nt(k, q) + bias])
    w = p.astype(BF16)
    attended = both_heads(matmul(v.T, w)).astype(BF16)
    dots = head_sums(g_t * attended.astype(F32))
    e = (p * (matmul_nt(v, g) - dots)).astype(BF16)
    grad = (both_heads(matmul(k.T, e)) * 0.125).astype(BF16)
    return attended.T, grad.T, matmul(e, q).astype(BF16), matmul(w, g).astype(BF16)


def column_bias(pattern_ref):
    key, stacked = iota((ROWS, 1), 0), iota((1, 2 * ROWS), 1)
    query = stacked & (ROWS - 1)
    bits = jnp.zeros(stacked.shape, jnp.int32)
    for h in range(2):
        for b in range(4):
            code = sum(pattern_ref[h, b, j] * (1 << j) for j in range(4))
            bits = jnp.where(stacked // 32 == 4 * h + b, code, bits)
    seen = jnp.zeros((ROWS, 2 * ROWS), jnp.int32)
    for j in range(4):
        seen = jnp.where(key // 32 == j, (bits >> j) & 1, seen)
    allowed = (key <= query) & (seen > 0)
    return jnp.where(allowed, 0.0, NEG)


def reorder(source, target):
    order, size, row = {}, 1, iota((1, BLOCK), 1)
    for name in reversed(source):
        order[name] = (row // size) & (source[name] - 1)
        size *= source[name]
    place = 0
    for name in target:
        place = place * source[name] + order[name]
    return jnp.where(place == iota((BLOCK, BLOCK), 0), 1.0, 0.0).astype(BF16)


def kernel(
    q_hbm, k_hbm, v_hbm, g_hbm, row_pattern_hbm, column_pattern_hbm,
    result,
    xc, xr, kv, back, backr, total, row_w, row_e, perm, bias,
    s1a, r1a, r1b, s2a, r2a, s2b, r2b, found, s3, r3,
    row_pattern, column_pattern, pattern_sem, in_sem, ring_sem, send_sem, recv_sem, back_send_sem, back_recv_sem,
):
    me = lax.axis_index("seq")
    y, zx = me // NZX, lax.rem(me, NZX)
    place_here = {"mp": lax.axis_index("mp"), "batch": lax.axis_index("batch")}
    after = {"seq": lax.rem(me + 1, ROWS), **place_here}
    before = {"seq": lax.rem(me + ROWS - 1, ROWS), **place_here}

    zx_places = [lax.rem(zx + i, NZX) for i in range(NZX)]
    y_places = [lax.rem(y + i, NY) for i in range(NY)]

    def device(seq):
        return {"seq": seq, **place_here}

    zx_peers = [(zx_places[i], device(y * NZX + zx_places[i])) for i in ZX_ORDER]
    y_peers = [(y_places[i], device(y_places[i] * NZX + zx)) for i in Y_ORDER]

    inputs = (q_hbm, k_hbm, v_hbm, g_hbm)

    this_row = pl.ds(CW, CW)
    row_places = (xr.at[0], kv.at[0, this_row], kv.at[1, this_row], xr.at[1])

    def loads_of(part, places):
        return [
            pltpu.make_async_copy(h.at[0, :, pl.ds(part * HALF, HALF)], place, in_sem.at[part, i])
            for i, (h, place) in enumerate(zip(inputs, places))
        ]

    column_loads = loads_of(1, [xc.at[i // 2, i % 2] for i in range(PIECES)])
    row_loads = loads_of(0, row_places)
    patterns = [
        pltpu.make_async_copy(row_pattern_hbm, row_pattern, pattern_sem.at[0]),
        pltpu.make_async_copy(column_pattern_hbm, column_pattern, pattern_sem.at[1]),
    ]
    for load in column_loads:
        load.start()

    barrier = pltpu.get_barrier_semaphore()

    def greet(peer):
        pl.semaphore_signal(barrier, inc=1, device_id=peer, device_id_type=MESH)

    for _, peer in zx_peers + y_peers:
        greet(peer)
    greet(after)
    greet(before)
    for load in row_loads + patterns:
        load.start()

    def exchange(step, source, landing, over_zx):
        place = (step, 0 if over_zx else 1)
        peers, mine = (zx_peers, zx) if over_zx else (y_peers, y)
        for other, peer in peers:
            pltpu.make_async_remote_copy(
                src_ref=source(other),
                dst_ref=landing(mine),
                send_sem=send_sem.at[place],
                recv_sem=recv_sem.at[place],
                device_id=peer,
                device_id_type=MESH,
            ).start()
        pltpu.make_async_copy(source(mine), landing(mine), recv_sem.at[place]).start()

    def send(step, source, dest, over_zx):
        exchange(step, lambda j: source.at[j], lambda j: dest.at[j], over_zx)

    def arrived(step, whole, over_zx):
        pltpu.make_async_copy(whole, whole, recv_sem.at[step, 0 if over_zx else 1]).wait()

    def sent(step, dest, over_zx):
        part = dest.at[pl.ds(0, dest.shape[0] - 1)]
        pltpu.make_async_copy(part, part, send_sem.at[step, 0 if over_zx else 1]).wait()

    def last_columns(j=None):
        rows = pl.ds(HALF, HALF) if j is None else pl.ds(pl.multiple_of(HALF + j * NZX, NZX), NZX)
        return (slice(None), slice(None), rows, slice(None))

    grid_rows = {"piece": 2, "y": NY, "zx": NZX}
    by_zx = ("zx", "piece", "y")
    perm[PACK] = reorder(grid_rows, by_zx)
    for load in column_loads:
        load.wait()
    for p in range(PAIRS):
        rows = xc[p, :, :HALF, :].reshape(BLOCK, HALF)
        packed = matmul(perm[PACK], rows).astype(BF16)
        s1a[:, p] = packed.reshape(NZX, 2 * NY, HALF)
    pl.semaphore_wait(barrier, (NZX - 1) + (NY - 1) + 2)

    send(0, s1a, r1a, True)
    exchange(0, lambda j: xc.at[last_columns(j)], lambda j: r1b.at[j], False)
    for load in row_loads:
        load.wait()
    forward = pltpu.make_async_remote_copy(
        src_ref=kv.at[:, this_row],
        dst_ref=kv.at[:, pl.ds(0, CW)],
        send_sem=ring_sem.at[0],
        recv_sem=ring_sem.at[1],
        device_id=after,
        device_id_type=MESH,
    )
    forward.start()

    for t, source, target in (
        (UNPACK, {"zx": NZX, "piece": 2, "y": NY}, ("piece", "y", "zx")),
        (ZX_TO_Y, {"zx": NZX, "piece": 2, "y": NY}, ("y", "piece", "zx")),
        (Y_TO_ZX, {"y": NY, "piece": 2, "zx": NZX}, ("zx", "piece", "y")),
        (SPREAD, {"piece": 2 * PIECES, "row": PART}, ("row", "piece")),
        (GATHER, {"row": PART, "piece": 2 * PIECES}, ("piece", "row")),
    ):
        perm[t] = reorder(source, target)
    for load in patterns:
        load.wait()
    bias[...] = column_bias(column_pattern)

    def swap(dest, source, t):
        for p in range(PAIRS):
            rows = matmul(perm[t], source[:, p].reshape(BLOCK, HALF)).astype(BF16)
            dest[:, p] = rows.reshape(dest.shape[:1] + dest.shape[2:])

    arrived(0, r1a, True)
    swap(s2a, r1a, ZX_TO_Y)
    send(1, s2a, r2a, False)
    arrived(0, r1b, False)
    swap(s2b, r1b, Y_TO_ZX)
    send(1, s2b, r2b, True)

    forward.wait()
    row_attention(xr, kv, row_pattern, me, result, total, row_w, row_e)
    back[...] = total[:, :CW, :].astype(BF16)
    backward = pltpu.make_async_remote_copy(
        src_ref=back,
        dst_ref=backr,
        send_sem=ring_sem.at[2],
        recv_sem=ring_sem.at[3],
        device_id=before,
        device_id_type=MESH,
    )
    backward.start()

    arrived(1, r2a, False)
    pieces = [r2a[:, i // 2, i % 2].reshape(ROWS, HALF) for i in range(PIECES)]
    for i, found_here in enumerate(column_attention(*pieces, bias[...])):
        found[0, i] = found_here
    arrived(1, r2b, True)
    pieces = []
    for p in range(PAIRS):
        rows = matmul(perm[UNPACK], r2b[:, p].reshape(BLOCK, HALF)).astype(BF16)
        pieces += [rows[:ROWS], rows[ROWS:]]
    for i, found_here in enumerate(column_attention(*pieces, bias[...])):
        found[1, i] = found_here

    for k in range(ROWS // PART):
        part = pl.ds(k * PART, PART)
        rows = found[:, :, part, :].reshape(BLOCK, HALF)
        s3[part] = matmul(perm[SPREAD], rows).astype(BF16).reshape(PART, 2 * PIECES, HALF)

    for i in ALL_ORDER:
        other = y_places[i // NZX] * NZX + zx_places[i % NZX]
        pltpu.make_async_remote_copy(
            src_ref=s3.at[other],
            dst_ref=r3.at[me],
            send_sem=back_send_sem,
            recv_sem=back_recv_sem,
            device_id=device(other),
            device_id_type=MESH,
        ).start()
    pltpu.make_async_copy(s3.at[me], r3.at[me], back_recv_sem).start()

    row_gradients(xr, kv, result, total, row_w, row_e)
    backward.wait()
    for i in range(2):
        result[2 + i, :, :HALF] = (total[i, CW:, :] + backr[i].astype(F32)).astype(BF16)

    pltpu.make_async_copy(r3, r3, back_recv_sem).wait()
    for k in range(ROWS // PART):
        part = pl.ds(k * PART, PART)
        rows = matmul(perm[GATHER], r3[part].reshape(BLOCK, HALF)).astype(BF16)
        for c in range(2):
            for i in range(PIECES):
                start = (c * PIECES + i) * PART
                place = pl.ds(c * HALF + k * PART, PART)
                result[i, place, HALF:] = rows[start : start + PART]

    for step, (over_zx, over_y) in enumerate(((r1a, r1b), (r2b, r2a))):
        sent(step, over_zx, True)
        sent(step, over_y, False)
    others = s3.at[pl.ds(0, ROWS - 1)]
    pltpu.make_async_copy(others, others, back_send_sem).wait()


def write_out(result, o0, o1, o2, o3, sem):
    copies = [
        pltpu.make_async_copy(result.at[i], o.at[0], sem.at[i])
        for i, o in enumerate((o0, o1, o2, o3))
    ]
    for copy in copies:
        copy.start()
    for copy in copies:
        copy.wait()


def per_device(queries, key_vectors, value_vectors, cotangent, row_pattern, column_pattern):
    by_zx = pltpu.VMEM((NZX, PAIRS, 2 * NY, HALF), BF16)
    by_y = pltpu.VMEM((NY, PAIRS, 2, NZX, HALF), BF16)
    weights = pltpu.VMEM((2, 3 * HALF, 2 * HALF), BF16)
    direct = pltpu.VMEM((ROWS, 2 * PIECES, HALF), BF16)
    vmem = pl.BlockSpec(memory_space=pltpu.VMEM)
    hbm = pl.BlockSpec(memory_space=pltpu.HBM)
    halves = pltpu.VMEM((PAIRS, 2, CW, HALF), BF16)
    pair = pltpu.VMEM((2, CW, HALF), BF16)
    in_hbm = [
        pltpu.with_memory_space_constraint(x, pltpu.HBM)
        for x in (queries, key_vectors, value_vectors, cotangent, row_pattern, column_pattern)
    ]
    result = pl.pallas_call(
        kernel,
        out_shape=pltpu.VMEM((PIECES, CW, 2 * HALF), BF16),
        in_specs=[hbm] * 6,
        out_specs=vmem,
        scratch_shapes=[
            halves, pair,
            pltpu.VMEM((2, 2 * CW, HALF), BF16),
            pair, pair,
            pltpu.VMEM((2, 2 * CW, HALF), F32),
            weights, weights,
            pltpu.VMEM((6, BLOCK, BLOCK), BF16),
            pltpu.VMEM((ROWS, 2 * ROWS), F32),
            by_zx, by_zx, by_y,
            by_y, by_y, by_zx, by_zx,
            pltpu.VMEM((2, PIECES, ROWS, HALF), BF16),
            direct, direct,
            pltpu.SMEM(row_pattern.shape, jnp.int32),
            pltpu.SMEM(column_pattern.shape, jnp.int32),
            pltpu.SemaphoreType.DMA((2,)),
            pltpu.SemaphoreType.DMA((2, PIECES)),
            pltpu.SemaphoreType.DMA((4,)),
            pltpu.SemaphoreType.DMA((2, 2)),
            pltpu.SemaphoreType.DMA((2, 2)),
            pltpu.SemaphoreType.DMA,
            pltpu.SemaphoreType.DMA,
        ],
        compiler_params=pltpu.CompilerParams(
            collective_id=0, has_side_effects=True, vmem_limit_bytes=40 * 1024 * 1024
        ),
        cost_estimate=pl.CostEstimate(
            flops=800_000_000, bytes_accessed=1_050_000, transcendentals=200_000
        ),
        name="grid_attention",
    )(*in_hbm)
    return pl.pallas_call(
        write_out,
        out_shape=[jax.ShapeDtypeStruct(queries.shape, BF16)] * 4,
        in_specs=[vmem],
        out_specs=[hbm] * 4,
        scratch_shapes=[pltpu.SemaphoreType.DMA((PIECES,))],
        cost_estimate=pl.CostEstimate(flops=0, bytes_accessed=1_050_000, transcendentals=0),
        compiler_params=pltpu.CompilerParams(vmem_limit_bytes=8 * 1024 * 1024),
        name="write_out",
    )(pltpu.with_memory_space_constraint(result, pltpu.VMEM))


def solution(mesh):
    rows = P(("batch", "seq"), None, "mp")
    heads = P("mp", None, None)
    return jax.shard_map(
        per_device,
        mesh=mesh,
        in_specs=(rows, rows, rows, rows, heads, heads),
        out_specs=(rows, rows, rows, rows),
        check_vma=False,
    )
```

```python
import jax
import jax.numpy as jnp
from jax import lax
from jax.experimental import pallas as pl
from jax.experimental.pallas import tpu as pltpu
from jax.sharding import PartitionSpec as P

MESH = pl.DeviceIdType.MESH
F32 = jnp.float32
BF16 = jnp.bfloat16
NEG = -1e30

NY = 8
NZX = 16
ROWS = NY * NZX
CW = 256
HALF = 128
DH = 64
PIECES = 4
PAIRS = PIECES // 2
BLOCK = 2 * ROWS
PART = 32
PACK, UNPACK, ZX_TO_Y, Y_TO_ZX, SPREAD, GATHER = range(6)


def hops(offset, size):
    return min(offset, size - offset)


def far_first(count, distance):
    return sorted(range(1, count), key=lambda i: (-distance(i), i * 37 % count))


Y_ORDER = far_first(NY, lambda i: hops(i, NY))
ZX_ORDER = far_first(NZX, lambda i: hops(i // 2, NZX // 2) + i % 2)
ALL_ORDER = far_first(ROWS, lambda i: hops(i // NZX, NY) + hops(i % NZX // 2, NZX // 2) + i % 2)


def iota(shape, axis):
    return lax.broadcasted_iota(jnp.int32, shape, axis)


def matmul(a, b):
    return lax.dot_general(a, b, (((1,), (0,)), ((), ())), preferred_element_type=F32)


def matmul_nt(a, b):
    return lax.dot_general(a, b, (((1,), (1,)), ((), ())), preferred_element_type=F32)


def per_head(x):
    first = iota(x.shape, 1) < DH
    zero = jnp.zeros_like(x)
    return jnp.concatenate([jnp.where(first, x, zero), jnp.where(first, zero, x)], axis=0)


def both_heads(wide):
    first = iota((HALF, HALF), 0) < DH
    return jnp.where(first, wide[:, :HALF], wide[:, HALF:])


def head_sums(x):
    return jnp.concatenate(
        [x[:DH].sum(0, keepdims=True), x[DH:].sum(0, keepdims=True)], axis=1
    )


def softmax(blocks):
    highest = blocks[0].max(axis=0, keepdims=True)
    for block in blocks[1:]:
        highest = jnp.maximum(highest, block.max(axis=0, keepdims=True))
    powers = [jnp.exp(block - highest) for block in blocks]
    total = powers[0].sum(axis=0, keepdims=True)
    for power in powers[1:]:
        total = total + power.sum(axis=0, keepdims=True)
    share = 1.0 / total
    return [power * share for power in powers]


def row_attention(x_ref, kv_ref, pattern_ref, row, out_ref, total_ref):
    shape = (HALF, 2 * HALF)
    same = iota(shape, 0) <= (iota((1, 2 * HALF), 1) & (HALF - 1))
    has_earlier = jnp.broadcast_to(row >= 1, shape)
    keys_t, values_t = kv_ref[0].T, kv_ref[1].T
    for b in range(2):
        start = b * HALF
        rows, window = pl.ds(start, HALF), pl.ds(start, 3 * HALF)
        first, second = (pattern_ref[h, b, 1 - b] * jnp.minimum(row + b, 1) for h in range(2))
        whole_open = jnp.where(iota((1, 2 * HALF), 1) < HALF, first, second) > 0
        q = per_head(x_ref[0, rows, :]) * jnp.asarray(0.125, BF16)
        g = per_head(x_ref[1, rows, :])
        keys, values = kv_ref[0, window, :], kv_ref[1, window, :]
        scores, weight_grads = matmul_nt(keys, q), matmul_nt(values, g)

        def chosen(x, earlier_else):
            earlier, whole, this = (x[i * HALF : (i + 1) * HALF] for i in range(3))
            return jnp.where(same, this, earlier_else(earlier)), whole

        diag, whole = chosen(scores, lambda x: jnp.where(has_earlier, x, NEG))
        p_diag, p_whole = softmax([diag, jnp.where(whole_open, whole, NEG)])

        def spread(at_diag, at_whole):
            at_diag, at_whole = at_diag.astype(BF16), at_whole.astype(BF16)
            zero = jnp.zeros_like(at_diag)
            return jnp.concatenate(
                [jnp.where(same, zero, at_diag), at_whole, jnp.where(same, at_diag, zero)], axis=0
            )

        w = spread(p_diag, p_whole)
        attended = both_heads(matmul(values_t[:, start : start + 3 * HALF], w)).astype(BF16)
        out_ref[0, rows, :HALF] = attended.T
        dots = head_sums(x_ref[1, rows, :].T.astype(F32) * attended.astype(F32))
        d_diag, d_whole = chosen(weight_grads, lambda x: x)
        e = spread(p_diag * (d_diag - dots), p_whole * (d_whole - dots))
        grad = both_heads(matmul(keys_t[:, start : start + 3 * HALF], e)) * 0.125
        out_ref[1, rows, :HALF] = grad.astype(BF16).T
        for i, term in enumerate((matmul(e, q), matmul(w, g))):
            if b == 0:
                total_ref[i, window, :] = term
            else:
                total_ref[i, HALF : 3 * HALF, :] += term[: 2 * HALF]
                total_ref[i, 3 * HALF :, :] = term[2 * HALF :]


def column_attention(q, k, v, g, bias):
    g_t = g.T.astype(F32)
    q = per_head(q) * jnp.asarray(0.125, BF16)
    g = per_head(g)
    (p,) = softmax([matmul_nt(k, q) + bias])
    w = p.astype(BF16)
    attended = both_heads(matmul(v.T, w)).astype(BF16)
    dots = head_sums(g_t * attended.astype(F32))
    e = (p * (matmul_nt(v, g) - dots)).astype(BF16)
    grad = (both_heads(matmul(k.T, e)) * 0.125).astype(BF16)
    return attended.T, grad.T, matmul(e, q).astype(BF16), matmul(w, g).astype(BF16)


def column_bias(pattern_ref):
    key, stacked = iota((ROWS, 1), 0), iota((1, 2 * ROWS), 1)
    query = stacked & (ROWS - 1)
    bits = jnp.zeros(stacked.shape, jnp.int32)
    for h in range(2):
        for b in range(4):
            code = sum(pattern_ref[h, b, j] * (1 << j) for j in range(4))
            bits = jnp.where(stacked // 32 == 4 * h + b, code, bits)
    seen = jnp.zeros((ROWS, 2 * ROWS), jnp.int32)
    for j in range(4):
        seen = jnp.where(key // 32 == j, (bits >> j) & 1, seen)
    allowed = (key <= query) & (seen > 0)
    return jnp.where(allowed, 0.0, NEG)


def reorder(source, target):
    order, size, row = {}, 1, iota((1, BLOCK), 1)
    for name in reversed(source):
        order[name] = (row // size) & (source[name] - 1)
        size *= source[name]
    place = 0
    for name in target:
        place = place * source[name] + order[name]
    return jnp.where(place == iota((BLOCK, BLOCK), 0), 1.0, 0.0).astype(BF16)


def kernel(
    q_hbm, k_hbm, v_hbm, g_hbm, row_pattern_hbm, column_pattern_hbm,
    result,
    xc, xr, kv, back, backr, total, perm, bias,
    s1a, r1a, r1b, s2a, r2a, s2b, r2b, found, s3, r3,
    row_pattern, column_pattern, pattern_sem, in_sem, ring_sem, send_sem, recv_sem, back_send_sem, back_recv_sem,
):
    me = lax.axis_index("seq")
    y, zx = me // NZX, lax.rem(me, NZX)
    place_here = {"mp": lax.axis_index("mp"), "batch": lax.axis_index("batch")}
    after = {"seq": lax.rem(me + 1, ROWS), **place_here}
    before = {"seq": lax.rem(me + ROWS - 1, ROWS), **place_here}

    zx_places = [lax.rem(zx + i, NZX) for i in range(NZX)]
    y_places = [lax.rem(y + i, NY) for i in range(NY)]

    def device(seq):
        return {"seq": seq, **place_here}

    zx_peers = [(zx_places[i], device(y * NZX + zx_places[i])) for i in ZX_ORDER]
    y_peers = [(y_places[i], device(y_places[i] * NZX + zx)) for i in Y_ORDER]

    inputs = (q_hbm, k_hbm, v_hbm, g_hbm)

    this_row = pl.ds(CW, CW)
    row_places = (xr.at[0], kv.at[0, this_row], kv.at[1, this_row], xr.at[1])

    def loads_of(part, places):
        return [
            pltpu.make_async_copy(h.at[0, :, pl.ds(part * HALF, HALF)], place, in_sem.at[part, i])
            for i, (h, place) in enumerate(zip(inputs, places))
        ]

    column_loads = loads_of(1, [xc.at[i // 2, i % 2] for i in range(PIECES)])
    row_loads = loads_of(0, row_places)
    patterns = [
        pltpu.make_async_copy(row_pattern_hbm, row_pattern, pattern_sem.at[0]),
        pltpu.make_async_copy(column_pattern_hbm, column_pattern, pattern_sem.at[1]),
    ]
    for load in column_loads:
        load.start()

    barrier = pltpu.get_barrier_semaphore()

    def greet(peer):
        pl.semaphore_signal(barrier, inc=1, device_id=peer, device_id_type=MESH)

    for _, peer in zx_peers + y_peers:
        greet(peer)
    greet(after)
    greet(before)
    for load in row_loads + patterns:
        load.start()

    def exchange(step, source, landing, over_zx):
        place = (step, 0 if over_zx else 1)
        peers, mine = (zx_peers, zx) if over_zx else (y_peers, y)
        for other, peer in peers:
            pltpu.make_async_remote_copy(
                src_ref=source(other),
                dst_ref=landing(mine),
                send_sem=send_sem.at[place],
                recv_sem=recv_sem.at[place],
                device_id=peer,
                device_id_type=MESH,
            ).start()
        pltpu.make_async_copy(source(mine), landing(mine), recv_sem.at[place]).start()

    def send(step, source, dest, over_zx):
        exchange(step, lambda j: source.at[j], lambda j: dest.at[j], over_zx)

    def arrived(step, whole, over_zx):
        pltpu.make_async_copy(whole, whole, recv_sem.at[step, 0 if over_zx else 1]).wait()

    def sent(step, dest, over_zx):
        part = dest.at[pl.ds(0, dest.shape[0] - 1)]
        pltpu.make_async_copy(part, part, send_sem.at[step, 0 if over_zx else 1]).wait()

    def last_columns(j=None):
        rows = pl.ds(HALF, HALF) if j is None else pl.ds(pl.multiple_of(HALF + j * NZX, NZX), NZX)
        return (slice(None), slice(None), rows, slice(None))

    grid_rows = {"piece": 2, "y": NY, "zx": NZX}
    by_zx = ("zx", "piece", "y")
    perm[PACK] = reorder(grid_rows, by_zx)
    for load in column_loads:
        load.wait()
    for p in range(PAIRS):
        rows = xc[p, :, :HALF, :].reshape(BLOCK, HALF)
        packed = matmul(perm[PACK], rows).astype(BF16)
        s1a[:, p] = packed.reshape(NZX, 2 * NY, HALF)
    pl.semaphore_wait(barrier, (NZX - 1) + (NY - 1) + 2)

    send(0, s1a, r1a, True)
    exchange(0, lambda j: xc.at[last_columns(j)], lambda j: r1b.at[j], False)
    for load in row_loads:
        load.wait()
    forward = pltpu.make_async_remote_copy(
        src_ref=kv.at[:, this_row],
        dst_ref=kv.at[:, pl.ds(0, CW)],
        send_sem=ring_sem.at[0],
        recv_sem=ring_sem.at[1],
        device_id=after,
        device_id_type=MESH,
    )
    forward.start()

    for t, source, target in (
        (UNPACK, {"zx": NZX, "piece": 2, "y": NY}, ("piece", "y", "zx")),
        (ZX_TO_Y, {"zx": NZX, "piece": 2, "y": NY}, ("y", "piece", "zx")),
        (Y_TO_ZX, {"y": NY, "piece": 2, "zx": NZX}, ("zx", "piece", "y")),
        (SPREAD, {"piece": 2 * PIECES, "row": PART}, ("row", "piece")),
        (GATHER, {"row": PART, "piece": 2 * PIECES}, ("piece", "row")),
    ):
        perm[t] = reorder(source, target)
    for load in patterns:
        load.wait()
    bias[...] = column_bias(column_pattern)

    def swap(dest, source, t):
        for p in range(PAIRS):
            rows = matmul(perm[t], source[:, p].reshape(BLOCK, HALF)).astype(BF16)
            dest[:, p] = rows.reshape(dest.shape[:1] + dest.shape[2:])

    arrived(0, r1a, True)
    swap(s2a, r1a, ZX_TO_Y)
    send(1, s2a, r2a, False)
    arrived(0, r1b, False)
    swap(s2b, r1b, Y_TO_ZX)
    send(1, s2b, r2b, True)

    forward.wait()
    row_attention(xr, kv, row_pattern, me, result, total)
    back[...] = total[:, :CW, :].astype(BF16)
    backward = pltpu.make_async_remote_copy(
        src_ref=back,
        dst_ref=backr,
        send_sem=ring_sem.at[2],
        recv_sem=ring_sem.at[3],
        device_id=before,
        device_id_type=MESH,
    )
    backward.start()

    arrived(1, r2a, False)
    pieces = [r2a[:, i // 2, i % 2].reshape(ROWS, HALF) for i in range(PIECES)]
    for i, found_here in enumerate(column_attention(*pieces, bias[...])):
        found[0, i] = found_here
    arrived(1, r2b, True)
    pieces = []
    for p in range(PAIRS):
        rows = matmul(perm[UNPACK], r2b[:, p].reshape(BLOCK, HALF)).astype(BF16)
        pieces += [rows[:ROWS], rows[ROWS:]]
    for i, found_here in enumerate(column_attention(*pieces, bias[...])):
        found[1, i] = found_here

    for k in range(ROWS // PART):
        part = pl.ds(k * PART, PART)
        rows = found[:, :, part, :].reshape(BLOCK, HALF)
        s3[part] = matmul(perm[SPREAD], rows).astype(BF16).reshape(PART, 2 * PIECES, HALF)

    mine = back_recv_sem.at[me // PART]
    for i in ALL_ORDER:
        other = y_places[i // NZX] * NZX + zx_places[i % NZX]
        pltpu.make_async_remote_copy(
            src_ref=s3.at[other],
            dst_ref=r3.at[me],
            send_sem=back_send_sem,
            recv_sem=mine,
            device_id=device(other),
            device_id_type=MESH,
        ).start()
    pltpu.make_async_copy(s3.at[me], r3.at[me], mine).start()

    backward.wait()
    for i in range(2):
        result[2 + i, :, :HALF] = (total[i, CW:, :] + backr[i].astype(F32)).astype(BF16)

    for k in (2, 1, 3, 0):
        k = lax.rem(me // PART + k, ROWS // PART)
        part = pl.ds(pl.multiple_of(k * PART, PART), PART)
        pltpu.make_async_copy(r3.at[part], r3.at[part], back_recv_sem.at[k]).wait()
        rows = matmul(perm[GATHER], r3[part].reshape(BLOCK, HALF)).astype(BF16)
        for c in range(2):
            for i in range(PIECES):
                start = (c * PIECES + i) * PART
                place = pl.ds(pl.multiple_of(c * HALF + k * PART, PART), PART)
                result[i, place, HALF:] = rows[start : start + PART]

    for step, (over_zx, over_y) in enumerate(((r1a, r1b), (r2b, r2a))):
        sent(step, over_zx, True)
        sent(step, over_y, False)
    others = s3.at[pl.ds(0, ROWS - 1)]
    pltpu.make_async_copy(others, others, back_send_sem).wait()


def write_out(result, o0, o1, o2, o3, sem):
    copies = [
        pltpu.make_async_copy(result.at[i], o.at[0], sem.at[i])
        for i, o in enumerate((o0, o1, o2, o3))
    ]
    for copy in copies:
        copy.start()
    for copy in copies:
        copy.wait()


def per_device(queries, key_vectors, value_vectors, cotangent, row_pattern, column_pattern):
    by_zx = pltpu.VMEM((NZX, PAIRS, 2 * NY, HALF), BF16)
    by_y = pltpu.VMEM((NY, PAIRS, 2, NZX, HALF), BF16)
    direct = pltpu.VMEM((ROWS, 2 * PIECES, HALF), BF16)
    vmem = pl.BlockSpec(memory_space=pltpu.VMEM)
    hbm = pl.BlockSpec(memory_space=pltpu.HBM)
    halves = pltpu.VMEM((PAIRS, 2, CW, HALF), BF16)
    pair = pltpu.VMEM((2, CW, HALF), BF16)
    in_hbm = [
        pltpu.with_memory_space_constraint(x, pltpu.HBM)
        for x in (queries, key_vectors, value_vectors, cotangent, row_pattern, column_pattern)
    ]
    result = pl.pallas_call(
        kernel,
        out_shape=pltpu.VMEM((PIECES, CW, 2 * HALF), BF16),
        in_specs=[hbm] * 6,
        out_specs=vmem,
        scratch_shapes=[
            halves, pair,
            pltpu.VMEM((2, 2 * CW, HALF), BF16),
            pair, pair,
            pltpu.VMEM((2, 2 * CW, HALF), F32),
            pltpu.VMEM((6, BLOCK, BLOCK), BF16),
            pltpu.VMEM((ROWS, 2 * ROWS), F32),
            by_zx, by_zx, by_y,
            by_y, by_y, by_zx, by_zx,
            pltpu.VMEM((2, PIECES, ROWS, HALF), BF16),
            direct, direct,
            pltpu.SMEM(row_pattern.shape, jnp.int32),
            pltpu.SMEM(column_pattern.shape, jnp.int32),
            pltpu.SemaphoreType.DMA((2,)),
            pltpu.SemaphoreType.DMA((2, PIECES)),
            pltpu.SemaphoreType.DMA((4,)),
            pltpu.SemaphoreType.DMA((2, 2)),
            pltpu.SemaphoreType.DMA((2, 2)),
            pltpu.SemaphoreType.DMA,
            pltpu.SemaphoreType.DMA((ROWS // PART,)),
        ],
        compiler_params=pltpu.CompilerParams(
            collective_id=0, has_side_effects=True, vmem_limit_bytes=40 * 1024 * 1024
        ),
        cost_estimate=pl.CostEstimate(
            flops=800_000_000, bytes_accessed=1_050_000, transcendentals=200_000
        ),
        name="grid_attention",
    )(*in_hbm)
    return pl.pallas_call(
        write_out,
        out_shape=[jax.ShapeDtypeStruct(queries.shape, BF16)] * 4,
        in_specs=[vmem],
        out_specs=[hbm] * 4,
        scratch_shapes=[pltpu.SemaphoreType.DMA((PIECES,))],
        cost_estimate=pl.CostEstimate(flops=0, bytes_accessed=1_050_000, transcendentals=0),
        compiler_params=pltpu.CompilerParams(vmem_limit_bytes=8 * 1024 * 1024),
        name="write_out",
    )(pltpu.with_memory_space_constraint(result, pltpu.VMEM))


def solution(mesh):
    rows = P(("batch", "seq"), None, "mp")
    heads = P("mp", None, None)
    return jax.shard_map(
        per_device,
        mesh=mesh,
        in_specs=(rows, rows, rows, rows, heads, heads),
        out_specs=(rows, rows, rows, rows),
        check_vma=False,
    )
```

```python
import jax
import jax.numpy as jnp
from jax import lax
from jax.experimental import pallas as pl
from jax.experimental.pallas import tpu as pltpu
from jax.sharding import PartitionSpec as P

MESH = pl.DeviceIdType.MESH
F32 = jnp.float32
BF16 = jnp.bfloat16
NEG = -1e30

NY = 8
NZX = 16
ROWS = NY * NZX
CW = 256
HALF = 128
DH = 64
PIECES = 4
PAIRS = PIECES // 2
BLOCK = 2 * ROWS
CHUNK = 64
PART = 32
PACK, UNPACK, ZX_TO_Y, Y_TO_ZX, SPREAD, GATHER = range(6)


def hops(offset, size):
    return min(offset, size - offset)


def far_first(count, distance):
    return sorted(range(1, count), key=lambda i: (-distance(i), i * 37 % count))


Y_ORDER = far_first(NY, lambda i: hops(i, NY))
ZX_ORDER = far_first(NZX, lambda i: hops(i // 2, NZX // 2) + i % 2)
ALL_ORDER = far_first(ROWS, lambda i: hops(i // NZX, NY) + hops(i % NZX // 2, NZX // 2) + i % 2)


def iota(shape, axis):
    return lax.broadcasted_iota(jnp.int32, shape, axis)


def matmul(a, b):
    return lax.dot_general(a, b, (((1,), (0,)), ((), ())), preferred_element_type=F32)


def matmul_nt(a, b):
    return lax.dot_general(a, b, (((1,), (1,)), ((), ())), preferred_element_type=F32)


def per_head(x):
    first = iota(x.shape, 1) < DH
    zero = jnp.zeros_like(x)
    return jnp.concatenate([jnp.where(first, x, zero), jnp.where(first, zero, x)], axis=0)


def both_heads(wide):
    first = iota((HALF, HALF), 0) < DH
    return jnp.where(first, wide[:, :HALF], wide[:, HALF:])


def head_sums(x):
    return jnp.concatenate(
        [x[:DH].sum(0, keepdims=True), x[DH:].sum(0, keepdims=True)], axis=1
    )


def softmax(blocks):
    highest = blocks[0].max(axis=0, keepdims=True)
    for block in blocks[1:]:
        highest = jnp.maximum(highest, block.max(axis=0, keepdims=True))
    powers = [jnp.exp(block - highest) for block in blocks]
    total = powers[0].sum(axis=0, keepdims=True)
    for power in powers[1:]:
        total = total + power.sum(axis=0, keepdims=True)
    share = 1.0 / total
    return [power * share for power in powers]


def row_attention(x_ref, kv_ref, pattern_ref, row, out_ref, total_ref):
    shape = (HALF, 2 * HALF)
    same = iota(shape, 0) <= (iota((1, 2 * HALF), 1) & (HALF - 1))
    has_earlier = jnp.broadcast_to(row >= 1, shape)
    keys_t, values_t = kv_ref[0].T, kv_ref[1].T
    for b in range(2):
        start = b * HALF
        rows, window = pl.ds(start, HALF), pl.ds(start, 3 * HALF)
        first, second = (pattern_ref[h, b, 1 - b] * jnp.minimum(row + b, 1) for h in range(2))
        whole_open = jnp.where(iota((1, 2 * HALF), 1) < HALF, first, second) > 0
        q = per_head(x_ref[0, rows, :]) * jnp.asarray(0.125, BF16)
        g = per_head(x_ref[1, rows, :])
        keys, values = kv_ref[0, window, :], kv_ref[1, window, :]
        scores, weight_grads = matmul_nt(keys, q), matmul_nt(values, g)

        def chosen(x, earlier_else):
            earlier, whole, this = (x[i * HALF : (i + 1) * HALF] for i in range(3))
            return jnp.where(same, this, earlier_else(earlier)), whole

        diag, whole = chosen(scores, lambda x: jnp.where(has_earlier, x, NEG))
        p_diag, p_whole = softmax([diag, jnp.where(whole_open, whole, NEG)])

        def spread(at_diag, at_whole):
            at_diag, at_whole = at_diag.astype(BF16), at_whole.astype(BF16)
            zero = jnp.zeros_like(at_diag)
            return jnp.concatenate(
                [jnp.where(same, zero, at_diag), at_whole, jnp.where(same, at_diag, zero)], axis=0
            )

        w = spread(p_diag, p_whole)
        attended = both_heads(matmul(values_t[:, start : start + 3 * HALF], w)).astype(BF16)
        out_ref[0, rows, :HALF] = attended.T
        dots = head_sums(x_ref[1, rows, :].T.astype(F32) * attended.astype(F32))
        d_diag, d_whole = chosen(weight_grads, lambda x: x)
        e = spread(p_diag * (d_diag - dots), p_whole * (d_whole - dots))
        grad = both_heads(matmul(keys_t[:, start : start + 3 * HALF], e)) * 0.125
        out_ref[1, rows, :HALF] = grad.astype(BF16).T
        for i, term in enumerate((matmul(e, q), matmul(w, g))):
            if b == 0:
                total_ref[i, window, :] = term
            else:
                total_ref[i, HALF : 3 * HALF, :] += term[: 2 * HALF]
                total_ref[i, 3 * HALF :, :] = term[2 * HALF :]


def column_attention(q, k, v, g, bias):
    g_t = g.T.astype(F32)
    q = per_head(q) * jnp.asarray(0.125, BF16)
    g = per_head(g)
    (p,) = softmax([matmul_nt(k, q) + bias])
    w = p.astype(BF16)
    attended = both_heads(matmul(v.T, w)).astype(BF16)
    dots = head_sums(g_t * attended.astype(F32))
    e = (p * (matmul_nt(v, g) - dots)).astype(BF16)
    grad = (both_heads(matmul(k.T, e)) * 0.125).astype(BF16)
    return attended.T, grad.T, matmul(e, q).astype(BF16), matmul(w, g).astype(BF16)


def column_bias(pattern_ref):
    key, stacked = iota((ROWS, 1), 0), iota((1, 2 * ROWS), 1)
    query = stacked & (ROWS - 1)
    bits = jnp.zeros(stacked.shape, jnp.int32)
    for h in range(2):
        for b in range(4):
            code = sum(pattern_ref[h, b, j] * (1 << j) for j in range(4))
            bits = jnp.where(stacked // 32 == 4 * h + b, code, bits)
    seen = jnp.zeros((ROWS, 2 * ROWS), jnp.int32)
    for j in range(4):
        seen = jnp.where(key // 32 == j, (bits >> j) & 1, seen)
    allowed = (key <= query) & (seen > 0)
    return jnp.where(allowed, 0.0, NEG)


def reorder(source, target):
    order, size, row = {}, 1, iota((1, BLOCK), 1)
    for name in reversed(source):
        order[name] = (row // size) & (source[name] - 1)
        size *= source[name]
    place = 0
    for name in target:
        place = place * source[name] + order[name]
    return jnp.where(place == iota((BLOCK, BLOCK), 0), 1.0, 0.0).astype(BF16)


def kernel(
    q_hbm, k_hbm, v_hbm, g_hbm, row_pattern_hbm, column_pattern_hbm,
    result,
    xc, xr, kv, back, backr, total, perm, bias,
    s1a, r1a, r1b, s2a, r2a, s2b, r2b, found, s3, r3,
    row_pattern, column_pattern, pattern_sem, in_sem, ring_sem, send_sem, recv_sem, back_send_sem, back_recv_sem,
):
    me = lax.axis_index("seq")
    y, zx = me // NZX, lax.rem(me, NZX)
    place_here = {"mp": lax.axis_index("mp"), "batch": lax.axis_index("batch")}
    after = {"seq": lax.rem(me + 1, ROWS), **place_here}
    before = {"seq": lax.rem(me + ROWS - 1, ROWS), **place_here}

    zx_places = [lax.rem(zx + i, NZX) for i in range(NZX)]
    y_places = [lax.rem(y + i, NY) for i in range(NY)]

    def device(seq):
        return {"seq": seq, **place_here}

    zx_peers = [(zx_places[i], device(y * NZX + zx_places[i])) for i in ZX_ORDER]
    y_peers = [(y_places[i], device(y_places[i] * NZX + zx)) for i in Y_ORDER]

    inputs = (q_hbm, k_hbm, v_hbm, g_hbm)

    this_row = pl.ds(CW, CW)
    row_places = (xr.at[0], kv.at[0, this_row], kv.at[1, this_row], xr.at[1])

    def loads_of(part, places):
        return [
            pltpu.make_async_copy(h.at[0, :, pl.ds(part * HALF, HALF)], place, in_sem.at[part, i])
            for i, (h, place) in enumerate(zip(inputs, places))
        ]

    column_loads = loads_of(1, [xc.at[i // 2, i % 2] for i in range(PIECES)])
    row_loads = loads_of(0, row_places)
    patterns = [
        pltpu.make_async_copy(row_pattern_hbm, row_pattern, pattern_sem.at[0]),
        pltpu.make_async_copy(column_pattern_hbm, column_pattern, pattern_sem.at[1]),
    ]
    for load in column_loads:
        load.start()

    barrier = pltpu.get_barrier_semaphore()

    def greet(peer):
        pl.semaphore_signal(barrier, inc=1, device_id=peer, device_id_type=MESH)

    for _, peer in zx_peers + y_peers:
        greet(peer)
    greet(after)
    greet(before)
    for load in row_loads + patterns:
        load.start()

    def exchange(step, source, landing, over_zx):
        place = (step, 0 if over_zx else 1)
        peers, mine = (zx_peers, zx) if over_zx else (y_peers, y)
        for other, peer in peers:
            pltpu.make_async_remote_copy(
                src_ref=source(other),
                dst_ref=landing(mine),
                send_sem=send_sem.at[place],
                recv_sem=recv_sem.at[place],
                device_id=peer,
                device_id_type=MESH,
            ).start()
        pltpu.make_async_copy(source(mine), landing(mine), recv_sem.at[place]).start()

    def send(step, source, dest, over_zx):
        exchange(step, lambda j: source.at[j], lambda j: dest.at[j], over_zx)

    def arrived(step, whole, over_zx):
        pltpu.make_async_copy(whole, whole, recv_sem.at[step, 0 if over_zx else 1]).wait()

    def sent(step, dest, over_zx):
        part = dest.at[pl.ds(0, dest.shape[0] - 1)]
        pltpu.make_async_copy(part, part, send_sem.at[step, 0 if over_zx else 1]).wait()

    def last_columns(j=None):
        rows = pl.ds(HALF, HALF) if j is None else pl.ds(pl.multiple_of(HALF + j * NZX, NZX), NZX)
        return (slice(None), slice(None), rows, slice(None))

    grid_rows = {"piece": 2, "y": NY, "zx": NZX}
    by_zx = ("zx", "piece", "y")
    perm[PACK] = reorder(grid_rows, by_zx)
    for load in column_loads:
        load.wait()
    for p in range(PAIRS):
        rows = xc[p, :, :HALF, :].reshape(BLOCK, HALF)
        packed = matmul(perm[PACK], rows).astype(BF16)
        s1a[:, p] = packed.reshape(NZX, 2 * NY, HALF)
    pl.semaphore_wait(barrier, (NZX - 1) + (NY - 1) + 2)

    send(0, s1a, r1a, True)
    exchange(0, lambda j: xc.at[last_columns(j)], lambda j: r1b.at[j], False)
    for load in row_loads:
        load.wait()

    def start_pieces(source, dest, first_sem, peer):
        for i in range(2):
            for start in range(0, CW, CHUNK):
                pltpu.make_async_remote_copy(
                    src_ref=source(i, start),
                    dst_ref=dest(i, start),
                    send_sem=ring_sem.at[first_sem],
                    recv_sem=ring_sem.at[first_sem + 1],
                    device_id=peer,
                    device_id_type=MESH,
                ).start()

    def wait_pieces(whole, sem):
        pltpu.make_async_copy(whole, whole, ring_sem.at[sem]).wait()

    start_pieces(
        lambda i, start: kv.at[i, pl.ds(CW + start, CHUNK)],
        lambda i, start: kv.at[i, pl.ds(start, CHUNK)],
        0,
        after,
    )

    for t, source, target in (
        (UNPACK, {"zx": NZX, "piece": 2, "y": NY}, ("piece", "y", "zx")),
        (ZX_TO_Y, {"zx": NZX, "piece": 2, "y": NY}, ("y", "piece", "zx")),
        (Y_TO_ZX, {"y": NY, "piece": 2, "zx": NZX}, ("zx", "piece", "y")),
        (SPREAD, {"piece": 2 * PIECES, "row": PART}, ("row", "piece")),
        (GATHER, {"row": PART, "piece": 2 * PIECES}, ("piece", "row")),
    ):
        perm[t] = reorder(source, target)
    for load in patterns:
        load.wait()
    bias[...] = column_bias(column_pattern)

    def swap(dest, source, t):
        for p in range(PAIRS):
            rows = matmul(perm[t], source[:, p].reshape(BLOCK, HALF)).astype(BF16)
            dest[:, p] = rows.reshape(dest.shape[:1] + dest.shape[2:])

    arrived(0, r1a, True)
    swap(s2a, r1a, ZX_TO_Y)
    send(1, s2a, r2a, False)
    arrived(0, r1b, False)
    swap(s2b, r1b, Y_TO_ZX)
    send(1, s2b, r2b, True)

    wait_pieces(kv.at[:, pl.ds(0, CW)], 1)
    row_attention(xr, kv, row_pattern, me, result, total)
    back[...] = total[:, :CW, :].astype(BF16)
    start_pieces(
        lambda i, start: back.at[i, pl.ds(start, CHUNK)],
        lambda i, start: backr.at[i, pl.ds(start, CHUNK)],
        2,
        before,
    )

    arrived(1, r2a, False)
    pieces = [r2a[:, i // 2, i % 2].reshape(ROWS, HALF) for i in range(PIECES)]
    for i, found_here in enumerate(column_attention(*pieces, bias[...])):
        found[0, i] = found_here
    arrived(1, r2b, True)
    pieces = []
    for p in range(PAIRS):
        rows = matmul(perm[UNPACK], r2b[:, p].reshape(BLOCK, HALF)).astype(BF16)
        pieces += [rows[:ROWS], rows[ROWS:]]
    for i, found_here in enumerate(column_attention(*pieces, bias[...])):
        found[1, i] = found_here

    for k in range(ROWS // PART):
        part = pl.ds(k * PART, PART)
        rows = found[:, :, part, :].reshape(BLOCK, HALF)
        s3[part] = matmul(perm[SPREAD], rows).astype(BF16).reshape(PART, 2 * PIECES, HALF)

    for i in ALL_ORDER:
        other = y_places[i // NZX] * NZX + zx_places[i % NZX]
        pltpu.make_async_remote_copy(
            src_ref=s3.at[other],
            dst_ref=r3.at[me],
            send_sem=back_send_sem,
            recv_sem=back_recv_sem,
            device_id=device(other),
            device_id_type=MESH,
        ).start()
    pltpu.make_async_copy(s3.at[me], r3.at[me], back_recv_sem).start()

    wait_pieces(backr, 3)
    for i in range(2):
        result[2 + i, :, :HALF] = (total[i, CW:, :] + backr[i].astype(F32)).astype(BF16)

    pltpu.make_async_copy(r3, r3, back_recv_sem).wait()
    for k in range(ROWS // PART):
        part = pl.ds(k * PART, PART)
        rows = matmul(perm[GATHER], r3[part].reshape(BLOCK, HALF)).astype(BF16)
        for c in range(2):
            for i in range(PIECES):
                start = (c * PIECES + i) * PART
                place = pl.ds(c * HALF + k * PART, PART)
                result[i, place, HALF:] = rows[start : start + PART]

    for step, (over_zx, over_y) in enumerate(((r1a, r1b), (r2b, r2a))):
        sent(step, over_zx, True)
        sent(step, over_y, False)
    wait_pieces(back, 0)
    wait_pieces(back, 2)
    others = s3.at[pl.ds(0, ROWS - 1)]
    pltpu.make_async_copy(others, others, back_send_sem).wait()


def write_out(result, o0, o1, o2, o3, sem):
    copies = [
        pltpu.make_async_copy(result.at[i], o.at[0], sem.at[i])
        for i, o in enumerate((o0, o1, o2, o3))
    ]
    for copy in copies:
        copy.start()
    for copy in copies:
        copy.wait()


def per_device(queries, key_vectors, value_vectors, cotangent, row_pattern, column_pattern):
    by_zx = pltpu.VMEM((NZX, PAIRS, 2 * NY, HALF), BF16)
    by_y = pltpu.VMEM((NY, PAIRS, 2, NZX, HALF), BF16)
    direct = pltpu.VMEM((ROWS, 2 * PIECES, HALF), BF16)
    vmem = pl.BlockSpec(memory_space=pltpu.VMEM)
    hbm = pl.BlockSpec(memory_space=pltpu.HBM)
    halves = pltpu.VMEM((PAIRS, 2, CW, HALF), BF16)
    pair = pltpu.VMEM((2, CW, HALF), BF16)
    in_hbm = [
        pltpu.with_memory_space_constraint(x, pltpu.HBM)
        for x in (queries, key_vectors, value_vectors, cotangent, row_pattern, column_pattern)
    ]
    result = pl.pallas_call(
        kernel,
        out_shape=pltpu.VMEM((PIECES, CW, 2 * HALF), BF16),
        in_specs=[hbm] * 6,
        out_specs=vmem,
        scratch_shapes=[
            halves, pair,
            pltpu.VMEM((2, 2 * CW, HALF), BF16),
            pair, pair,
            pltpu.VMEM((2, 2 * CW, HALF), F32),
            pltpu.VMEM((6, BLOCK, BLOCK), BF16),
            pltpu.VMEM((ROWS, 2 * ROWS), F32),
            by_zx, by_zx, by_y,
            by_y, by_y, by_zx, by_zx,
            pltpu.VMEM((2, PIECES, ROWS, HALF), BF16),
            direct, direct,
            pltpu.SMEM(row_pattern.shape, jnp.int32),
            pltpu.SMEM(column_pattern.shape, jnp.int32),
            pltpu.SemaphoreType.DMA((2,)),
            pltpu.SemaphoreType.DMA((2, PIECES)),
            pltpu.SemaphoreType.DMA((4,)),
            pltpu.SemaphoreType.DMA((2, 2)),
            pltpu.SemaphoreType.DMA((2, 2)),
            pltpu.SemaphoreType.DMA,
            pltpu.SemaphoreType.DMA,
        ],
        compiler_params=pltpu.CompilerParams(
            collective_id=0, has_side_effects=True, vmem_limit_bytes=40 * 1024 * 1024
        ),
        cost_estimate=pl.CostEstimate(
            flops=800_000_000, bytes_accessed=1_050_000, transcendentals=200_000
        ),
        name="grid_attention",
    )(*in_hbm)
    return pl.pallas_call(
        write_out,
        out_shape=[jax.ShapeDtypeStruct(queries.shape, BF16)] * 4,
        in_specs=[vmem],
        out_specs=[hbm] * 4,
        scratch_shapes=[pltpu.SemaphoreType.DMA((PIECES,))],
        cost_estimate=pl.CostEstimate(flops=0, bytes_accessed=1_050_000, transcendentals=0),
        compiler_params=pltpu.CompilerParams(vmem_limit_bytes=8 * 1024 * 1024),
        name="write_out",
    )(pltpu.with_memory_space_constraint(result, pltpu.VMEM))


def solution(mesh):
    rows = P(("batch", "seq"), None, "mp")
    heads = P("mp", None, None)
    return jax.shard_map(
        per_device,
        mesh=mesh,
        in_specs=(rows, rows, rows, rows, heads, heads),
        out_specs=(rows, rows, rows, rows),
        check_vma=False,
    )
```
